32 devices in a mesh: dp: 8 (over z, x), mp: 4 (over y, core).
Axes of the slice: x: 2, y: 2, z: 4, core: 2. Of those that a mesh axis runs over, the one named last changes fastest.
Arguments:
- tokens: bfloat16 [32768, 768], P(('dp', 'mp')), may hold values from -6 to 6
- w_qkv: bfloat16 [768, 2304], replicated, may hold values from -0.21875 to 0.21875
- bias_q: bfloat16 [768], replicated, may hold values from -3 to 3
- bias_v: bfloat16 [768], replicated, may hold values from -3 to 3
- w_out: bfloat16 [768, 768], replicated, may hold values from -0.4375 to 0.4375
- bias_out: bfloat16 [768], replicated, may hold values from -3 to 3
- norm1_gain: bfloat16 [768], replicated, may hold values from 0.5 to 1.5
- norm1_bias: bfloat16 [768], replicated, may hold values from -2 to 2
- w_in: bfloat16 [3072, 768], P('mp'), may hold values from -0.21875 to 0.21875
- bias_in: bfloat16 [3072], P('mp'), may hold values from -3 to 3
- w_down: bfloat16 [3072, 768], P('mp'), may hold values from -0.109375 to 0.109375
- bias_down: bfloat16 [768], replicated, may hold values from -3 to 3
- norm2_gain: bfloat16 [768], replicated, may hold values from 0.5 to 1.5
- norm2_bias: bfloat16 [768], replicated, may hold values from -2 to 2
- mask_logits: float32 [12, 512, 512], P(None, ('dp', 'mp')), may hold values from -8 to 8
- mask_noise: int32 [12, 512, 512], P(None, ('dp', 'mp')), may hold values from 1 to 65535
- grad_out: bfloat16 [32768, 768], P(('dp', 'mp')), may hold values from -6 to 6
Outputs:
- out: bfloat16 [32768, 768], P(('dp', 'mp'))
- grad_tokens: bfloat16 [32768, 768], P(('dp', 'mp'))
- grad_w_qkv: float32 [768, 2304], replicated
- grad_bias_q: float32 [768], replicated
- grad_bias_v: float32 [768], replicated
- grad_w_out: float32 [768, 768], replicated
- grad_bias_out: float32 [768], replicated
- grad_norm1_gain: float32 [768], replicated
- grad_norm1_bias: float32 [768], replicated
- grad_w_in: float32 [3072, 768], P('mp')
- grad_bias_in: float32 [3072], P('mp')
- grad_w_down: float32 [3072, 768], P('mp')
- grad_bias_down: float32 [768], replicated
- grad_norm2_gain: float32 [768], replicated
- grad_norm2_bias: float32 [768], replicated
- grad_mask_logits: float32 [12, 512, 512], P(None, ('dp', 'mp'))
The draws below stay inside these ranges and needn't reach their ends.
All inputs are finite; a program needn't handle non-finite values.
Results may differ from the reference program's by a relative error of at most 0.013.
The reference program's roundings to bfloat16 on the way count: a program that leaves them out, or rounds other values in their place, can miss the bound.
Values may be sent and summed in bfloat16 or wider, within the bound.
No kernel may reach another device: no remote copies, remote signals or barrier semaphores. Data moves between devices by JAX's collectives and lax.ppermute only.
A program may use at most 256 MiB of HBM per device.

```python
import math
import jax
import jax.numpy as jnp
from jax import lax

D = 768
H = 12
DH = 64
FF = 3072
SEQ = 512
TOKENS = 32768


def with_ends(values, stream_key, low, top_value):
    longest = values.shape.index(max(values.shape))
    spots = []
    for shift in (0, 1):
        where = [jax.random.randint(jax.random.fold_in(stream_key, axis), (), 0, length) for axis, length in enumerate(values.shape)]
        where[longest] = (where[longest] + shift) % values.shape[longest]
        spots.append(tuple(where))
    return values.at[spots[0]].set(low).at[spots[1]].set(top_value)


def block_scale(key, shape, cuts, least, high):
    factor_of = 1.0
    for axis_at, parts in cuts:
        steps = jax.random.uniform(jax.random.fold_in(jax.random.fold_in(key, 6), axis_at), (parts,), jnp.float32, least / len(cuts), high / len(cuts))
        factor_of = factor_of * jnp.repeat(jnp.exp(steps), shape[axis_at] // parts).reshape((-1,) + (1,) * (len(shape) - 1 - axis_at))
    return factor_of


def gaussian(stream_key, shape, scale, limit, pieces=(), held_as=jnp.bfloat16):
    factor_of = block_scale(stream_key, shape, pieces, -0.22, 0.18) if pieces else 1.0
    array = jax.random.normal(stream_key, shape, jnp.float32) * scale * factor_of
    return jnp.minimum(jnp.maximum(array, -limit), limit).astype(held_as)


def setup_inputs(seed: int = 0) -> dict:
    key_of = jax.random.split(jax.random.key(seed), 18)
    return {
        "tokens": gaussian(key_of[0], (TOKENS, D), 1.0, 6.0, ((0, 32),)),
        "w_qkv": gaussian(key_of[1], (D, 3 * D), D ** -0.5, 0.21875),
        "bias_q": gaussian(key_of[2], (D,), 0.5, 3.0),
        "bias_v": gaussian(key_of[3], (D,), 0.5, 3.0),
        "w_out": gaussian(key_of[4], (D, D), (D // 4) ** -0.5, 0.4375),
        "bias_out": gaussian(key_of[5], (D,), 0.5, 3.0),
        "norm1_gain": jnp.clip(1.0 + 0.1 * jax.random.normal(key_of[6], (D,), jnp.float32), 0.5, 1.5).astype(jnp.bfloat16),
        "norm1_bias": gaussian(key_of[7], (D,), 0.3, 2.0),
        "w_in": gaussian(key_of[8], (FF, D), D ** -0.5, 0.21875, ((0, 4),)),
        "bias_in": gaussian(key_of[9], (FF,), 0.5, 3.0, ((0, 4),)),
        "w_down": gaussian(key_of[10], (FF, D), FF ** -0.5, 0.109375, ((0, 4),)),
        "bias_down": gaussian(key_of[11], (D,), 0.5, 3.0),
        "norm2_gain": jnp.clip(1.0 + 0.1 * jax.random.normal(key_of[12], (D,), jnp.float32), 0.5, 1.5).astype(jnp.bfloat16),
        "norm2_bias": gaussian(key_of[13], (D,), 0.3, 2.0),
        "mask_logits": gaussian(key_of[14], (H, SEQ, SEQ), 1.5, 8.0, ((1, 32),), jnp.float32),
        "mask_noise": with_ends(jax.random.randint(key_of[15], (H, SEQ, SEQ), 1, 65536), jax.random.fold_in(key_of[15], 1), 1, 65535).astype(jnp.int32),
        "grad_out": gaussian(key_of[16], (TOKENS, D), 1.0, 6.0, ((0, 32),)),
    }


MASK_SCALE = 4.0
NORM_EPS = 1e-12
HIGH = lax.Precision.HIGHEST

@jax.custom_vjp
def low(v):
    return lax.optimization_barrier(v.astype(jnp.bfloat16)).astype(jnp.float32)

@jax.custom_vjp
def low_back(v):
    return v

def low_keep(v):
    return (low(v), None)

def low_pass(kept, grad):
    return (grad,)

def back_keep(v):
    return (v, None)

def back_low(kept, grad):
    return (low(grad),)
low.defvjp(low_keep, low_pass)
low_back.defvjp(back_keep, back_low)

def layer_norm(value, gain, shift):
    center = lax.optimization_barrier(jnp.mean(value, axis=-1, keepdims=True))
    centered = value - center
    spread = lax.optimization_barrier(jnp.mean(centered * centered, axis=-1, keepdims=True))
    return centered * lax.rsqrt(spread + NORM_EPS) * gain + shift

def relaxed_mask(mask_logits, mask_noise):
    fraction = mask_noise.astype(jnp.float32) / 65536.0
    return jax.nn.sigmoid(mask_logits + jnp.log(fraction) - jnp.log(1.0 - fraction))

def block_forward(params, mask_value, block):
    w_qkv, bias_q, bias_v, w_out, bias_out, gain_one, shift_one, w_in, bias_in, w_down, bias_down, gain_two, shift_two = params
    width = w_out.shape[0]
    count = block.shape[0] // SEQ
    shift_qkv = jnp.concatenate([bias_q, jnp.zeros_like(bias_q), bias_v])
    projected = jnp.dot(low(block), w_qkv, precision=HIGH) + shift_qkv
    projected = low(low_back(projected))
    split = projected.reshape(count, SEQ, 3, H, DH)
    query = split[:, :, 0]
    keys = split[:, :, 1]
    values = split[:, :, 2]
    scores = low_back(jnp.einsum('bqhd,bkhd->bhqk', query, keys, precision=HIGH) * (1.0 / math.sqrt(DH)))
    scores = scores + MASK_SCALE * (mask_value - 1.0)[None]
    highest = lax.optimization_barrier(jnp.max(scores, axis=-1, keepdims=True))
    powers = jnp.exp(scores - highest)
    probs = powers / lax.optimization_barrier(jnp.sum(powers, axis=-1, keepdims=True))
    mixed = jnp.einsum('bhqk,bkhd->bqhd', low(probs), values, precision=HIGH)
    mixed = low(low_back(mixed.reshape(count * SEQ, width)))
    attn = low_back(jnp.dot(mixed, w_out, precision=HIGH)) + bias_out
    first = layer_norm(block + attn, gain_one, shift_one)
    pre = lax.dot_general(low(first), w_in, (((1,), (1,)), ((), ())), precision=HIGH) + bias_in
    pre = low_back(pre)
    active = low(jax.nn.gelu(pre, approximate=False))
    branch = low_back(jnp.dot(active, w_down, precision=HIGH)) + bias_down
    return layer_norm(first + branch, gain_two, shift_two)

def reference(tokens, w_qkv, bias_q, bias_v, w_out, bias_out, norm1_gain, norm1_bias, w_in, bias_in, w_down, bias_down, norm2_gain, norm2_bias, mask_logits, mask_noise, grad_out):
    params = tuple((p.astype(jnp.float32) for p in (w_qkv, bias_q, bias_v, w_out, bias_out, norm1_gain, norm1_bias, w_in, bias_in, w_down, bias_down, norm2_gain, norm2_bias)))
    inputs = tokens.astype(jnp.float32)
    total = inputs.shape[0]
    width = inputs.shape[1]
    n_sequences = total // SEQ
    group = math.gcd(n_sequences, 8)

    def forward(weights, logits, rows):
        mask_value = relaxed_mask(logits, mask_noise)
        blocks = rows.reshape(n_sequences // group, group * SEQ, width)
        stepper = jax.checkpoint(lambda block: block_forward(weights, mask_value, block))
        result = lax.map(stepper, blocks)
        return result.reshape(total, width)
    result, pullback = jax.vjp(forward, params, mask_logits.astype(jnp.float32), inputs)
    grad_params, grad_logits, grad_rows = pullback(grad_out.astype(jnp.float32))
    return (result.astype(jnp.bfloat16), grad_rows.astype(jnp.bfloat16), grad_params[0], grad_params[1], grad_params[2], grad_params[3], grad_params[4], grad_params[5], grad_params[6], grad_params[7], grad_params[8], grad_params[9], grad_params[10], grad_params[11], grad_params[12], grad_logits)
```

```python
import functools

import jax
import jax.numpy as jnp
from jax import lax
from jax.experimental import pallas as pl
from jax.experimental.pallas import tpu as pltpu
from jax.sharding import PartitionSpec as P

MASK_SCALE = 4.0

BF = jnp.bfloat16
F32 = jnp.float32
NT = (((1,), (1,)), ((), ()))
NN = (((1,), (0,)), ((), ()))
TN = (((0,), (0,)), ((), ()))
VMEM_LIMIT = 56 * 1024 * 1024
SIZES = (8, 4, 4)

def cost(us):
    return pl.CostEstimate(flops=int(us * 1.0e9), transcendentals=0, bytes_accessed=int(us * 2.0e6))

def dot(a, b, dims=NN):
    return lax.dot_general(a, b, dims, preferred_element_type=F32)

def identity(n):
    return (lax.broadcasted_iota(jnp.int32, (n, n), 0) == lax.broadcasted_iota(jnp.int32, (n, n), 1)).astype(F32).astype(BF)

def params(*sem):
    return pltpu.CompilerParams(dimension_semantics=sem or None, vmem_limit_bytes=VMEM_LIMIT)

def place_mask(order_ref, pieces, codes, bias, eye):
    slots = 16
    rows = codes.shape[0] // slots
    for head in range(2):
        for slot in range(slots):
            group = pieces[head * 4 + slot // 4]
            start = pl.multiple_of(order_ref[head * slots + slot] * rows, rows)
            codes[pl.ds(start, rows), :] = group[slot % 4]
        turned = dot(eye, codes[...], NT)
        bias[head] = jnp.where(turned > 0.0, turned - 4.0, turned)

def halves(seqs, length, lane):
    half = seqs // 2
    return [pl.BlockSpec((length, lane), lambda s, *_: (jnp.minimum(s, half - 1), 0)),
            pl.BlockSpec((length, lane), lambda s, *_: (jnp.maximum(s - half, 0), 0))]

def attend_body(order_ref, q_ref, k_ref, v_ref, *refs):
    pieces, (own_ref, other_ref, total_ref), (codes, bias) = refs[:8], refs[8:11], refs[11:]
    length = codes.shape[0]
    @pl.when(pl.program_id(0) == 0)
    def _():
        place_mask(order_ref, pieces, codes, bias, identity(length))
    half = q_ref.shape[2] // 2
    lanes = lax.broadcasted_iota(jnp.int32, (1, 2 * half), 1)
    query, keys = q_ref[0], k_ref[0]
    values_t = v_ref[0].T
    outs = []
    for head in range(2):
        own = (lanes >= half) if head else (lanes < half)
        scores = dot(keys, jnp.where(own, query, jnp.zeros_like(query)), NT) + bias[head]
        highest = jnp.max(scores, axis=0, keepdims=True)
        powers = jnp.exp(scores - highest)
        summed = jnp.sum(powers, axis=0, keepdims=True)
        probs = (powers * (1.0 / summed)).astype(BF)
        outs.append(dot(values_t[head * half:(head + 1) * half], probs))
        total_ref[0, head:head + 1, :] = highest + jnp.log(summed)
    mixed = jnp.concatenate(outs, axis=0).T.astype(BF)
    step = pl.program_id(0)
    @pl.when(step < pl.num_programs(0) // 2)
    def _():
        own_ref[...] = mixed
    @pl.when(step >= pl.num_programs(0) // 2)
    def _():
        other_ref[...] = mixed

def attend(pair, order, qkv, pieces):
    _, tokens, width = qkv.shape
    length = pieces[0].shape[2]
    seqs = tokens // length
    lane = 128
    def part(which):
        return pl.BlockSpec((1, length, lane), lambda s, o: (which, s, pair))
    whole = [pl.BlockSpec(p.shape, lambda s, o: (0, 0, 0)) for p in pieces]
    return pl.pallas_call(
        attend_body,
        grid_spec=pltpu.PrefetchScalarGridSpec(
            num_scalar_prefetch=1, grid=(seqs,),
            in_specs=[part(0), part(1), part(2), *whole],
            out_specs=[*halves(seqs, length, lane), pl.BlockSpec((1, 8, length), lambda s, o: (s, 0, 0))],
            scratch_shapes=[pltpu.VMEM((length, length), BF), pltpu.VMEM((2, length, length), F32)],
        ),
        out_shape=[jax.ShapeDtypeStruct((tokens // 2, lane), BF)] * 2 + [jax.ShapeDtypeStruct((seqs, 8, length), F32)],
        compiler_params=params("arbitrary"),
        cost_estimate=cost(9),
        name="attend",
    )(order, qkv, qkv, qkv, *pieces)

def attend_back_body(order_ref, q_ref, k_ref, v_ref, mixed_own, mixed_other, ga_own, ga_other, wout_ref, total_ref, *refs):
    pieces, (own_ref, other_ref), mask_outs, (codes, bias, acc) = refs[:8], refs[8:10], refs[10:16], refs[16:]
    length = codes.shape[0]
    step = pl.program_id(0)
    @pl.when(step == 0)
    def _():
        place_mask(order_ref, pieces, codes, bias, identity(length))
        acc[...] = jnp.zeros_like(acc)
    half = q_ref.shape[2] // 2
    lanes = lax.broadcasted_iota(jnp.int32, (1, 2 * half), 1)
    query, keys, values = q_ref[0], k_ref[0], v_ref[0]
    keys_t = keys.T
    is_own = step < pl.num_programs(0) // 2
    grad = dot(jnp.where(is_own, ga_own[...], ga_other[...]), wout_ref[...], NT).astype(BF)
    mixed = jnp.where(is_own, mixed_own[...], mixed_other[...])
    inner = (grad.astype(F32) * mixed.astype(F32)).T
    dq, dk, dv = [], [], []
    for head in range(2):
        own = (lanes >= half) if head else (lanes < half)
        scores = dot(keys, jnp.where(own, query, jnp.zeros_like(query)), NT) + bias[head]
        probs = jnp.exp(scores - total_ref[0, head:head + 1, :])
        delta = jnp.sum(inner[head * half:(head + 1) * half], axis=0, keepdims=True)
        grad_probs = dot(values, jnp.where(own, grad, jnp.zeros_like(grad)), NT)
        grad_scores = probs * (grad_probs - delta)
        acc[head] += grad_scores
        low = grad_scores.astype(BF)
        dv.append(dot(probs.astype(BF), grad))
        dk.append(dot(low, query))
        dq.append(dot(keys_t[head * half:(head + 1) * half], low))
    first = lanes < half
    result = jnp.concatenate([(jnp.concatenate(dq, axis=0).T * 0.125).astype(BF),
                              jnp.where(first, dk[0], dk[1]).astype(BF),
                              jnp.where(first, dv[0], dv[1]).astype(BF)], axis=1)
    @pl.when(is_own)
    def _():
        own_ref[...] = result
    @pl.when(jnp.logical_not(is_own))
    def _():
        other_ref[...] = result
    @pl.when(step == pl.num_programs(0) - 1)
    def _():
        eye = identity(length)
        rows = length // 16
        for head in range(2):
            turned = dot(eye, acc[head].astype(BF), NT)
            acc[head] = turned
            at = 16
            for i, size in enumerate(SIZES):
                at -= size
                for j in range(size):
                    start = pl.multiple_of(order_ref[head * 16 + at + j] * rows, rows)
                    mask_outs[head * 3 + i][j] = acc[head, pl.ds(start, rows), :].astype(BF)

def attend_back(pair, order, qkv, mixed, grad_attn, w_out_own, total, pieces):
    _, tokens, width = qkv.shape
    length = pieces[0].shape[2]
    seqs = tokens // length
    rows = length // 16
    lane = 128
    wide = grad_attn[0].shape[1]
    def part(which):
        return pl.BlockSpec((1, length, lane), lambda s, o: (which, s, pair))
    whole = [pl.BlockSpec(p.shape, lambda s, o: (0, 0, 0)) for p in pieces]
    sizes = SIZES * 2
    return pl.pallas_call(
        attend_back_body,
        grid_spec=pltpu.PrefetchScalarGridSpec(
            num_scalar_prefetch=1, grid=(seqs,),
            in_specs=[part(0), part(1), part(2), *halves(seqs, length, lane), *halves(seqs, length, wide),
                      pl.BlockSpec((lane, wide), lambda s, o: (pair, 0)),
                      pl.BlockSpec((1, 8, length), lambda s, o: (s, 0, 0)), *whole],
            out_specs=halves(seqs, length, 3 * lane) + [pl.BlockSpec((n, rows, length), lambda s, o: (0, 0, 0)) for n in sizes],
            scratch_shapes=[pltpu.VMEM((length, length), BF), pltpu.VMEM((2, length, length), F32), pltpu.VMEM((2, length, length), F32)],
        ),
        out_shape=[jax.ShapeDtypeStruct((tokens // 2, 3 * lane), BF)] * 2 + [jax.ShapeDtypeStruct((n, rows, length), BF) for n in sizes],
        compiler_params=params("arbitrary"),
        cost_estimate=cost(13),
        name="attend_back",
    )(order, qkv, qkv, qkv, *mixed, *grad_attn, w_out_own, total, *pieces)

def full(shape):
    return pl.BlockSpec(shape, lambda *_: (0,) * len(shape))

def project_body(core_ref, own_ref, other_ref, w_ref, shift_ref, out_ref):
    third = pl.program_id(0)
    scale = jnp.where(third == 0, 0.125, 1.0)
    rows = own_ref.shape[0]
    for i, ref in enumerate((own_ref, other_ref)):
        value = (dot(ref[...], w_ref[...]) + shift_ref[...]).astype(BF)
        out_ref[0, i * rows:(i + 1) * rows] = (value.astype(F32) * scale).astype(BF)

def project(core, own_tokens, other_tokens, w_qkv, shift):
    rows, width = own_tokens.shape
    own = width // 2
    return pl.pallas_call(
        project_body,
        grid_spec=pltpu.PrefetchScalarGridSpec(
            num_scalar_prefetch=1, grid=(3,),
            in_specs=[full((rows, width)), full((rows, width)),
                      pl.BlockSpec((width, own), lambda t, c: (0, 2 * t + c[0])),
                      pl.BlockSpec((1, own), lambda t, c: (0, 2 * t + c[0]))],
            out_specs=pl.BlockSpec((1, 2 * rows, own), lambda t, c: (t, 0, 0)),
        ),
        out_shape=jax.ShapeDtypeStruct((3, 2 * rows, own), BF),
        compiler_params=params("arbitrary"),
        cost_estimate=cost(8),
        name="project",
    )(core, own_tokens, other_tokens, w_qkv, shift)

def erf_parts(u):
    x = jnp.abs(u) * 0.7071067811865476
    t = 1.0 / (1.0 + 0.3275911 * x)
    e = jnp.exp(-0.5 * u * u)
    poly = t * (0.127414796 + t * (-0.142248368 + t * (0.7107068705 + t * (-0.7265760135 + t * 0.5307027145))))
    tail = poly * e
    return jnp.where(u < 0.0, tail, 1.0 - tail), e * 0.3989422804014327

def row_mean(v):
    return jnp.mean(v, axis=-1, keepdims=True)

def ffn_body(*refs):
    tok_ref, gout_ref = refs[:2]
    mixed, (wout_ref, vec_ref, bin_ref), w_in, w_down = refs[2:8], refs[8:11], refs[11:15], refs[15:19]
    out_ref, low_ref, active_ref, slope_ref, gsec_ref, gbr_ref, norm_ref, inv_ref, sums_ref = refs[19:]
    bias_out, gain1, shift1, bias_down, gain2, shift2 = (vec_ref[i:i + 1] for i in range(6))
    gathered = jnp.concatenate([m[...] for m in mixed], axis=1)
    value = tok_ref[...].astype(F32) + dot(gathered, wout_ref[...]) + bias_out
    centered = value - row_mean(value)
    inverse = lax.rsqrt(row_mean(centered * centered) + 1e-12)
    normal = centered * inverse
    norm_ref[...] = normal
    inv_ref[...] = jnp.broadcast_to(inverse, inv_ref.shape)
    first = normal * gain1 + shift1
    low = first.astype(BF)
    low_ref[...] = low
    width = low.shape[1]
    branch = first + bias_down
    for b in range(4):
        pre = dot(low, w_in[b][...], NT) + bin_ref[b:b + 1]
        cum, dens = erf_parts(pre)
        act = (pre * cum).astype(BF)
        active_ref[:, b * width:(b + 1) * width] = act
        slope_ref[:, b * width:(b + 1) * width] = (cum + pre * dens).astype(slope_ref.dtype)
        branch += dot(act, w_down[b][...])
    centered = branch - row_mean(branch)
    inverse = lax.rsqrt(row_mean(centered * centered) + 1e-12)
    normal = centered * inverse
    out_ref[...] = (normal * gain2 + shift2).astype(BF)
    grad = gout_ref[...].astype(F32)
    inner = grad * gain2
    back = inverse * (inner - row_mean(inner) - normal * row_mean(inner * normal))
    gsec_ref[...] = back
    gbr_ref[...] = back.astype(BF)
    @pl.when(pl.program_id(0) == 0)
    def _():
        sums_ref[...] = jnp.zeros_like(sums_ref)
    total = lambda v: jnp.sum(v, axis=0, keepdims=True)
    sums_ref[0:1] += total(grad * normal)
    sums_ref[1:2] += total(grad)
    sums_ref[2:3] += total(back)

def ffn(tokens, grad_out, mixed, w_out, vecs, b_in, w_in, w_down, tile=256):
    rows, width = tokens.shape
    hidden = 4 * width
    row = lambda n: pl.BlockSpec((tile, n), lambda i: (i, 0))
    sds = jax.ShapeDtypeStruct
    return pl.pallas_call(
        ffn_body,
        grid=(rows // tile,),
        in_specs=[row(width), row(width)] + [row(m.shape[1]) for m in mixed]
        + [full(a.shape) for a in (w_out, vecs, b_in, *w_in, *w_down)],
        out_specs=[row(width), row(width), row(hidden), row(hidden), row(width), row(width), row(width), row(128), full((8, width))],
        out_shape=[sds((rows, width), BF), sds((rows, width), BF), sds((rows, hidden), BF), sds((rows, hidden), BF),
                   sds((rows, width), F32), sds((rows, width), BF), sds((rows, width), F32), sds((rows, 128), F32), sds((8, width), F32)],
        compiler_params=params("arbitrary"),
        cost_estimate=cost(30),
        name="ffn",
    )(tokens, grad_out, *mixed, w_out, vecs, b_in, *w_in, *w_down)

def ffn_back_body(*refs):
    gbr_ref, slope_ref, gsec_ref, norm_ref, inv_ref, vec_ref = refs[:6]
    w_in, w_down = refs[6:10], refs[10:14]
    gpre_ref, gone_ref, gattn_ref, sums_ref = refs[14:]
    gain1 = vec_ref[1:2]
    @pl.when(pl.program_id(0) == 0)
    def _():
        sums_ref[...] = jnp.zeros_like(sums_ref)
    total = lambda v: jnp.sum(v, axis=0, keepdims=True)
    width = gbr_ref.shape[1]
    grad = gsec_ref[...]
    low = gbr_ref[...]
    for b in range(4):
        at = slice(b * width, (b + 1) * width)
        gpre = (dot(low, w_down[b][...], NT) * slope_ref[:, at].astype(F32)).astype(BF)
        gpre_ref[:, at] = gpre
        sums_ref[4 + b:5 + b] += total(gpre.astype(F32))
        grad += dot(gpre, w_in[b][...])
    normal, inverse = norm_ref[...], inv_ref[:, 0:1]
    inner = grad * gain1
    back = inverse * (inner - row_mean(inner) - normal * row_mean(inner * normal))
    gone_ref[...] = back
    gattn_ref[...] = back.astype(BF)
    sums_ref[0:1] += total(grad * normal)
    sums_ref[1:2] += total(grad)
    sums_ref[2:3] += total(back)

def ffn_back(grad_branch, slope, grad_second, normal, inverse, vecs, w_in, w_down, tile=256):
    rows, width = grad_branch.shape
    hidden = 4 * width
    row = lambda n: pl.BlockSpec((tile, n), lambda i: (i, 0))
    sds = jax.ShapeDtypeStruct
    return pl.pallas_call(
        ffn_back_body,
        grid=(rows // tile,),
        in_specs=[row(width), row(hidden), row(width), row(width), row(128)] + [full(a.shape) for a in (vecs, *w_in, *w_down)],
        out_specs=[row(hidden), row(width), row(width), full((8, width))],
        out_shape=[sds((rows, hidden), BF), sds((rows, width), F32), sds((rows, width), BF), sds((8, width), F32)],
        compiler_params=params("arbitrary"),
        cost_estimate=cost(18),
        name="ffn_back",
    )(grad_branch, slope, grad_second, normal, inverse, vecs, *w_in, *w_down)

def outer_send_body(a_ref, b_ref, out_ref):
    out_ref[0] = dot(a_ref[...], b_ref[...], TN).astype(BF)

def outer_send(a, b):
    rows, width = b.shape
    return pl.pallas_call(
        outer_send_body,
        grid=(2,),
        in_specs=[pl.BlockSpec((rows, width), lambda i: (0, 2 * i + 1)), full((rows, width))],
        out_specs=pl.BlockSpec((1, width, width), lambda i: (i, 0, 0)),
        out_shape=jax.ShapeDtypeStruct((2, width, width), BF),
        compiler_params=params("arbitrary"),
        cost_estimate=cost(6),
        name="outer_send",
    )(a, b)

def outer_keep_body(a_ref, b_ref, add_ref, keep_ref, send_ref):
    value = dot(a_ref[...], b_ref[...], TN) + add_ref[0].astype(F32)
    @pl.when(pl.program_id(0) == 0)
    def _():
        send_ref[...] = value.astype(BF)
    @pl.when(pl.program_id(0) == 1)
    def _():
        keep_ref[...] = value

def outer_keep(a, b, add):
    rows, width = b.shape
    return pl.pallas_call(
        outer_keep_body,
        grid=(2,),
        in_specs=[pl.BlockSpec((rows, width), lambda i: (0, 2 - 2 * i)), full((rows, width)),
                  pl.BlockSpec((1, width, width), lambda i: (1 - i, 0, 0))],
        out_specs=[full((width, width)), full((width, width))],
        out_shape=[jax.ShapeDtypeStruct((width, width), F32), jax.ShapeDtypeStruct((width, width), BF)],
        compiler_params=params("arbitrary"),
        cost_estimate=cost(7),
        name="outer_keep",
    )(a, b, add)

def outer_slots_body(order_ref, a_own, a_other, *refs):
    bs, outs, (sums_ref, acc) = refs[:-5], refs[-5:-2], refs[-2:]
    count = len(bs) // 2
    own, other = (jnp.concatenate([r[...] for r in part], axis=1) if count > 1 else part[0][...] for part in (bs[:count], bs[count:]))
    acc[...] = dot(a_own[...], own, TN) + dot(a_other[...], other, TN)
    sums_ref[0:1] = jnp.sum(own.astype(F32), axis=0, keepdims=True) + jnp.sum(other.astype(F32), axis=0, keepdims=True)
    at = 16
    rows = acc.shape[0] // 16
    for out, size in zip(outs, SIZES):
        at -= size
        for j in range(size):
            start = pl.multiple_of(order_ref[at + j] * rows, rows)
            out[j] = acc[pl.ds(start, rows), :].astype(BF)

def outer_slots(order, a, own, other):
    width = a[0].shape[1]
    wide = sum(b.shape[1] for b in own)
    shapes = [(n, width // 16, wide) for n in SIZES]
    return pl.pallas_call(
        outer_slots_body,
        grid_spec=pltpu.PrefetchScalarGridSpec(
            num_scalar_prefetch=1, grid=(1,),
            in_specs=[full(x.shape) for x in (*a, *own, *other)],
            out_specs=[full(s) for s in shapes] + [full((8, wide))],
            scratch_shapes=[pltpu.VMEM((width, wide), F32)],
        ),
        out_shape=[jax.ShapeDtypeStruct(s, BF) for s in shapes] + [jax.ShapeDtypeStruct((8, wide), F32)],
        compiler_params=params("arbitrary"),
        cost_estimate=cost(5.6),
        name="outer_slots",
    )(order, *a, *own, *other)

def grad_tokens_body(*refs):
    pieces, one_ref, w_ref, out_ref = refs[:6], refs[6], refs[7], refs[8]
    wide = jnp.concatenate([r[...] for r in pieces], axis=1)
    out_ref[...] = (one_ref[...] + dot(wide, w_ref[...], NT)).astype(BF)

def grad_tokens(pieces, grad_one, w, tile=256):
    rows, width = grad_one.shape
    row = lambda n: pl.BlockSpec((tile, n), lambda i: (i, 0))
    return pl.pallas_call(
        grad_tokens_body,
        grid=(rows // tile,),
        in_specs=[row(p.shape[1]) for p in pieces] + [row(width), full(w.shape)],
        out_specs=row(width),
        out_shape=jax.ShapeDtypeStruct((rows, width), BF),
        compiler_params=params("arbitrary"),
        cost_estimate=cost(6),
        name="grad_tokens",
    )(*pieces, grad_one, w)

def place_rows_body(order_ref, *refs):
    pieces, out_ref = refs[:-1], refs[-1]
    rows = pieces[0].shape[1]
    at = 0
    for piece in pieces:
        for j in range(piece.shape[0]):
            start = pl.multiple_of(order_ref[at] * rows, rows)
            out_ref[pl.ds(start, rows), :] = piece[j].astype(F32)
            at += 1

def place_rows(order, pieces):
    count = sum(p.shape[0] for p in pieces)
    _, rows, width = pieces[0].shape
    return pl.pallas_call(
        place_rows_body,
        grid_spec=pltpu.PrefetchScalarGridSpec(
            num_scalar_prefetch=1, grid=(1,), in_specs=[full(p.shape) for p in pieces], out_specs=full((count * rows, width))),
        out_shape=jax.ShapeDtypeStruct((count * rows, width), F32),
        compiler_params=params("arbitrary"),
        cost_estimate=cost(2),
        name="place_rows",
    )(order, *pieces)

def place_heads_body(order_ref, core_ref, *refs):
    pieces, out_ref = refs[:-1], refs[-1]
    width = out_ref.shape[0]
    per = len(pieces) // 6
    for pair in range(3):
        for side in range(2):
            own = pieces[(pair * 2 + side) * per:(pair * 2 + side + 1) * per]
            rows = own[0].shape[1]
            at = 0
            head = core_ref[side] * 3 + pair
            for piece in own:
                for j in range(piece.shape[0]):
                    start = pl.multiple_of(order_ref[pair * 16 + at] * rows, rows)
                    value = piece[j].astype(F32)
                    for third in range(3):
                        column = pl.multiple_of(third * width + head * 128, 128)
                        out_ref[pl.ds(start, rows), pl.ds(column, 128)] = value[:, third * 128:(third + 1) * 128]
                    at += 1

def place_heads(order, core, pieces):
    width = 16 * pieces[0].shape[1]
    return pl.pallas_call(
        place_heads_body,
        grid_spec=pltpu.PrefetchScalarGridSpec(
            num_scalar_prefetch=2, grid=(1,), in_specs=[full(p.shape) for p in pieces], out_specs=full((width, 3 * width))),
        out_shape=jax.ShapeDtypeStruct((width, 3 * width), F32),
        compiler_params=params("arbitrary"),
        cost_estimate=cost(5),
        name="place_heads",
    )(order, core, *pieces)

def place_turned_body(order_ref, core_ref, *refs):
    pieces, out_ref, acc = refs[:-2], refs[-2], refs[-1]
    per = len(pieces) // 2
    wide = acc.shape[1]
    for side in range(2):
        at = 0
        for piece in pieces[side * per:(side + 1) * per]:
            rows = piece.shape[1]
            for j in range(piece.shape[0]):
                start = pl.multiple_of(order_ref[at] * rows, rows)
                acc[pl.ds(start, rows), :] = piece[j].astype(F32)
                at += 1
        start = pl.multiple_of(core_ref[side] * wide, wide)
        out_ref[pl.ds(start, wide), :] = acc[...].T

def place_turned(order, core, pieces):
    _, rows, wide = pieces[0].shape
    width = 16 * rows
    return pl.pallas_call(
        place_turned_body,
        grid_spec=pltpu.PrefetchScalarGridSpec(
            num_scalar_prefetch=2, grid=(1,), in_specs=[full(p.shape) for p in pieces], out_specs=full((2 * wide, width)),
            scratch_shapes=[pltpu.VMEM((width, wide), F32)]),
        out_shape=jax.ShapeDtypeStruct((2 * wide, width), F32),
        compiler_params=params("arbitrary"),
        cost_estimate=cost(4),
        name="place_turned",
    )(order, core, *pieces)


AXES = ("dp", "mp")
CORE, ROW, COLUMN, DEPTH = 1, 2, 4, 8


class Links:
    def __init__(self, dp, mp):
        self.dp, self.mp = dp, mp
        self.direct = dp == 8 and mp == 4
        self.at_dp, self.at_mp = lax.axis_index("dp"), lax.axis_index("mp")
        self.core, self.row = self.at_mp % 2, self.at_mp // 2
        slot = jnp.arange(16)
        z, low, high = slot & 3, (slot >> 2) & 1, slot >> 3
        if self.direct:
            def chip(x, y):
                return ((self.at_dp ^ (x | (z << 1))) * 2 + (self.row ^ y)).astype(jnp.int32)
            self.order_a, self.order_b = chip(low, high), chip(high, low)
            self.eighths = (self.at_dp ^ (((slot[:8] >> 2) & 1) | ((slot[:8] & 3) << 1))).astype(jnp.int32)
        else:
            self.order_a = self.order_b = slot.astype(jnp.int32)
            self.eighths = slot[:8].astype(jnp.int32)
        self.cores = jnp.stack([self.core, 1 - self.core]).astype(jnp.int32)

    def swap(self, value, bits):
        count = self.dp * self.mp
        return lax.ppermute(value, AXES, [(i, i ^ bits) for i in range(count)])

    def add_all(self, value):
        if not self.direct:
            return lax.psum(value, AXES)
        for bits in (1, 2, 4, 8, 16):
            value = value + self.swap(value, bits)
        return value


def pick(index, first, second):
    return jnp.where(index == 0, first, second)


def mask_codes(links, code):
    heads, rows, length = code.shape
    half = heads // 2
    if not links.direct:
        whole = lax.all_gather(code, AXES, axis=1, tiled=True)
        own = lax.dynamic_slice_in_dim(whole, links.core * half, half, 0).reshape(half, 16, length // 16, length)
        return [[own[2 * p + h, 4 * i:4 * i + 4] for h in range(2) for i in range(4)] for p in range(half // 2)]
    keep = pick(links.core, code[:half], code[half:])
    came = links.swap(pick(links.core, code[half:], code[:half]), CORE)
    chip = pick(links.core, jnp.concatenate([keep, came], 1), jnp.concatenate([came, keep], 1))
    result = []
    for p in range(half // 2):
        own = chip[2 * p:2 * p + 2]
        deep = [own] + [links.swap(own, k * DEPTH) for k in (1, 2, 3)]
        pieces = []
        for h, (near, far) in enumerate(((COLUMN, ROW), (ROW, COLUMN))):
            group = jnp.stack([d[h] for d in deep])
            second = links.swap(group, near)
            pieces += [group, second, links.swap(group, far), links.swap(second, far)]
        result.append(pieces)
    return result


def scatter_slots(links, slots, far, near):
    away, mid, last = slots
    came = links.swap(away, far)
    came_mid = links.swap((mid.astype(F32) + came[4:].astype(F32)).astype(BF), near)
    total = last.astype(F32) + came[:4].astype(F32) + came_mid.astype(F32)
    own = total[0]
    for k in (1, 2, 3):
        own = own + links.swap(total[k].astype(BF), k * DEPTH).astype(F32)
    return own


def gather_slots(links, own, far, near):
    group = jnp.concatenate([own] + [links.swap(own, k * DEPTH) for k in (1, 2, 3)])
    second = links.swap(group, near)
    return [group, second, links.swap(group, far), links.swap(second, far)]


def sum_slots(links, slots, far, near):
    if not links.direct:
        whole = jnp.concatenate(slots[::-1])
        own = lax.psum(whole.astype(F32), "dp")
        parts = lax.all_gather(own, "mp")
        own = parts[links.core] + parts[links.core + 2]
        other = parts[1 - links.core] + parts[3 - links.core]
        return [own], [other]
    own = scatter_slots(links, slots, far, near)
    groups = gather_slots(links, own.astype(BF)[None], far, near)
    return groups, [links.swap(g, CORE) for g in groups]


def in_slots(links, value):
    if not links.direct:
        return value
    eighth = value.shape[0] // 8
    parts = [lax.dynamic_slice_in_dim(value, links.eighths[r] * eighth, eighth, 0) for r in range(8)]
    return jnp.concatenate(parts)


def weight_blocks(links, value, straight):
    if not links.direct:
        whole = lax.all_gather(value, "mp")
        return [whole[links.at_mp ^ k] for k in range(4)]
    own = in_slots(links, value)
    eighth = own.shape[0] // 8
    beside = links.swap(own, CORE)
    first = links.swap(own[:eighth], ROW)
    group = jnp.concatenate([first] + [links.swap(first, k * DEPTH) for k in (1, 2, 3)])
    rest = links.swap(own[4 * eighth:], ROW) if straight else links.swap(group, COLUMN)
    across = jnp.concatenate([group, rest])
    return [own, beside, across, links.swap(across, CORE)]


def hidden_gradient(links, a, b):
    sent = outer_send(a, b)
    if not links.direct:
        zero = jnp.zeros_like(sent)
        keep, near = outer_keep(a, b, zero)
        blocks = jnp.stack([keep, sent[0].astype(F32), near.astype(F32), sent[1].astype(F32)])
        blocks = jnp.stack([blocks[links.at_mp ^ k] for k in range(4)])
        mine = lax.psum_scatter(blocks, "mp", scatter_dimension=0, tiled=False)
        return lax.psum(mine, "dp")
    keep, near = outer_keep(a, b, links.swap(sent, CORE))
    eighth = keep.shape[0] // 8
    came = links.swap(near, ROW)
    total = keep + came.astype(F32)
    beside = links.swap(total[4 * eighth:].astype(BF), COLUMN)
    total = total[:4 * eighth] + beside.astype(F32)
    own = total[:eighth]
    for k in (1, 2, 3):
        own = own + links.swap(total[k * eighth:(k + 1) * eighth].astype(BF), k * DEPTH).astype(F32)
    own = own.astype(BF)[None]
    group = jnp.concatenate([own] + [links.swap(own, k * DEPTH) for k in (1, 2, 3)])
    return place_rows(links.eighths, [group, links.swap(group, COLUMN)])


def body(dp, mp, tokens, w_qkv, bias_q, bias_v, w_out, bias_out, norm1_gain, norm1_bias, w_in, bias_in, w_down, bias_down,
         norm2_gain, norm2_bias, mask_logits, mask_noise, grad_out):
    width = w_out.shape[0]
    heads, rows_own, length = mask_logits.shape
    half = heads // 2
    links = Links(dp, mp)
    core = links.core
    fraction = mask_noise.astype(F32) / 65536.0
    logit = mask_logits + jnp.log(fraction) - jnp.log(1.0 - fraction)
    mask_own = jax.nn.sigmoid(logit)
    tail = jax.nn.sigmoid(-jnp.abs(logit)) * MASK_SCALE
    pieces = mask_codes(links, jnp.where(logit < 0.0, tail, -tail).astype(BF))
    both = jnp.concatenate([links.order_a, links.order_b])
    other_tokens = links.swap(tokens, CORE)
    wide = lambda v: v.astype(F32)
    shift = jnp.concatenate([wide(bias_q), jnp.zeros((width,), F32), wide(bias_v)])[None]
    qkv = project(links.cores[:1], tokens, other_tokens, w_qkv, shift)
    own_side = lax.dynamic_slice_in_dim(w_out, core * (width // 2), width // 2, 0)
    other_side = lax.dynamic_slice_in_dim(w_out, (1 - core) * (width // 2), width // 2, 0)
    w_out_sides = jnp.concatenate([own_side, other_side])
    columns = w_qkv.reshape(width, 3, 2, 3, 128).transpose(2, 0, 3, 1, 4).reshape(2, width, 3 * width // 2)
    w_qkv_sides = jnp.concatenate([columns[core], columns[1 - core]], axis=1)
    blocks_in = weight_blocks(links, w_in, False)
    blocks_down = weight_blocks(links, w_down, True)
    if links.direct:
        own_bias = in_slots(links, bias_in)
        pair_bias = jnp.stack([own_bias, links.swap(own_bias, CORE)])
        blocks_bias = jnp.concatenate([pair_bias, links.swap(pair_bias, ROW)]).astype(F32)
    else:
        blocks_bias = lax.all_gather(bias_in, "mp")
        blocks_bias = jnp.stack([blocks_bias[links.at_mp ^ k] for k in range(4)]).astype(F32)
    mixed, totals = [], []
    for p in range(half // 2):
        own, other, total = attend(p, both, qkv, pieces[p])
        mixed.append((own, other))
        totals.append(total)
    came = [links.swap(other, CORE) for _, other in mixed]
    vecs = jnp.stack([wide(v) for v in (bias_out, norm1_gain, norm1_bias, bias_down, norm2_gain, norm2_bias)]
                     + [jnp.zeros((width,), F32)] * 2)
    out, first_low, active, slope, grad_second, grad_branch, normal, inverse, sums_a = ffn(
        tokens, grad_out, [own for own, _ in mixed] + came, w_out_sides, vecs, blocks_bias, blocks_in, blocks_down)
    grad_w_down = hidden_gradient(links, active, grad_branch)
    grad_pre, grad_one, grad_attn, sums_b = ffn_back(
        grad_branch, slope, grad_second, normal, inverse, vecs, blocks_in, blocks_down)
    other_attn = links.swap(grad_attn, CORE)
    grad_w_in = hidden_gradient(links, grad_pre, first_low)
    chip_tokens = (tokens, other_tokens)
    *slots, _ = outer_slots(links.order_b, (grad_attn, other_attn), [own for own, _ in mixed], [other for _, other in mixed])
    own, other = sum_slots(links, slots, COLUMN, ROW)
    grad_w_out = place_turned(links.order_b, links.cores, own + other)
    mask_sums, d_own, d_other, placed, column_sums, orders = [], [], [], [], [], []
    for p in range(half // 2):
        own, other, *slots = attend_back(p, both, qkv, mixed[p], (grad_attn, other_attn), own_side, totals[p], pieces[p])
        d_own.append(own)
        d_other.append(links.swap(other, CORE))
        if links.direct:
            mask_sums.append(scatter_slots(links, slots[:3], ROW, COLUMN))
            mask_sums.append(scatter_slots(links, slots[3:], COLUMN, ROW))
        else:
            mask_sums += [jnp.concatenate(slots[3 * h:3 * h + 3][::-1]).reshape(length, length) for h in range(2)]
        far, near, order = ((ROW, COLUMN, links.order_a), (COLUMN, ROW, links.order_b))[p % 2]
        *slots, sums = outer_slots(order, chip_tokens, [own], [other])
        column_sums.append(sums[0].reshape(3, 128))
        orders.append(order)
        for side in sum_slots(links, slots, far, near):
            placed += side
    grad_w_qkv = place_heads(jnp.concatenate(orders), links.cores, placed)
    grad_in = grad_tokens([*d_own, *d_other], grad_one, w_qkv_sides)
    mask_sum = jnp.stack(mask_sums)
    if links.direct:
        mine = pick(core, mask_sum[:, :rows_own], mask_sum[:, rows_own:])
        theirs = links.swap(pick(core, mask_sum[:, rows_own:], mask_sum[:, :rows_own]), CORE)
        mask_sum = pick(core, jnp.concatenate([mine, theirs]), jnp.concatenate([theirs, mine]))
    else:
        zero = jnp.zeros_like(mask_sum)
        mask_sum = pick(core, jnp.concatenate([mask_sum, zero]), jnp.concatenate([zero, mask_sum])).astype(F32)
        mask_sum = lax.psum_scatter(mask_sum, AXES, scatter_dimension=1, tiled=True)
    grad_mask_logits = mask_sum * (MASK_SCALE * mask_own * (1.0 - mask_own))
    hidden = jnp.stack([sums_b[4:8][links.at_mp ^ k] for k in range(4)])
    hidden = hidden.reshape(4, 8, width // 8)
    hidden = jnp.stack([hidden[:, (links.eighths if not links.direct else inverse_eighths(links))[r]] for r in range(8)], axis=1)
    small = jnp.concatenate([sums_a[:3], sums_b[:3], hidden.reshape(4, width)])
    small = links.add_all(small)
    grad_bias_in = small[6 + links.at_mp]
    bias = jnp.stack(column_sums, axis=1).reshape(3, width // 2)
    zero = jnp.zeros_like(bias)
    bias = links.add_all(pick(core, jnp.concatenate([bias, zero], 1), jnp.concatenate([zero, bias], 1)))
    return (out, grad_in, grad_w_qkv, bias[0], bias[2], grad_w_out, small[5], small[3], small[4], grad_w_in, grad_bias_in,
            grad_w_down, small[2], small[0], small[1], grad_mask_logits)


def inverse_eighths(links):
    place = jnp.arange(8) ^ links.at_dp
    return (((place & 1) << 2) | (place >> 1)).astype(jnp.int32)


def solution(mesh):
    both, none = ("dp", "mp"), P()
    rows, mask, split = P(both, None), P(None, both, None), P("mp", None)
    ins = (rows, none, none, none, none, none, none, none, split, P("mp"), split, none, none, none, mask, mask, rows)
    outs = (rows, rows, none, none, none, none, none, none, none, split, P("mp"), split, none, none, none, mask)
    step = functools.partial(body, mesh.shape["dp"], mesh.shape["mp"])
    return jax.shard_map(step, mesh=mesh, in_specs=ins, out_specs=outs, check_vma=False)
```

```python
import functools

import jax
import jax.numpy as jnp
from jax import lax
from jax.experimental import pallas as pl
from jax.experimental.pallas import tpu as pltpu
from jax.sharding import PartitionSpec as P

MASK_SCALE = 4.0

BF = jnp.bfloat16
F32 = jnp.float32
NT = (((1,), (1,)), ((), ()))
NN = (((1,), (0,)), ((), ()))
TN = (((0,), (0,)), ((), ()))
VMEM_LIMIT = 56 * 1024 * 1024
SIZES = (8, 4, 2, 2)

ORDER_A, ORDER_B, OWN_CORE, OTHER_CORE, PLACE = 0, 16, 32, 33, 34

COST = 0.05

def cost(us):
    return pl.CostEstimate(flops=int(us * 1.0e9 * COST), transcendentals=0, bytes_accessed=int(us * 2.0e6 * COST))

def dot(a, b, dims=NN):
    return lax.dot_general(a, b, dims, preferred_element_type=F32)

def identity(n):
    return (lax.broadcasted_iota(jnp.int32, (n, n), 0) == lax.broadcasted_iota(jnp.int32, (n, n), 1)).astype(F32).astype(BF)

def params(*sem):
    return pltpu.CompilerParams(dimension_semantics=sem or None, vmem_limit_bytes=VMEM_LIMIT)

def place_mask(order_ref, pieces, codes, bias, eye):
    rows = codes.shape[0] // 16
    for head in range(2):
        slot = 0
        for group in pieces[head * 3:head * 3 + 3]:
            for j in range(group.shape[0]):
                start = pl.multiple_of(order_ref[head * 16 + slot] * rows, rows)
                codes[pl.ds(start, rows), :] = group[j, 0]
                slot += 1
        turned = dot(eye, codes[...], NT)
        bias[head] = jnp.where(turned > 0.0, turned - 4.0, turned)

def halves(seqs, length, lane):
    half = seqs // 2
    return [pl.BlockSpec((length, lane), lambda i, s, *_: (jnp.minimum(s, half - 1), i)),
            pl.BlockSpec((length, lane), lambda i, s, *_: (jnp.maximum(s - half, 0), i))]

def mask_specs(pieces):
    return [pl.BlockSpec((p.shape[0], 1, *p.shape[2:]), lambda i, s, *_: (0, i, 0, 0)) for p in pieces]

def qkv_specs(first, length):
    def part(which):
        return pl.BlockSpec((1, length, 128), lambda i, s, *_: (which, s, first + i))
    return [part(0), part(1), part(2)]

def attend_body(order_ref, q_ref, k_ref, v_ref, *refs):
    pieces, (own_ref, other_ref, total_ref), (codes, bias) = refs[:6], refs[6:9], refs[9:]
    length = codes.shape[0]
    step, count = pl.program_id(1), pl.num_programs(1)
    @pl.when(step == 0)
    def _():
        place_mask(order_ref, pieces, codes, bias, identity(length))
    half = q_ref.shape[2] // 2
    lanes = lax.broadcasted_iota(jnp.int32, (1, 2 * half), 1)
    query, keys = q_ref[0], k_ref[0]
    values_t = v_ref[0].T
    outs = []
    for head in range(2):
        own = (lanes >= half) if head else (lanes < half)
        scores = dot(keys, jnp.where(own, query, jnp.zeros_like(query)), NT) + bias[head]
        highest = jnp.max(scores, axis=0, keepdims=True)
        powers = jnp.exp(scores - highest)
        summed = jnp.sum(powers, axis=0, keepdims=True)
        probs = (powers * (1.0 / summed)).astype(BF)
        outs.append(dot(values_t[head * half:(head + 1) * half], probs))
        total_ref[0, 0, head:head + 1, :] = highest + jnp.log(summed)
    mixed = jnp.concatenate(outs, axis=0).T.astype(BF)
    @pl.when(step < count // 2)
    def _():
        own_ref[...] = mixed
    @pl.when(step >= count // 2)
    def _():
        other_ref[...] = mixed

def attend(first, count, order, qkv, pieces):
    _, tokens, width = qkv.shape
    length = pieces[0].shape[3]
    seqs = tokens // length
    sds = jax.ShapeDtypeStruct
    return pl.pallas_call(
        attend_body,
        grid_spec=pltpu.PrefetchScalarGridSpec(
            num_scalar_prefetch=1, grid=(count, seqs),
            in_specs=qkv_specs(first, length) + mask_specs(pieces),
            out_specs=[*halves(seqs, length, 128), pl.BlockSpec((1, 1, 8, length), lambda i, s, *_: (i, s, 0, 0))],
            scratch_shapes=[pltpu.VMEM((length, length), BF), pltpu.VMEM((2, length, length), F32)],
        ),
        out_shape=[sds((tokens // 2, count * 128), BF)] * 2 + [sds((count, seqs, 8, length), F32)],
        compiler_params=params("arbitrary", "arbitrary"),
        cost_estimate=cost(9 * count),
        name="attend",
    )(order, qkv, qkv, qkv, *pieces)

def attend_back_body(groups, has_out, info_ref, *refs):
    (q_ref, k_ref, v_ref, mixed_own, mixed_other, ga_own, ga_other, wout_ref, total_ref, tok_own, tok_other), refs = refs[:11], refs[11:]
    pieces, refs = refs[:6], refs[6:]
    all_own, all_other, small_ref = (), (), None
    if has_out:
        all_own, all_other, small_ref, refs = refs[:has_out], refs[has_out:2 * has_out], refs[2 * has_out], refs[2 * has_out + 1:]
    own_ref, other_ref, refs = refs[0], refs[1], refs[2:]
    outs, refs = refs[:4 * len(groups)], refs[4 * len(groups):]
    codes, bias, acc, weight, extra = refs[:5]
    weight_out = refs[5] if has_out else None
    length = codes.shape[0]
    step, steps = pl.program_id(0), pl.num_programs(0)
    @pl.when(step == 0)
    def _():
        place_mask(info_ref, pieces, codes, bias, identity(length))
        acc[...] = jnp.zeros_like(acc)
        weight[...] = jnp.zeros_like(weight)
        extra[...] = jnp.zeros_like(extra)
        if has_out:
            extra[0:small_ref.shape[0], :] = small_ref[...]
            weight_out[...] = jnp.zeros_like(weight_out)
    half = q_ref.shape[2] // 2
    lanes = lax.broadcasted_iota(jnp.int32, (1, 2 * half), 1)
    query, keys, values = q_ref[0], k_ref[0], v_ref[0]
    keys_t = keys.T
    is_own = step < steps // 2
    grad_attn = jnp.where(is_own, ga_own[...], ga_other[...])
    grad = dot(grad_attn, wout_ref[...], NT).astype(BF)
    mixed = jnp.where(is_own, mixed_own[...], mixed_other[...])
    inner = (grad.astype(F32) * mixed.astype(F32)).T
    dq, dk, dv = [], [], []
    for head in range(2):
        own = (lanes >= half) if head else (lanes < half)
        scores = dot(keys, jnp.where(own, query, jnp.zeros_like(query)), NT) + bias[head]
        probs = jnp.exp(scores - total_ref[0, 0, head:head + 1, :])
        delta = jnp.sum(inner[head * half:(head + 1) * half], axis=0, keepdims=True)
        grad_probs = dot(values, jnp.where(own, grad, jnp.zeros_like(grad)), NT)
        grad_scores = probs * (grad_probs - delta)
        acc[head] += grad_scores
        low = grad_scores.astype(BF)
        dv.append(dot(probs.astype(BF), grad))
        dk.append(dot(low, query))
        dq.append(dot(keys_t[head * half:(head + 1) * half], low))
    first = lanes < half
    result = jnp.concatenate([(jnp.concatenate(dq, axis=0).T * 0.125).astype(BF),
                              jnp.where(first, dk[0], dk[1]).astype(BF),
                              jnp.where(first, dv[0], dv[1]).astype(BF)], axis=1)
    @pl.when(is_own)
    def _():
        own_ref[...] = result
    @pl.when(jnp.logical_not(is_own))
    def _():
        other_ref[...] = result
    weight[...] += dot(jnp.where(is_own, tok_own[...], tok_other[...]), result, TN)
    sums = jnp.sum(result.astype(F32), axis=0, keepdims=True)
    for third in range(3):
        extra[64 + third:65 + third, :] += sums[:, third * 128:(third + 1) * 128]
    if has_out:
        whole = jnp.where(is_own, jnp.concatenate([m[...] for m in all_own], axis=1),
                          jnp.concatenate([m[...] for m in all_other], axis=1))
        weight_out[...] += dot(grad_attn, whole, TN)
    rows, wrows = length // 16, weight.shape[0] // 16
    @pl.when(step == steps - 1)
    def _():
        eye = identity(length)
        for head in range(2):
            acc[head] = dot(eye, acc[head].astype(BF), NT)
        for g, (order, segments) in enumerate(groups):
            at = 16
            for out in outs[4 * g:4 * g + 4]:
                at -= out.shape[0]
                for j in range(out.shape[0]):
                    place = info_ref[order + at + j]
                    row = 0
                    for kind, k in segments:
                        if kind == "mask":
                            value = acc[k, pl.ds(pl.multiple_of(place * rows, rows), rows), :].astype(BF)
                            for t in range(length // 128):
                                out[j, row:row + rows, :] = value[:, t * 128:(t + 1) * 128]
                                row += rows
                        elif kind == "extra":
                            out[j, row:row + 16, :] = extra[pl.ds(pl.multiple_of(place * 16, 16), 16), :].astype(BF)
                            row += 16
                        else:
                            source = weight if kind == "weight" else weight_out
                            value = source[pl.ds(pl.multiple_of(place * wrows, wrows), wrows), k * 128:(k + 1) * 128]
                            out[j, row:row + wrows, :] = value.astype(BF)
                            row += wrows

def segment_rows(kind, length, width):
    return {"mask": length // 4, "extra": 16}.get(kind, width // 16)

def attend_back(pair, local, groups, info, qkv, mixed, grad_attn, w_out, total, tokens, pieces, all_mixed=(), small=None):
    _, seqs, _, length = total.shape
    rows_all, width = 2 * tokens[0].shape[0], tokens[0].shape[1]
    half = seqs // 2
    def split(wide, at=0):
        return [pl.BlockSpec((length, wide), lambda s, *_: (jnp.minimum(s, half - 1), at)),
                pl.BlockSpec((length, wide), lambda s, *_: (jnp.maximum(s - half, 0), at))]
    def part(which):
        return pl.BlockSpec((1, length, 128), lambda s, *_: (which, s, pair))
    masks = [pl.BlockSpec((p.shape[0], 1, *p.shape[2:]), lambda s, *_: (0, local, 0, 0)) for p in pieces]
    extras, extra_specs = [], []
    scratch = [pltpu.VMEM((length, length), BF), pltpu.VMEM((2, length, length), F32), pltpu.VMEM((2, length, length), F32),
               pltpu.VMEM((width, 384), F32), pltpu.VMEM((256, 128), F32)]
    if all_mixed:
        extras = [m[0] for m in all_mixed] + [m[1] for m in all_mixed] + [small]
        extra_specs = [split(m.shape[1])[k // len(all_mixed)] for k, m in enumerate(extras[:-1])] + [full(small.shape)]
        scratch.append(pltpu.VMEM((width, width // 2), F32))
    sds = jax.ShapeDtypeStruct
    shapes = [(n, sum(segment_rows(kind, length, width) for kind, _ in segments), 128) for _, segments in groups for n in SIZES]
    return pl.pallas_call(
        functools.partial(attend_back_body, groups, len(all_mixed)),
        grid_spec=pltpu.PrefetchScalarGridSpec(
            num_scalar_prefetch=1, grid=(seqs,),
            in_specs=[part(0), part(1), part(2), *split(128, local), *split(width),
                      pl.BlockSpec((128, width), lambda s, info: (info[OWN_CORE] * 3 + pair, 0)),
                      pl.BlockSpec((1, 1, 8, length), lambda s, *_: (local, s, 0, 0)), *split(width), *masks, *extra_specs],
            out_specs=split(384) + [full(x) for x in shapes],
            scratch_shapes=scratch,
        ),
        out_shape=[sds((rows_all // 2, 384), BF)] * 2 + [sds(x, BF) for x in shapes],
        compiler_params=params("arbitrary"),
        cost_estimate=cost(18 + 3 * bool(all_mixed)),
        name="attend_back",
    )(info, qkv, qkv, qkv, *mixed, *grad_attn, w_out, total, *tokens, *pieces, *extras)

def full(shape):
    return pl.BlockSpec(shape, lambda *_: (0,) * len(shape))

def project_body(info_ref, own_ref, other_ref, w_ref, shift_ref, out_ref):
    third = pl.program_id(0)
    scale = jnp.where(third == 0, 0.125, 1.0)
    rows = own_ref.shape[0]
    for i, ref in enumerate((own_ref, other_ref)):
        value = (dot(ref[...], w_ref[...]) + shift_ref[...]).astype(BF)
        out_ref[0, i * rows:(i + 1) * rows] = (value.astype(F32) * scale).astype(BF)

def project(info, own_tokens, other_tokens, w_qkv, shift):
    rows, width = own_tokens.shape
    own = width // 2
    return pl.pallas_call(
        project_body,
        grid_spec=pltpu.PrefetchScalarGridSpec(
            num_scalar_prefetch=1, grid=(3,),
            in_specs=[full((rows, width)), full((rows, width)),
                      pl.BlockSpec((width, own), lambda t, info: (0, 2 * t + info[OWN_CORE])),
                      pl.BlockSpec((1, own), lambda t, info: (0, 2 * t + info[OWN_CORE]))],
            out_specs=pl.BlockSpec((1, 2 * rows, own), lambda t, c: (t, 0, 0)),
        ),
        out_shape=jax.ShapeDtypeStruct((3, 2 * rows, own), BF),
        compiler_params=params("arbitrary"),
        cost_estimate=cost(8),
        name="project",
    )(info, own_tokens, other_tokens, w_qkv, shift)

def erf_parts(u):
    x = jnp.abs(u) * 0.7071067811865476
    t = 1.0 / (1.0 + 0.3275911 * x)
    e = jnp.exp(-0.5 * u * u)
    poly = t * (0.127414796 + t * (-0.142248368 + t * (0.7107068705 + t * (-0.7265760135 + t * 0.5307027145))))
    tail = poly * e
    return jnp.where(u < 0.0, tail, 1.0 - tail), e * 0.3989422804014327

def row_mean(v):
    return jnp.mean(v, axis=-1, keepdims=True)

def ffn_body(info_ref, *refs):
    tok_ref, gout_ref = refs[:2]
    count = len(refs) - 22
    mixed, (wout_ref, vec_ref, bin_ref), refs = refs[2:2 + count], refs[2 + count:5 + count], refs[5 + count:]
    w_in, w_down = refs[:4], refs[4:8]
    out_ref, low_ref, active_ref, slope_ref, gsec_ref, gbr_ref, norm_ref, inv_ref, sums_ref = refs[8:]
    bias_out, gain1, shift1, bias_down, gain2, shift2 = (vec_ref[i:i + 1] for i in range(6))
    value = tok_ref[...].astype(F32) + bias_out
    half = wout_ref.shape[0] // 2
    for side in range(2):
        part = jnp.concatenate([m[...] for m in mixed[side * count // 2:(side + 1) * count // 2]], axis=1)
        start = pl.multiple_of(info_ref[OWN_CORE + side] * half, half)
        value += dot(part, wout_ref[pl.ds(start, half), :])
    centered = value - row_mean(value)
    inverse = lax.rsqrt(row_mean(centered * centered) + 1e-12)
    normal = centered * inverse
    norm_ref[...] = normal
    inv_ref[...] = jnp.broadcast_to(inverse, inv_ref.shape)
    first = normal * gain1 + shift1
    low = first.astype(BF)
    low_ref[...] = low
    width = low.shape[1]
    branch = first + bias_down
    for b in range(4):
        pre = dot(low, w_in[b][...], NT) + bin_ref[b:b + 1]
        cum, dens = erf_parts(pre)
        act = (pre * cum).astype(BF)
        active_ref[b * width:(b + 1) * width, :] = act.T
        slope_ref[:, b * width:(b + 1) * width] = (cum + pre * dens).astype(slope_ref.dtype)
        branch += dot(act, w_down[b][...])
    centered = branch - row_mean(branch)
    inverse = lax.rsqrt(row_mean(centered * centered) + 1e-12)
    normal = centered * inverse
    out_ref[...] = (normal * gain2 + shift2).astype(BF)
    grad = gout_ref[...].astype(F32)
    inner = grad * gain2
    back = inverse * (inner - row_mean(inner) - normal * row_mean(inner * normal))
    gsec_ref[...] = back
    gbr_ref[...] = back.astype(BF)
    @pl.when(pl.program_id(0) == 0)
    def _():
        sums_ref[...] = jnp.zeros_like(sums_ref)
    total = lambda v: jnp.sum(v, axis=0, keepdims=True)
    sums_ref[0:1] += total(grad * normal)
    sums_ref[1:2] += total(grad)
    sums_ref[2:3] += total(back)

def ffn(info, tokens, grad_out, mixed, w_out, vecs, b_in, w_in, w_down, tile=256):
    rows, width = tokens.shape
    hidden = 4 * width
    row = lambda n: pl.BlockSpec((tile, n), lambda i, *_: (i, 0))
    sds = jax.ShapeDtypeStruct
    return pl.pallas_call(
        ffn_body,
        grid_spec=pltpu.PrefetchScalarGridSpec(num_scalar_prefetch=1, grid=(rows // tile,), in_specs=[row(width), row(width)] + [row(m.shape[1]) for m in mixed]
        + [full(a.shape) for a in (w_out, vecs, b_in, *w_in, *w_down)],
        out_specs=[row(width), row(width), pl.BlockSpec((hidden, tile), lambda i, *_: (0, i)), row(hidden), row(width), row(width), row(width), row(128),
                   full((8, width))]),
        out_shape=[sds((rows, width), BF), sds((rows, width), BF), sds((hidden, rows), BF), sds((rows, hidden), BF),
                   sds((rows, width), F32), sds((rows, width), BF), sds((rows, width), F32), sds((rows, 128), F32), sds((8, width), F32)],
        compiler_params=params("arbitrary"),
        cost_estimate=cost(30),
        name="ffn",
    )(info, tokens, grad_out, *mixed, w_out, vecs, b_in, *w_in, *w_down)

def ffn_back_body(info_ref, *refs):
    gbr_ref, slope_ref, gsec_ref, norm_ref, inv_ref, vec_ref, before_ref = refs[:7]
    w_in, w_down = refs[7:11], refs[11:15]
    gpre_ref, gone_ref, gattn_ref, small_ref, sums_ref = refs[15:]
    gain1 = vec_ref[1:2]
    @pl.when(pl.program_id(0) == 0)
    def _():
        sums_ref[...] = jnp.zeros_like(sums_ref)
    total = lambda v: jnp.sum(v, axis=0, keepdims=True)
    width = gbr_ref.shape[1]
    grad = gsec_ref[...]
    low = gbr_ref[...]
    for b in range(4):
        at = slice(b * width, (b + 1) * width)
        gpre = (dot(low, w_down[b][...], NT) * slope_ref[:, at].astype(F32)).astype(BF)
        gpre_ref[at, :] = gpre.T
        sums_ref[4 + b:5 + b] += total(gpre.astype(F32))
        grad += dot(gpre, w_in[b][...])
    normal, inverse = norm_ref[...], inv_ref[:, 0:1]
    inner = grad * gain1
    back = inverse * (inner - row_mean(inner) - normal * row_mean(inner * normal))
    gone_ref[...] = back
    gattn_ref[...] = back.astype(BF)
    sums_ref[0:1] += total(grad * normal)
    sums_ref[1:2] += total(grad)
    sums_ref[2:3] += total(back)
    @pl.when(pl.program_id(0) == pl.num_programs(0) - 1)
    def _():
        small_ref[...] = jnp.zeros_like(small_ref)
        tiles = width // 128
        for t in range(tiles):
            at = slice(t * 128, (t + 1) * 128)
            for k in range(3):
                small_ref[k * tiles + t:k * tiles + t + 1] = before_ref[k:k + 1, at]
                small_ref[(3 + k) * tiles + t:(3 + k) * tiles + t + 1] = sums_ref[k:k + 1, at]
            for k in range(4):
                small_ref[pl.ds((6 + info_ref[PLACE + k]) * tiles + t, 1), :] = sums_ref[4 + k:5 + k, at]

def ffn_back(info, grad_branch, slope, grad_second, normal, inverse, vecs, before, w_in, w_down, tile=256):
    rows, width = grad_branch.shape
    hidden = 4 * width
    row = lambda n: pl.BlockSpec((tile, n), lambda i, *_: (i, 0))
    sds = jax.ShapeDtypeStruct
    return pl.pallas_call(
        ffn_back_body,
        grid_spec=pltpu.PrefetchScalarGridSpec(num_scalar_prefetch=1, grid=(rows // tile,), in_specs=[row(width), row(hidden), row(width), row(width), row(128)] + [full(a.shape) for a in (vecs, before, *w_in, *w_down)],
        out_specs=[pl.BlockSpec((hidden, tile), lambda i, *_: (0, i)), row(width), row(width), full((64, 128))],
            scratch_shapes=[pltpu.VMEM((8, width), F32)]),
        out_shape=[sds((hidden, rows), BF), sds((rows, width), F32), sds((rows, width), BF), sds((64, 128), F32)],
        compiler_params=params("arbitrary"),
        cost_estimate=cost(18),
        name="ffn_back",
    )(info, grad_branch, slope, grad_second, normal, inverse, vecs, before, *w_in, *w_down)

def outer_send_body(a_ref, b_ref, out_ref):
    out_ref[0] = dot(a_ref[...], b_ref[...]).astype(BF)

def outer_send(a, b):
    rows, width = b.shape
    return pl.pallas_call(
        outer_send_body,
        grid=(2,),
        in_specs=[pl.BlockSpec((width, rows), lambda i: (2 * i + 1, 0)), full((rows, width))],
        out_specs=pl.BlockSpec((1, width, width), lambda i: (i, 0, 0)),
        out_shape=jax.ShapeDtypeStruct((2, width, width), BF),
        compiler_params=params("arbitrary"),
        cost_estimate=cost(6),
        name="outer_send",
    )(a, b)

def outer_keep_body(a_ref, b_ref, add_ref, keep_ref, send_ref):
    value = dot(a_ref[...], b_ref[...]) + add_ref[0].astype(F32)
    @pl.when(pl.program_id(0) == 0)
    def _():
        send_ref[...] = value.astype(BF)
    @pl.when(pl.program_id(0) == 1)
    def _():
        keep_ref[...] = value

def outer_keep(a, b, add):
    rows, width = b.shape
    return pl.pallas_call(
        outer_keep_body,
        grid=(2,),
        in_specs=[pl.BlockSpec((width, rows), lambda i: (2 - 2 * i, 0)), full((rows, width)),
                  pl.BlockSpec((1, width, width), lambda i: (1 - i, 0, 0))],
        out_specs=[full((width, width)), full((width, width))],
        out_shape=[jax.ShapeDtypeStruct((width, width), F32), jax.ShapeDtypeStruct((width, width), BF)],
        compiler_params=params("arbitrary"),
        cost_estimate=cost(7),
        name="outer_keep",
    )(a, b, add)

def grad_tokens_body(info_ref, *refs):
    pieces, (one_ref, w_ref, out_ref, sides) = refs[:-4], refs[-4:]
    width = one_ref.shape[1]
    @pl.when(pl.program_id(0) == 0)
    def _():
        for side in range(2):
            for pair in range(3):
                for third in range(3):
                    start = pl.multiple_of(third * width + (info_ref[OWN_CORE + side] * 3 + pair) * 128, 128)
                    at = ((side * 3 + pair) * 3 + third) * 128
                    sides[:, at:at + 128] = w_ref[:, pl.ds(start, 128)]
    wide = jnp.concatenate([r[...] for r in pieces], axis=1)
    out_ref[...] = (one_ref[...] + dot(wide, sides[...], NT)).astype(BF)

def grad_tokens(info, pieces, grad_one, w, tile=256):
    rows, width = grad_one.shape
    row = lambda n: pl.BlockSpec((tile, n), lambda i, *_: (i, 0))
    return pl.pallas_call(
        grad_tokens_body,
        grid_spec=pltpu.PrefetchScalarGridSpec(
            num_scalar_prefetch=1, grid=(rows // tile,),
            in_specs=[row(p.shape[1]) for p in pieces] + [row(width), full(w.shape)],
            out_specs=row(width),
            scratch_shapes=[pltpu.VMEM(w.shape, BF)]),
        out_shape=jax.ShapeDtypeStruct((rows, width), BF),
        compiler_params=params("arbitrary"),
        cost_estimate=cost(9),
        name="grad_tokens",
    )(info, *pieces, grad_one, w)

def place_pair_body(order_of, extra_at, aliased, info_ref, *refs):
    refs = refs[aliased:]
    count = 1 + max(piece for piece, _, _ in order_of)
    sides, out_ref, extras = (refs[:count], refs[count:2 * count]), refs[2 * count], refs[2 * count + 1:]
    rows = out_ref.shape[0] // 16
    for side in range(2):
        for third, (piece, order, first) in enumerate(order_of):
            @pl.when(pl.program_id(0) == side * 3 + third)
            def _(side=side, piece=piece, order=order, first=first):
                for slot in range(16):
                    start = pl.multiple_of(info_ref[order + slot] * rows, rows)
                    out_ref[pl.ds(start, rows), :] = sides[side][piece][slot, first:first + rows, :].astype(F32)
    @pl.when(pl.program_id(0) == 0)
    def _():
        piece, order, first = extra_at
        for side in range(2):
            for slot in range(16):
                start = pl.multiple_of(info_ref[order + slot] * 16, 16)
                extras[side][pl.ds(start, 16), :] = sides[side][piece][slot, first:first + 16, :].astype(F32)

def place_pair(pair, order_of, extra_at, info, width, own, other, whole=None):
    sds = jax.ShapeDtypeStruct
    aliased = int(whole is not None)
    return pl.pallas_call(
        functools.partial(place_pair_body, order_of, extra_at, aliased),
        grid_spec=pltpu.PrefetchScalarGridSpec(
            num_scalar_prefetch=1, grid=(6,),
            in_specs=[pl.BlockSpec(memory_space=pl.ANY)] * aliased + [full(p.shape) for p in (*own, *other)],
            out_specs=[pl.BlockSpec((width, 128), lambda i, info: (0, i % 3 * (width // 128) + info[OWN_CORE + i // 3] * 3 + pair)),
                       full((256, 128)), full((256, 128))]),
        out_shape=[sds((width, 3 * width), F32), sds((256, 128), F32), sds((256, 128), F32)],
        input_output_aliases={1: 0} if aliased else {},
        compiler_params=params("arbitrary"),
        cost_estimate=cost(3),
        name="place_pair",
    )(info, *([whole] if aliased else []), *own, *other)

def place_turned_body(order, first, info_ref, own_ref, other_ref, out_ref, acc):
    width, wide = acc.shape
    rows = width // 16
    for side, piece in enumerate((own_ref, other_ref)):
        for slot in range(16):
            start = pl.multiple_of(info_ref[order + slot] * rows, rows)
            for t in range(3):
                at = first + t * rows
                acc[pl.ds(start, rows), t * 128:(t + 1) * 128] = piece[slot, at:at + rows, :].astype(F32)
        start = pl.multiple_of(info_ref[OWN_CORE + side] * wide, wide)
        out_ref[pl.ds(start, wide), :] = acc[...].T

def place_turned(order, first, info, width, own, other):
    return pl.pallas_call(
        functools.partial(place_turned_body, order, first),
        grid_spec=pltpu.PrefetchScalarGridSpec(
            num_scalar_prefetch=1, grid=(1,), in_specs=[full(own.shape), full(other.shape)], out_specs=full((width, width)),
            scratch_shapes=[pltpu.VMEM((width, width // 2), F32)]),
        out_shape=jax.ShapeDtypeStruct((width, width), F32),
        compiler_params=params("arbitrary"),
        cost_estimate=cost(4),
        name="place_turned",
    )(info, own, other)


AXES = ("dp", "mp")
CORE, ROW, COLUMN, NEAR_DEPTH, FAR_DEPTH = 1, 2, 4, 8, 16
PARTS = ((0, 1), (1, 2))
WEIGHT = [("weight", k) for k in range(3)]
MASKS = [("mask", 0), ("mask", 1)]
OUT = [("out", k) for k in range(3)]
STEPS = ((1, ORDER_B, [*MASKS, *WEIGHT, *OUT, ("extra", 0)]), (2, ORDER_B, [*MASKS, *WEIGHT, ("extra", 0)]),
         (0, ORDER_A, [*MASKS, *WEIGHT, ("extra", 0)]))


class Order:
    def __init__(self):
        self.last = None

    def hold(self, value):
        return value if self.last is None else lax.optimization_barrier((value, self.last))[0]

    def do(self, step, *operands):
        result = step(*self.hold(operands))
        self.last = jax.tree.leaves(result)[0]
        return result


class Links:
    def __init__(self, dp, mp):
        self.dp, self.mp = dp, mp
        self.direct = dp == 8 and mp == 4
        self.at_dp, self.at_mp = lax.axis_index("dp"), lax.axis_index("mp")
        self.core, self.row, self.column = self.at_mp % 2, self.at_mp // 2, self.at_dp % 2
        self.near_deep, self.far_deep = self.at_dp // 2 % 2, self.at_dp // 4
        slot = jnp.arange(16)
        z, low, high = (((slot >> 1) & 1) << 1) | ((slot & 1) << 2), (slot >> 2) & 1, slot >> 3
        if self.direct:
            def chip(x, y):
                return (self.at_dp ^ (x | z)) * 2 + (self.row ^ y)
            orders = [chip(low, high), chip(high, low)]
        else:
            orders = [slot, slot]
        rest = jnp.stack([self.core, 1 - self.core, *(self.at_mp ^ k for k in range(4))])
        self.info = jnp.concatenate([*orders, rest]).astype(jnp.int32)

    def swap(self, value, bits):
        count = self.dp * self.mp
        return lax.ppermute(value, AXES, [(i, i ^ bits) for i in range(count)])

    def grow(self, value, *axes):
        for bits in axes:
            value = jnp.concatenate([value, self.swap(value, bits)])
        return value


def pick(index, first, second):
    return jnp.where(index == 0, first, second)


def in_order(index, own, other, axis=0):
    return pick(index, jnp.stack([own, other], axis), jnp.stack([other, own], axis))


def at(value, index, axis):
    return lax.dynamic_index_in_dim(value, index, axis, False)


def axes_of(order):
    return (ROW, COLUMN) if order == ORDER_A else (COLUMN, ROW)


def add(*values):
    return sum(v.astype(F32) for v in values)


def any_hidden(links, keep, near):
    zero = jnp.zeros_like(keep)
    blocks = jnp.stack([keep, zero, near.astype(F32), zero])
    blocks = jnp.stack([blocks[links.at_mp ^ k] for k in range(4)])
    return lax.psum(lax.psum_scatter(blocks, "mp", scatter_dimension=0, tiled=False), "dp")


class Hidden:
    def __init__(self, links, order, keep, near):
        self.links, self.order, self.shape = links, order, keep.shape
        self.parts = (2, 2, 2, keep.shape[0] // 8, keep.shape[1])
        self.total, self.came = keep, links.swap(near, ROW)

    def halve(self, index, axis, bits):
        def step(total, came):
            total = total.reshape(self.parts[-axis - 3:]) + came.reshape(self.parts[-axis - 3:]).astype(F32)
            return at(total, 1 - index, axis).astype(BF), at(total, index, axis)
        away, self.total = self.order.do(step, self.total, self.came)
        self.came = self.links.swap(away, bits)

    def column(self):
        self.halve(self.links.column, 2, COLUMN)

    def near_deep(self):
        self.halve(self.links.near_deep, 1, NEAR_DEPTH)

    def far_deep(self):
        self.halve(self.links.far_deep, 0, FAR_DEPTH)

    def spread_far(self):
        self.total = self.order.do(lambda a, b: add(a, b).astype(BF), self.total, self.came)
        self.came = self.links.swap(self.total, FAR_DEPTH)

    def spread(self, index, axis, bits):
        self.total = self.order.do(lambda a, b: in_order(index, a, b, axis), self.total, self.came)
        self.came = self.links.swap(self.total, bits)

    def spread_near(self):
        self.spread(self.links.far_deep, 0, NEAR_DEPTH)

    def spread_column(self):
        self.spread(self.links.near_deep, 1, COLUMN)

    def whole(self):
        self.result = self.order.do(lambda a, b: in_order(self.links.column, a, b, 2).astype(F32).reshape(self.shape), self.total, self.came)


class Slots:
    def __init__(self, links, order, axes, masks):
        self.links, self.order, self.axes, self.masks = links, order, axes, masks
        self.slots, self.came = [], []

    def far(self, slots):
        self.slots.append(slots)
        self.came.append(self.links.swap(slots[0], self.axes[0]))

    def near(self):
        def step(mids, came):
            return jnp.concatenate([add(m, c[4:]).astype(BF) for m, c in zip(mids, came)], axis=1)
        self.beside = self.links.swap(self.order.do(step, [s[1] for s in self.slots], self.came), self.axes[1])

    def deep(self, which, first, last):
        slots, came, beside = which
        return jnp.concatenate([add(s, c[first:last]) for s, c in zip(slots, came)], axis=1) + beside[first:last].astype(F32)

    def near_deep(self):
        step = lambda *which: self.deep(which, 2, 4).astype(BF)
        sent = self.order.do(step, [s[2] for s in self.slots], self.came, self.beside)
        self.behind = self.links.swap(sent, NEAR_DEPTH)

    def far_deep(self):
        def step(which, behind):
            total = self.deep(which, 0, 2) + behind.astype(F32)
            return total[1].astype(BF), total[0]
        sent, self.total = self.order.do(step, ([s[3] for s in self.slots], self.came, self.beside), self.behind)
        self.came = self.links.swap(sent, FAR_DEPTH)

    def spread_far(self):
        def step(total, came):
            total = total + came.astype(F32)
            row, masks, rest = 0, [], []
            for slots, count in zip(self.slots, self.masks):
                rows = slots[0].shape[1]
                masks.append(total[row:row + count])
                rest.append(total[row + count:row + rows])
                row += rows
            return jnp.concatenate(rest)[None].astype(BF), masks
        self.whole, self.mask_rows = self.order.do(step, self.total, self.came)
        self.came = self.links.swap(self.whole, FAR_DEPTH)

    def spread(self, bits):
        self.whole = self.order.do(lambda a, b: jnp.concatenate([a, b]), self.whole, self.came)
        self.came = self.links.swap(self.whole, bits)


def body(dp, mp, tokens, w_qkv, bias_q, bias_v, w_out, bias_out, norm1_gain, norm1_bias, w_in, bias_in, w_down, bias_down,
         norm2_gain, norm2_bias, mask_logits, mask_noise, grad_out):
    width = w_out.shape[0]
    heads, rows_own, length = mask_logits.shape
    half = heads // 2
    links, order = Links(dp, mp), Order()
    core, info, swap, do = links.core, links.info, links.swap, order.do
    wide = lambda v: v.astype(F32)

    def chances(logits, noise):
        fraction = noise.astype(F32) / 65536.0
        return logits + jnp.log(fraction) - jnp.log(1.0 - fraction)

    def codes(logits, noise):
        logit = chances(logits, noise)
        tail = jax.nn.sigmoid(-jnp.abs(logit)) * MASK_SCALE
        return jnp.where(logit < 0.0, tail, -tail).astype(BF)

    shift = jnp.concatenate([wide(bias_q), jnp.zeros((width,), F32), wide(bias_v)])[None]
    vecs = jnp.stack([wide(v) for v in (bias_out, norm1_gain, norm1_bias, bias_down, norm2_gain, norm2_bias)]
                     + [jnp.zeros((width,), F32)] * 2)
    mixed, totals, came = [], [], []

    def attention(part, pieces):
        own, other, total = do(lambda q, m: attend(*PARTS[part], info, q, m), qkv, pieces)
        mixed.append((own, other))
        came.append(swap(other, CORE))
        totals.append(total)

    if links.direct:
        plane = (1, rows_own, length)

        def two_sides(logits, noise, bias):
            code = codes(logits, noise)
            row = jnp.pad(bias, (0, rows_own * length - bias.shape[0])).reshape(plane)
            return jnp.concatenate([pick(core, code[half:], code[:half]), row]), pick(core, code[:half], code[half:])
        away, keep = do(two_sides, mask_logits, mask_noise, bias_in)
        beside = swap(away, CORE)
        other_tokens = swap(tokens, CORE)

        def chip_codes(keep, beside):
            chip = in_order(core, keep, beside[:half], 1).reshape(half // 2, 2, 2 * rows_own, length)
            return chip.transpose(1, 0, 2, 3)[None], beside[half].reshape(-1)[:bias_in.shape[0]]
        chip, near_bias = do(chip_codes, keep, beside)
        behind = swap(chip, FAR_DEPTH)
        eighth = w_in.shape[0] // 8
        split = lambda w: w.reshape(4, 2, eighth, width)

        def to_row(w_in, w_down, *biases):
            parts = [at(at(split(w), links.at_dp // 2, 0), links.column, 0) for w in (w_in, w_down)]
            return jnp.concatenate([*parts, jnp.pad(jnp.stack(biases), ((0, 14), (0, 0)))]), at(split(w_down), 1 - links.column, 1)
        piece, straight = do(to_row, w_in, w_down, bias_in, near_bias)
        piece, straight = swap(piece, ROW), swap(straight, ROW)
        qkv = do(lambda *v: project(info, *v), tokens, other_tokens, w_qkv, shift)
        axes = ((COLUMN, ROW), (ROW, COLUMN))
        groups, seconds, fars = [None] * 2, [None] * 2, [None] * 2

        def gather_near(part):
            groups[part] = do(lambda a, b: [jnp.concatenate([a[:, h], b[:, h]]) for h in range(2)], *deep[part])
            seconds[part] = [swap(groups[part][h], axes[h][0]) for h in range(2)]

        def gather_far(part):
            both = do(lambda g, s: [jnp.concatenate(v) for v in zip(g, s)], groups[part], seconds[part])
            fars[part] = [swap(both[h], axes[h][1]) for h in range(2)]

        pairs = do(lambda a, b: [jnp.concatenate([a[:, :, p:p + n], b[:, :, p:p + n]]) for p, n in PARTS], chip, behind)
        deep = [(v, swap(v, NEAR_DEPTH)) for v in pairs]
        gather_near(0)
        piece = order.hold(piece)
        across_bias = list(piece[2 * eighth:2 * eighth + 2])
        piece = piece[:2 * eighth]
        behind = swap(piece, FAR_DEPTH)
        gather_far(0)
        gather_near(1)
        pieces = [None] * 2
        pieces[0] = [v for h in range(2) for v in (groups[0][h], seconds[0][h], fars[0][h])]
        attention(0, pieces[0])
        gather_far(1)
        pair = do(lambda a, b: in_order(links.far_deep, a, b), piece, behind)
        behind = swap(pair, NEAR_DEPTH)
        near_in, near_down = (swap(order.hold(w), CORE) for w in (w_in, w_down))
        group = do(lambda a, b: [v.reshape(4, eighth, width) for v in jnp.split(in_order(links.near_deep, a, b, 1), 2, axis=2)], pair, behind)
        around = swap(group[0], COLUMN)
        across_down = do(lambda a, b: in_order(links.column, a, b, 1).reshape(w_in.shape), group[1], straight)
        far_down = swap(across_down, CORE)
        pieces[1] = [v for h in range(2) for v in (groups[1][h], seconds[1][h], fars[1][h])]
        attention(1, pieces[1])
        across_in = do(lambda a, b: in_order(links.column, a, b, 1).reshape(w_in.shape), group[0], around)
        blocks_in = [w_in, near_in, across_in, swap(across_in, CORE)]
        blocks_down = [w_down, near_down, across_down, far_down]
        blocks_bias = [bias_in, near_bias, *across_bias]
    else:
        other_tokens = swap(tokens, CORE)
        qkv = project(info, tokens, other_tokens, w_qkv, shift)
        whole = lax.all_gather(codes(mask_logits, mask_noise), AXES, axis=1, tiled=True)
        own = lax.dynamic_slice_in_dim(whole, core * half, half, 0).reshape(half // 2, 2, 16, length // 16, length)
        own = own.transpose(1, 2, 0, 3, 4)
        pieces = [[own[h, a:b, p:p + n] for h in range(2) for a, b in ((0, 4), (4, 8), (8, 16))] for p, n in PARTS]
        attention(0, pieces[0])
        attention(1, pieces[1])
        blocks_in, blocks_down, blocks_bias = ([v[links.at_mp ^ k] for k in range(4)]
                                               for v in (lax.all_gather(w, "mp") for w in (w_in, w_down, bias_in)))
    biases = wide(jnp.stack(blocks_bias))
    out, first_low, active, slope, grad_second, grad_branch, normal, inverse, sums = do(
        lambda *v: ffn(info, *v), tokens, grad_out, [own for own, _ in mixed] + came, w_out, vecs, biases, blocks_in, blocks_down)
    sent_down = do(outer_send, active, grad_branch)
    grad_pre, grad_one, grad_attn, small = do(lambda *v: ffn_back(info, *v), grad_branch, slope, grad_second, normal, inverse, vecs,
                                              sums, blocks_in, blocks_down)
    other_attn = swap(grad_attn, CORE)
    keep_down = do(lambda *v: outer_keep(*v)[::-1], active, grad_branch, swap(sent_down, CORE))
    if links.direct:
        down = Hidden(links, order, keep_down[1], keep_down[0])
    sent_in = do(outer_send, grad_pre, first_low)
    d_own, d_other, slots = [None] * 3, [None] * 3, []

    def back(step):
        pair, place, segments = STEPS[step]
        part = min(pair, 1)
        local = pair - PARTS[part][0]
        own, other, *outs = do(
            lambda *v: attend_back(pair, local, [(place, segments)], info, *v), qkv, mixed[part], (grad_attn, other_attn), w_out,
            totals[part], (tokens, other_tokens), pieces[part], () if step else mixed, small)
        slots.append(outs)
        if links.direct:
            chains[step].far(outs)
        d_own[pair] = own
        d_other[pair] = swap(other, CORE)

    masks = [sum(kind == "mask" for kind, _ in segments) * length // 4 for _, _, segments in STEPS]
    chains = [Slots(links, order, axes_of(place), [count]) for (_, place, _), count in zip(STEPS, masks)]
    back(0)
    if links.direct:
        down.column()
    keep_in = do(lambda *v: outer_keep(*v)[::-1], grad_pre, first_low, swap(sent_in, CORE))
    if links.direct:
        inside = Hidden(links, order, keep_in[1], keep_in[0])
    back(1)
    if links.direct:
        zero, one, two = chains
        down.near_deep()
        zero.near()
    back(2)
    if links.direct:
        near, far = COLUMN, ROW
        for chain, step in (
            (inside, "column"), (down, "far_deep"), (zero, "near_deep"), (one, "near"), (None, "tokens"),
            (inside, "near_deep"), (two, "near"), (zero, "far_deep"), (down, "spread_far"), (one, "near_deep"),
            (inside, "far_deep"), (two, "near_deep"), (zero, "spread_far"), (down, "spread_near"), (one, "far_deep"),
            (inside, "spread_far"), (two, "far_deep"), (zero, NEAR_DEPTH), (down, "spread_column"), (one, "spread_far"),
            (inside, "spread_near"), (two, "spread_far"), (zero, near), (one, NEAR_DEPTH),
            (inside, "spread_column"), (two, NEAR_DEPTH), (down, "whole"), (zero, far), (one, near),
            (two, near), (inside, "whole"), (zero, CORE), (one, far), (two, far), (one, CORE), (two, CORE),
        ):
            if step == "tokens":
                grad_in = do(lambda *v: grad_tokens(info, *v), [*d_own, *d_other], grad_one, w_qkv)
            elif isinstance(step, int):
                chain.spread(step)
            else:
                getattr(chain, step)()
        grad_w_down, grad_w_in = down.result, inside.result
        placed = [(chain.whole, chain.came) for chain in chains]
        mask_rows = [chain.mask_rows[0].reshape(2, 4, length // 16, 128) for chain in chains]
    else:
        grad_w_down, grad_w_in = any_hidden(links, *keep_down[::-1]), any_hidden(links, *keep_in[::-1])
        grad_in = grad_tokens(info, [*d_own, *d_other], grad_one, w_qkv)
        placed, mask_rows = [], []
        for s, count in zip(slots, masks):
            own = wide(jnp.concatenate(s[::-1]))
            both = lax.psum(in_order(core, own, jnp.zeros_like(own)), AXES)
            sides = [both[core], both[1 - core]]
            placed.append([v[:, count:] for v in sides])
            mask_rows.append(jnp.stack([v[:, :count].reshape(16, 2, 4, length // 16, 128).transpose(1, 2, 0, 3, 4) for v in sides]))
    grad_w_qkv = grad_w_out = small = None
    bias, by_pair = [None] * 3, [None] * 3
    for step, (pair, _, segments) in enumerate(STEPS):
        found, row = {}, 0
        for kind, k in segments:
            if kind != "mask":
                found[kind, k] = (0, ORDER_A, row)
                row += segment_rows(kind, length, width)
        own, other = placed[step]
        if step == 0:
            grad_w_out = do(lambda *v: place_turned(ORDER_A, found["out", 0][2], info, width, *v), own, other)
        grad_w_qkv, *extras = do(
            lambda a, b, *w: place_pair(pair, [found["weight", k] for k in range(3)], found["extra", 0], info, width, [a], [b], *w),
            own, other, *([grad_w_qkv] if step else []))
        if step == 0:
            small = (extras[0][:60] + extras[1][:60]).reshape(10, width)
        bias[pair] = jnp.stack([e[64:67] for e in extras])
        by_pair[pair] = mask_rows[step]
    bias = jnp.stack(bias, axis=2)
    bias = pick(core, bias, bias[::-1]).transpose(1, 0, 2, 3).reshape(3, width)
    if links.direct:
        mask_sum = jnp.stack(by_pair).transpose(0, 1, 3, 2, 4).reshape(half, 2 * rows_own, length)
        mine = pick(core, mask_sum[:, :rows_own], mask_sum[:, rows_own:])
        theirs = swap(pick(core, mask_sum[:, rows_own:], mask_sum[:, :rows_own]), CORE)
    else:
        mine, theirs = jnp.stack(by_pair, axis=1).transpose(0, 1, 2, 4, 5, 3, 6).reshape(2, half, length, length)
        place = (links.at_dp * mp + links.at_mp) * rows_own
        mine, theirs = (lax.dynamic_slice_in_dim(m, place, rows_own, 1) for m in (mine, theirs))
    mask_sum = pick(core, jnp.concatenate([mine, theirs]), jnp.concatenate([theirs, mine]))
    mask_own = jax.nn.sigmoid(chances(mask_logits, mask_noise))
    grad_mask_logits = mask_sum * (MASK_SCALE * mask_own * (1.0 - mask_own))
    return (out, grad_in, grad_w_qkv, bias[0], bias[2], grad_w_out, small[5], small[3], small[4], grad_w_in, small[6 + links.at_mp],
            grad_w_down, small[2], small[0], small[1], grad_mask_logits)


def solution(mesh):
    both, none = ("dp", "mp"), P()
    rows, mask, split = P(both, None), P(None, both, None), P("mp", None)
    ins = (rows, none, none, none, none, none, none, none, split, P("mp"), split, none, none, none, mask, mask, rows)
    outs = (rows, rows, none, none, none, none, none, none, none, split, P("mp"), split, none, none, none, mask)
    step = functools.partial(body, mesh.shape["dp"], mesh.shape["mp"])
    return jax.shard_map(step, mesh=mesh, in_specs=ins, out_specs=outs, check_vma=False)
```

```python
import functools

import jax
import jax.numpy as jnp
from jax import lax
from jax.experimental import pallas as pl
from jax.experimental.pallas import tpu as pltpu
from jax.sharding import PartitionSpec as P

MASK_SCALE = 4.0

BF = jnp.bfloat16
F32 = jnp.float32
NT = (((1,), (1,)), ((), ()))
NN = (((1,), (0,)), ((), ()))
TN = (((0,), (0,)), ((), ()))
VMEM_LIMIT = 56 * 1024 * 1024
SIZES = (8, 4, 2, 2)

ORDER_A, ORDER_B, OWN_CORE, OTHER_CORE, PLACE, COLUMN_AT, NEAR_AT, FAR_AT = 0, 16, 32, 33, 34, 38, 39, 40

COST = 0.001

def cost(us):
    return pl.CostEstimate(flops=int(us * 1.0e9 * COST), transcendentals=0, bytes_accessed=int(us * 2.0e6 * COST))

def dot(a, b, dims=NN):
    return lax.dot_general(a, b, dims, preferred_element_type=F32)

def bf(*shape):
    return jax.ShapeDtypeStruct(shape, BF)

def f32(*shape):
    return jax.ShapeDtypeStruct(shape, F32)

def identity(n):
    return (lax.broadcasted_iota(jnp.int32, (n, n), 0) == lax.broadcasted_iota(jnp.int32, (n, n), 1)).astype(F32).astype(BF)

def params(*sem):
    return pltpu.CompilerParams(dimension_semantics=sem or None, vmem_limit_bytes=VMEM_LIMIT)

def place_mask(order_ref, pieces, codes, bias, eye):
    rows = codes.shape[0] // 16
    for head in range(2):
        slot = 0
        for group in pieces[head * 3:head * 3 + 3]:
            for j in range(group.shape[1]):
                start = pl.multiple_of(order_ref[head * 16 + slot] * rows, rows)
                codes[pl.ds(start, rows), :] = group[0, j]
                slot += 1
        turned = dot(eye, codes[...], NT)
        bias[head] = jnp.where(turned > 0.0, turned - 4.0, turned)

def halves(seqs, length, lane):
    half = seqs // 2
    return [pl.BlockSpec((length, lane), lambda i, s, *_: (jnp.minimum(s, half - 1), i)),
            pl.BlockSpec((length, lane), lambda i, s, *_: (jnp.maximum(s - half, 0), i))]

def mask_specs(pieces):
    return [pl.BlockSpec((1, *p.shape[1:]), lambda i, s, *_: (i, 0, 0, 0)) for p in pieces]

def qkv_specs(first, length):
    def part(which):
        return pl.BlockSpec((1, length, 128), lambda i, s, *_: (which, s, first + i))
    return [part(0), part(1), part(2)]

def attend_body(order_ref, q_ref, k_ref, v_ref, *refs):
    pieces, (own_ref, other_ref, total_ref), (codes, bias) = refs[:6], refs[6:9], refs[9:]
    length = codes.shape[0]
    step, count = pl.program_id(1), pl.num_programs(1)
    @pl.when(step == 0)
    def _():
        place_mask(order_ref, pieces, codes, bias, identity(length))
    half = q_ref.shape[2] // 2
    lanes = lax.broadcasted_iota(jnp.int32, (1, 2 * half), 1)
    query, keys = q_ref[0], k_ref[0]
    values_t = v_ref[0].T
    outs = []
    for head in range(2):
        own = (lanes >= half) if head else (lanes < half)
        scores = dot(keys, jnp.where(own, query, jnp.zeros_like(query)), NT) + bias[head]
        highest = jnp.max(scores, axis=0, keepdims=True)
        powers = jnp.exp(scores - highest)
        summed = jnp.sum(powers, axis=0, keepdims=True)
        probs = (powers * (1.0 / summed)).astype(BF)
        outs.append(dot(values_t[head * half:(head + 1) * half], probs))
        total_ref[0, 0, head:head + 1, :] = highest + jnp.log(summed)
    mixed = jnp.concatenate(outs, axis=0).T.astype(BF)
    @pl.when(step < count // 2)
    def _():
        own_ref[...] = mixed
    @pl.when(step >= count // 2)
    def _():
        other_ref[...] = mixed

def attend(first, count, order, qkv, pieces):
    _, tokens, width = qkv.shape
    length = pieces[0].shape[3]
    seqs = tokens // length
    sds = jax.ShapeDtypeStruct
    return pl.pallas_call(
        attend_body,
        grid_spec=pltpu.PrefetchScalarGridSpec(
            num_scalar_prefetch=1, grid=(count, seqs),
            in_specs=qkv_specs(first, length) + mask_specs(pieces),
            out_specs=[*halves(seqs, length, 128), pl.BlockSpec((1, 1, 8, length), lambda i, s, *_: (i, s, 0, 0))],
            scratch_shapes=[pltpu.VMEM((length, length), BF), pltpu.VMEM((2, length, length), F32)],
        ),
        out_shape=[sds((tokens // 2, count * 128), BF)] * 2 + [sds((count, seqs, 8, length), F32)],
        compiler_params=params("arbitrary", "arbitrary"),
        cost_estimate=cost(9 * count),
        name="attend",
    )(order, qkv, qkv, qkv, *pieces)

def attend_back_body(groups, has_out, info_ref, *refs):
    (q_ref, k_ref, v_ref, mixed_own, mixed_other, ga_own, ga_other, wout_ref, total_ref, tok_own, tok_other), refs = refs[:11], refs[11:]
    pieces, refs = refs[:6], refs[6:]
    all_own, all_other, small_ref = (), (), None
    if has_out:
        all_own, all_other, small_ref, refs = refs[:has_out], refs[has_out:2 * has_out], refs[2 * has_out], refs[2 * has_out + 1:]
    own_ref, other_ref, refs = refs[0], refs[1], refs[2:]
    outs, refs = refs[:4 * len(groups)], refs[4 * len(groups):]
    codes, bias, acc, weight, extra = refs[:5]
    weight_out = refs[5] if has_out else None
    length = codes.shape[0]
    step, steps = pl.program_id(0), pl.num_programs(0)
    @pl.when(step == 0)
    def _():
        place_mask(info_ref, pieces, codes, bias, identity(length))
        acc[...] = jnp.zeros_like(acc)
        weight[...] = jnp.zeros_like(weight)
        extra[...] = jnp.zeros_like(extra)
        if has_out:
            extra[0:small_ref.shape[0], :] = small_ref[...]
            weight_out[...] = jnp.zeros_like(weight_out)
    half = q_ref.shape[2] // 2
    lanes = lax.broadcasted_iota(jnp.int32, (1, 2 * half), 1)
    query, keys, values = q_ref[0], k_ref[0], v_ref[0]
    keys_t = keys.T
    is_own = step < steps // 2
    grad_attn = jnp.where(is_own, ga_own[...], ga_other[...])
    grad = dot(grad_attn, wout_ref[...], NT).astype(BF)
    mixed = jnp.where(is_own, mixed_own[...], mixed_other[...])
    inner = (grad.astype(F32) * mixed.astype(F32)).T
    dq, dk, dv = [], [], []
    for head in range(2):
        own = (lanes >= half) if head else (lanes < half)
        scores = dot(keys, jnp.where(own, query, jnp.zeros_like(query)), NT) + bias[head]
        probs = jnp.exp(scores - total_ref[0, 0, head:head + 1, :])
        delta = jnp.sum(inner[head * half:(head + 1) * half], axis=0, keepdims=True)
        grad_probs = dot(values, jnp.where(own, grad, jnp.zeros_like(grad)), NT)
        grad_scores = probs * (grad_probs - delta)
        acc[head] += grad_scores
        low = grad_scores.astype(BF)
        dv.append(dot(probs.astype(BF), grad))
        dk.append(dot(low, query))
        dq.append(dot(keys_t[head * half:(head + 1) * half], low))
    first = lanes < half
    result = jnp.concatenate([(jnp.concatenate(dq, axis=0).T * 0.125).astype(BF),
                              jnp.where(first, dk[0], dk[1]).astype(BF),
                              jnp.where(first, dv[0], dv[1]).astype(BF)], axis=1)
    @pl.when(is_own)
    def _():
        own_ref[...] = result
    @pl.when(jnp.logical_not(is_own))
    def _():
        other_ref[...] = result
    weight[...] += dot(jnp.where(is_own, tok_own[...], tok_other[...]), result, TN)
    sums = jnp.sum(result.astype(F32), axis=0, keepdims=True)
    for third in range(3):
        extra[64 + third:65 + third, :] += sums[:, third * 128:(third + 1) * 128]
    if has_out:
        whole = jnp.where(is_own, jnp.concatenate([m[...] for m in all_own], axis=1),
                          jnp.concatenate([m[...] for m in all_other], axis=1))
        weight_out[...] += dot(grad_attn, whole, TN)
    rows, wrows = length // 16, weight.shape[0] // 16
    @pl.when(step == steps - 1)
    def _():
        eye = identity(length)
        for head in range(2):
            acc[head] = dot(eye, acc[head].astype(BF), NT)
        for g, (order, segments) in enumerate(groups):
            at = 16
            for out in outs[4 * g:4 * g + 4]:
                at -= out.shape[0]
                for j in range(out.shape[0]):
                    place = info_ref[order + at + j]
                    row = 0
                    for kind, k in segments:
                        if kind == "mask":
                            value = acc[k, pl.ds(pl.multiple_of(place * rows, rows), rows), :].astype(BF)
                            for t in range(length // 128):
                                out[j, row:row + rows, :] = value[:, t * 128:(t + 1) * 128]
                                row += rows
                        elif kind == "extra":
                            out[j, row:row + 16, :] = extra[pl.ds(pl.multiple_of(place * 16, 16), 16), :].astype(BF)
                            row += 16
                        else:
                            source = weight if kind == "weight" else weight_out
                            value = source[pl.ds(pl.multiple_of(place * wrows, wrows), wrows), k * 128:(k + 1) * 128]
                            out[j, row:row + wrows, :] = value.astype(BF)
                            row += wrows

def segment_rows(kind, length, width):
    return {"mask": length // 4, "extra": 16}.get(kind, width // 16)

def attend_back(pair, local, groups, info, qkv, mixed, grad_attn, w_out, total, tokens, pieces, all_mixed=(), small=None):
    _, seqs, _, length = total.shape
    rows_all, width = 2 * tokens[0].shape[0], tokens[0].shape[1]
    half = seqs // 2
    def split(wide, at=0):
        return [pl.BlockSpec((length, wide), lambda s, *_: (jnp.minimum(s, half - 1), at)),
                pl.BlockSpec((length, wide), lambda s, *_: (jnp.maximum(s - half, 0), at))]
    def part(which):
        return pl.BlockSpec((1, length, 128), lambda s, *_: (which, s, pair))
    masks = [pl.BlockSpec((1, *p.shape[1:]), lambda s, *_: (local, 0, 0, 0)) for p in pieces]
    extras, extra_specs = [], []
    scratch = [pltpu.VMEM((length, length), BF), pltpu.VMEM((2, length, length), F32), pltpu.VMEM((2, length, length), F32),
               pltpu.VMEM((width, 384), F32), pltpu.VMEM((256, 128), F32)]
    if all_mixed:
        extras = [m[0] for m in all_mixed] + [m[1] for m in all_mixed] + [small]
        extra_specs = [split(m.shape[1])[k // len(all_mixed)] for k, m in enumerate(extras[:-1])] + [full(small.shape)]
        scratch.append(pltpu.VMEM((width, width // 2), F32))
    sds = jax.ShapeDtypeStruct
    shapes = [(n, sum(segment_rows(kind, length, width) for kind, _ in segments), 128) for _, segments in groups for n in SIZES]
    return pl.pallas_call(
        functools.partial(attend_back_body, groups, len(all_mixed)),
        grid_spec=pltpu.PrefetchScalarGridSpec(
            num_scalar_prefetch=1, grid=(seqs,),
            in_specs=[part(0), part(1), part(2), *split(128, local), *split(width),
                      pl.BlockSpec((128, width), lambda s, info: (info[OWN_CORE] * 3 + pair, 0)),
                      pl.BlockSpec((1, 1, 8, length), lambda s, *_: (local, s, 0, 0)), *split(width), *masks, *extra_specs],
            out_specs=split(384) + [full(x) for x in shapes],
            scratch_shapes=scratch,
        ),
        out_shape=[sds((rows_all // 2, 384), BF)] * 2 + [sds(x, BF) for x in shapes],
        compiler_params=params("arbitrary"),
        cost_estimate=cost(18 + 3 * bool(all_mixed)),
        name="attend_back",
    )(info, qkv, qkv, qkv, *mixed, *grad_attn, w_out, total, *tokens, *pieces, *extras)

def full(shape):
    return pl.BlockSpec(shape, lambda *_: (0,) * len(shape))

def project_body(info_ref, own_ref, other_ref, w_ref, shift_ref, out_ref):
    third = pl.program_id(0)
    scale = jnp.where(third == 0, 0.125, 1.0)
    rows = own_ref.shape[0]
    for i, ref in enumerate((own_ref, other_ref)):
        value = (dot(ref[...], w_ref[...]) + shift_ref[...]).astype(BF)
        out_ref[0, i * rows:(i + 1) * rows] = (value.astype(F32) * scale).astype(BF)

def project(info, own_tokens, other_tokens, w_qkv, shift):
    rows, width = own_tokens.shape
    own = width // 2
    return pl.pallas_call(
        project_body,
        grid_spec=pltpu.PrefetchScalarGridSpec(
            num_scalar_prefetch=1, grid=(3,),
            in_specs=[full((rows, width)), full((rows, width)),
                      pl.BlockSpec((width, own), lambda t, info: (0, 2 * t + info[OWN_CORE])),
                      pl.BlockSpec((1, own), lambda t, info: (0, 2 * t + info[OWN_CORE]))],
            out_specs=pl.BlockSpec((1, 2 * rows, own), lambda t, c: (t, 0, 0)),
        ),
        out_shape=jax.ShapeDtypeStruct((3, 2 * rows, own), BF),
        compiler_params=params("arbitrary"),
        cost_estimate=cost(8),
        name="project",
    )(info, own_tokens, other_tokens, w_qkv, shift)

def erf_parts(u):
    d = 1.0 + 0.23164189 * jnp.abs(u)
    t = pl.reciprocal(d, approx=True)
    t = t * (2.0 - d * t)
    e = jnp.exp2((-0.7213475204444817 * u) * u)
    poly = t * (0.127414796 + t * (-0.142248368 + t * (0.7107068705 + t * (-0.7265760135 + t * 0.5307027145))))
    tail = poly * e
    return jnp.where(u < 0.0, tail, 1.0 - tail), e * 0.3989422804014327

def row_mean(v):
    return jnp.mean(v, axis=-1, keepdims=True)

def column_sum(v):
    return jnp.sum(v, axis=0, keepdims=True)

def norm_parts(value):
    centered = value - row_mean(value)
    inverse = lax.rsqrt(row_mean(centered * centered) + 1e-12)
    return centered * inverse, inverse

def norm_back(inner, normal, inverse):
    return inverse * (inner - row_mean(inner) - normal * row_mean(inner * normal))

ANYWHERE = pl.BlockSpec(memory_space=pl.ANY)

def hidden_blocks(first, low, branch, bin_ref, w_in, w_down, active_ref, slope_ref):
    width = low.shape[1]
    pre = dot(low, w_in[0][...], NT)
    for b in range(len(w_in)):
        ahead = dot(low, w_in[b + 1][...], NT) if b + 1 < len(w_in) else None
        strips = []
        for r in range(0, pre.shape[0], 64):
            parts = []
            for c in range(0, width, 256):
                u = pre[r:r + 64, c:c + 256] + bin_ref[first + b:first + b + 1, c:c + 256]
                cum, dens = erf_parts(u)
                parts.append((u * cum).astype(BF))
                slope_ref[r:r + 64, b * width + c:b * width + c + 256] = (cum + u * dens).astype(slope_ref.dtype)
            strips.append(jnp.concatenate(parts, axis=1))
        act = jnp.concatenate(strips, axis=0)
        active_ref[b * width:(b + 1) * width, :] = act.T
        branch += dot(act, w_down[b][...])
        pre = ahead
    return branch

def ffn_first_body(info_ref, tok_ref, *refs):
    count = len(refs) - 13
    mixed, (wout_ref, vec_ref, bin_ref), refs = refs[:count], refs[count:3 + count], refs[3 + count:]
    w_in, w_down, (low_ref, active_ref, slope_ref, norm_ref, inv_ref, branch_ref) = refs[:2], refs[2:4], refs[4:]
    bias_out, gain1, shift1, bias_down = (vec_ref[i:i + 1] for i in range(4))
    value = tok_ref[...].astype(F32) + bias_out
    half = wout_ref.shape[0] // 2
    for side in range(2):
        part = jnp.concatenate([m[...] for m in mixed[side * count // 2:(side + 1) * count // 2]], axis=1)
        start = pl.multiple_of(info_ref[OWN_CORE + side] * half, half)
        value += dot(part, wout_ref[pl.ds(start, half), :])
    normal, inverse = norm_parts(value)
    norm_ref[...] = normal
    inv_ref[...] = jnp.broadcast_to(inverse, inv_ref.shape)
    first = normal * gain1 + shift1
    low = first.astype(BF)
    low_ref[...] = low
    branch_ref[...] = hidden_blocks(0, low, first + bias_down, bin_ref, w_in, w_down, active_ref, slope_ref)

def ffn_second_body(low_ref, branch_ref, gout_ref, vec_ref, bin_ref, *refs):
    w_in, w_down, (out_ref, active_ref, slope_ref, gsec_ref, gbr_ref, sums_ref) = refs[:2], refs[2:4], refs[4:]
    gain2, shift2 = vec_ref[4:5], vec_ref[5:6]
    branch = hidden_blocks(2, low_ref[...], branch_ref[...], bin_ref, w_in, w_down, active_ref, slope_ref)
    normal, inverse = norm_parts(branch)
    out_ref[...] = (normal * gain2 + shift2).astype(BF)
    grad = gout_ref[...].astype(F32)
    back = norm_back(grad * gain2, normal, inverse)
    gsec_ref[...] = back
    gbr_ref[...] = back.astype(BF)
    @pl.when(pl.program_id(0) == 0)
    def _():
        sums_ref[...] = jnp.zeros_like(sums_ref)
    sums_ref[0:1] += column_sum(grad * normal)
    sums_ref[1:2] += column_sum(grad)
    sums_ref[2:3] += column_sum(back)

def ffn_first(info, tokens, mixed, w_out, vecs, b_in, w_in, w_down, tile=256):
    rows, width = tokens.shape
    hidden = 2 * width
    row = lambda n: pl.BlockSpec((tile, n), lambda i, *_: (i, 0))
    return pl.pallas_call(
        ffn_first_body,
        grid_spec=pltpu.PrefetchScalarGridSpec(
            num_scalar_prefetch=1, grid=(rows // tile,),
            in_specs=[row(width)] + [row(m.shape[1]) for m in mixed] + [full(a.shape) for a in (w_out, vecs, b_in, *w_in, *w_down)],
            out_specs=[row(width), pl.BlockSpec((hidden, tile), lambda i, *_: (0, i)), row(hidden), row(width), row(128), row(width)]),
        out_shape=[bf(rows, width), bf(hidden, rows), bf(rows, hidden), f32(rows, width), f32(rows, 128), f32(rows, width)],
        compiler_params=params("arbitrary"),
        cost_estimate=cost(17),
        name="ffn_first",
    )(info, tokens, *mixed, w_out, vecs, b_in, *w_in, *w_down)

def ffn_second(low, branch, grad_out, vecs, b_in, w_in, w_down, tile=256):
    rows, width = low.shape
    hidden = 2 * width
    row = lambda n: pl.BlockSpec((tile, n), lambda i: (i, 0))
    return pl.pallas_call(
        ffn_second_body,
        grid=(rows // tile,),
        in_specs=[row(width)] * 3 + [full(a.shape) for a in (vecs, b_in, *w_in, *w_down)],
        out_specs=[row(width), pl.BlockSpec((hidden, tile), lambda i: (0, i)), row(hidden), row(width), row(width), full((8, width))],
        out_shape=[bf(rows, width), bf(hidden, rows), bf(rows, hidden), f32(rows, width), bf(rows, width), f32(8, width)],
        compiler_params=params("arbitrary"),
        cost_estimate=cost(17),
        name="ffn_second",
    )(low, branch, grad_out, vecs, b_in, *w_in, *w_down)

def ffn_back_body(info_ref, *refs):
    gbr_ref, *slopes, gsec_ref, norm_ref, inv_ref, vec_ref, before_ref = refs[:8]
    w_in, w_down = refs[8:12], refs[12:16]
    gpre_ref, gone_ref, gattn_ref, small_ref, sums_ref = refs[16:]
    gain1 = vec_ref[1:2]
    @pl.when(pl.program_id(0) == 0)
    def _():
        sums_ref[...] = jnp.zeros_like(sums_ref)
    total = lambda v: jnp.sum(v, axis=0, keepdims=True)
    width = gbr_ref.shape[1]
    grad = gsec_ref[...]
    low = gbr_ref[...]
    for b in range(4):
        at = slice(b * width, (b + 1) * width)
        slope = slopes[b // 2][:, b % 2 * width:(b % 2 + 1) * width]
        gpre = (dot(low, w_down[b][...], NT) * slope.astype(F32)).astype(BF)
        gpre_ref[at, :] = gpre.T
        sums_ref[4 + b:5 + b] += total(gpre.astype(F32))
        grad += dot(gpre, w_in[b][...])
    normal, inverse = norm_ref[...], inv_ref[:, 0:1]
    inner = grad * gain1
    back = inverse * (inner - row_mean(inner) - normal * row_mean(inner * normal))
    gone_ref[...] = back
    gattn_ref[...] = back.astype(BF)
    sums_ref[0:1] += total(grad * normal)
    sums_ref[1:2] += total(grad)
    sums_ref[2:3] += total(back)
    @pl.when(pl.program_id(0) == pl.num_programs(0) - 1)
    def _():
        small_ref[...] = jnp.zeros_like(small_ref)
        tiles = width // 128
        for t in range(tiles):
            at = slice(t * 128, (t + 1) * 128)
            for k in range(3):
                small_ref[k * tiles + t:k * tiles + t + 1] = before_ref[k:k + 1, at]
                small_ref[(3 + k) * tiles + t:(3 + k) * tiles + t + 1] = sums_ref[k:k + 1, at]
            for k in range(4):
                small_ref[pl.ds((6 + info_ref[PLACE + k]) * tiles + t, 1), :] = sums_ref[4 + k:5 + k, at]

def ffn_back(info, grad_branch, slopes, grad_second, normal, inverse, vecs, before, w_in, w_down, tile=256):
    rows, width = grad_branch.shape
    hidden = 4 * width
    row = lambda n: pl.BlockSpec((tile, n), lambda i, *_: (i, 0))
    sds = jax.ShapeDtypeStruct
    return pl.pallas_call(
        ffn_back_body,
        grid_spec=pltpu.PrefetchScalarGridSpec(num_scalar_prefetch=1, grid=(rows // tile,), in_specs=[row(width), row(hidden // 2), row(hidden // 2), row(width), row(width), row(128)]
            + [full(a.shape) for a in (vecs, before, *w_in, *w_down)],
        out_specs=[pl.BlockSpec((hidden, tile), lambda i, *_: (0, i)), row(width), row(width), full((64, 128))],
            scratch_shapes=[pltpu.VMEM((8, width), F32)]),
        out_shape=[sds((hidden, rows), BF), sds((rows, width), F32), sds((rows, width), BF), sds((64, 128), F32)],
        compiler_params=params("arbitrary"),
        cost_estimate=cost(18),
        name="ffn_back",
    )(info, grad_branch, *slopes, grad_second, normal, inverse, vecs, before, *w_in, *w_down)

def outer_body(a_ref, other_ref, b_ref, out_ref):
    for k, ref in enumerate((a_ref, other_ref)):
        @pl.when(pl.program_id(0) == k)
        def _(ref=ref):
            out_ref[0] = dot(ref[...], b_ref[...]).astype(out_ref.dtype)

def outer(firsts, kind, a, other, b):
    rows, width = b.shape
    return pl.pallas_call(
        outer_body,
        grid=(2,),
        in_specs=[pl.BlockSpec((width, rows), lambda i: (firsts[0], 0)), pl.BlockSpec((width, rows), lambda i: (firsts[1], 0)), full((rows, width))],
        out_specs=pl.BlockSpec((1, width, width), lambda i: (i, 0, 0)),
        out_shape=kind(2, width, width),
        compiler_params=params("arbitrary"),
        cost_estimate=cost(6),
        name="outer",
    )(a, other, b)

def grad_tokens_body(info_ref, *refs):
    pieces, (one_ref, w_ref, out_ref, sides) = refs[:-4], refs[-4:]
    width = one_ref.shape[1]
    @pl.when(pl.program_id(0) == 0)
    def _():
        for side in range(2):
            for pair in range(3):
                for third in range(3):
                    start = pl.multiple_of(third * width + (info_ref[OWN_CORE + side] * 3 + pair) * 128, 128)
                    at = ((side * 3 + pair) * 3 + third) * 128
                    sides[:, at:at + 128] = w_ref[:, pl.ds(start, 128)]
    wide = jnp.concatenate([r[...] for r in pieces], axis=1)
    out_ref[...] = (one_ref[...] + dot(wide, sides[...], NT)).astype(BF)

def grad_tokens(info, pieces, grad_one, w, tile=256):
    rows, width = grad_one.shape
    row = lambda n: pl.BlockSpec((tile, n), lambda i, *_: (i, 0))
    return pl.pallas_call(
        grad_tokens_body,
        grid_spec=pltpu.PrefetchScalarGridSpec(
            num_scalar_prefetch=1, grid=(rows // tile,),
            in_specs=[row(p.shape[1]) for p in pieces] + [row(width), full(w.shape)],
            out_specs=row(width),
            scratch_shapes=[pltpu.VMEM(w.shape, BF)]),
        out_shape=jax.ShapeDtypeStruct((rows, width), BF),
        compiler_params=params("arbitrary"),
        cost_estimate=cost(9),
        name="grad_tokens",
    )(info, *pieces, grad_one, w)

def wide(ref_value):
    return ref_value.astype(F32)

def place_pair_body(pair, firsts, extra_at, out_at, aliased, info_ref, *refs):
    refs = refs[aliased:]
    sides, out_ref, extras, refs = refs[:2], refs[2], refs[3:5], refs[5:]
    turned_ref, refs = (refs[0], refs[1:]) if out_at is not None else (None, refs)
    columns, sems = refs[:2]
    width = columns.shape[1]
    rows = width // 16
    copies = []
    for side in range(2):
        for third, first in enumerate(firsts):
            which = side * 3 + third
            for slot in range(16):
                start = pl.multiple_of(info_ref[ORDER_A + slot] * rows, rows)
                columns[which, pl.ds(start, rows), :] = sides[side][slot, first:first + rows, :].astype(F32)
            at = pl.multiple_of(third * width + (info_ref[OWN_CORE + side] * 3 + pair) * 128, 128)
            copy = pltpu.make_async_copy(columns.at[which], out_ref.at[:, pl.ds(at, 128)], sems.at[which])
            copy.start()
            copies.append(copy)
    for side in range(2):
        for slot in range(16):
            start = pl.multiple_of(info_ref[ORDER_A + slot] * 16, 16)
            extras[side][pl.ds(start, 16), :] = sides[side][slot, extra_at:extra_at + 16, :].astype(F32)
    if out_at is not None:
        acc = refs[2]
        wide = acc.shape[1]
        for side in range(2):
            for slot in range(16):
                start = pl.multiple_of(info_ref[ORDER_A + slot] * rows, rows)
                for t in range(3):
                    at = out_at + t * rows
                    acc[pl.ds(start, rows), t * 128:(t + 1) * 128] = sides[side][slot, at:at + rows, :].astype(F32)
            start = pl.multiple_of(info_ref[OWN_CORE + side] * wide, wide)
            turned_ref[pl.ds(start, wide), :] = acc[...].T
    for copy in copies:
        copy.wait()

def place_pair(pair, firsts, extra_at, out_at, info, width, own, other, whole=None):
    aliased = int(whole is not None)
    turned = out_at is not None
    return pl.pallas_call(
        functools.partial(place_pair_body, pair, firsts, extra_at, out_at, aliased),
        grid_spec=pltpu.PrefetchScalarGridSpec(
            num_scalar_prefetch=1, grid=(1,),
            in_specs=[ANYWHERE] * aliased + [full(own.shape), full(other.shape)],
            out_specs=[ANYWHERE, full((256, 128)), full((256, 128))] + [full((width, width))] * turned,
            scratch_shapes=[pltpu.VMEM((6, width, 128), F32), pltpu.SemaphoreType.DMA((6,))] + [pltpu.VMEM((width, width // 2), F32)] * turned),
        out_shape=[f32(width, 3 * width), f32(256, 128), f32(256, 128)] + [f32(width, width)] * turned,
        input_output_aliases={1: 0} if aliased else {},
        compiler_params=params("arbitrary"),
        cost_estimate=cost(3),
        name="place_pair",
    )(info, *([whole] if aliased else []), own, other)


AXES = ("dp", "mp")
CORE, ROW, COLUMN, NEAR_DEPTH, FAR_DEPTH = 1, 2, 4, 8, 16
PARTS = ((0, 1), (1, 2))
WEIGHT = [("weight", k) for k in range(3)]
MASKS = [("mask", 0), ("mask", 1)]
OUT = [("out", k) for k in range(3)]
STEPS = ((1, ORDER_B, [*MASKS, *WEIGHT, *OUT, ("extra", 0)]), (2, ORDER_B, [*MASKS, *WEIGHT, ("extra", 0)]),
         (0, ORDER_B, [*MASKS, *WEIGHT, ("extra", 0)]))
SCHEDULE = (
    "send_down", "own_down", (3, "first"), "ffn", 0, (3, "second"), 1, (3, "near_deep"), 2, (0, "near"), (3, "far_deep"),
    (1, "near"), "send_in", (3, "spread_far"), "own_in", (4, "first"), (0, "near_deep"), (2, "near"), (1, "near_deep"),
    (3, "spread_near"), "tokens", (0, "far_deep"), (2, "near_deep"), (1, "far_deep"), (3, "spread_column"), (4, "second"),
    (0, "spread_far"), (2, "far_deep"), (1, "spread_far"), (0, "spread_near"), (3, "whole"), (4, "near_deep"),
    (2, "spread_far"), (0, "gather_column"), (1, "spread_near"), (4, "far_deep"), (2, "spread_near"), (0, "gather_row"),
    (1, "gather_column"), (4, "spread_far"), (2, "gather_column"), (1, "gather_row"), (2, "gather_row"), (4, "spread_near"),
    (0, "gather_core"), (1, "gather_core"), (0, "place"), (4, "spread_column"), (2, "gather_core"), (1, "place"),
    (2, "place"), (4, "whole"),
)


class Order:
    def __init__(self):
        self.last = None

    def hold(self, value):
        return value if self.last is None else lax.optimization_barrier((value, self.last))[0]

    def do(self, step, *operands):
        result = step(*self.hold(operands))
        self.last = jax.tree.leaves(result)[0]
        return result


class Links:
    def __init__(self, dp, mp):
        self.dp, self.mp = dp, mp
        self.direct = dp == 8 and mp == 4
        self.at_dp, self.at_mp = lax.axis_index("dp"), lax.axis_index("mp")
        self.core, self.row, self.column = self.at_mp % 2, self.at_mp // 2, self.at_dp % 2
        self.near_deep, self.far_deep = self.at_dp // 2 % 2, self.at_dp // 4
        slot = jnp.arange(16)
        z, low, high = (((slot >> 1) & 1) << 1) | ((slot & 1) << 2), (slot >> 2) & 1, slot >> 3
        if self.direct:
            def chip(x, y):
                return (self.at_dp ^ (x | z)) * 2 + (self.row ^ y)
            orders = [chip(low, high), chip(high, low)]
        else:
            orders = [slot, slot]
        rest = jnp.stack([self.core, 1 - self.core, *(self.at_mp ^ k for k in range(4)),
                          self.column, self.near_deep, self.far_deep])
        self.info = jnp.concatenate([*orders, rest]).astype(jnp.int32)

    def swap(self, value, bits):
        count = self.dp * self.mp
        return lax.ppermute(value, AXES, [(i, i ^ bits) for i in range(count)])

    def grow(self, value, *axes):
        for bits in axes:
            value = jnp.concatenate([value, self.swap(value, bits)])
        return value


def pick(index, first, second):
    return jnp.where(index == 0, first, second)


def in_order(index, own, other, axis=0):
    return pick(index, jnp.stack([own, other], axis), jnp.stack([other, own], axis))


def at(value, index, axis):
    return lax.dynamic_index_in_dim(value, index, axis, False)


def axes_of(order):
    return (ROW, COLUMN) if order == ORDER_A else (COLUMN, ROW)


def add(*values):
    return sum(v.astype(F32) for v in values)


def any_hidden(links, keep):
    zero = jnp.zeros_like(keep[0])
    blocks = jnp.stack([keep[0], zero, keep[1], zero])
    blocks = jnp.stack([blocks[links.at_mp ^ k] for k in range(4)])
    return lax.psum(lax.psum_scatter(blocks, "mp", scatter_dimension=0, tiled=False), "dp")


class Hidden:
    def __init__(self, links, order, axis):
        self.links, self.order, self.axis = links, order, axis

    def begin(self, keep, came):
        self.shape = keep.shape[1:]
        self.parts = (2, 2, 2, 2, self.shape[0] // 8, self.shape[1])
        self.total, self.came = keep, came

    def first(self):
        column = self.links.column

        def step(keep, came):
            total = add(keep, came).reshape(self.parts)
            if self.axis == ROW:
                return total[1].astype(BF), total[0]
            return at(total, 1 - column, 3).astype(BF), at(total, column, 3)
        away, self.total = self.order.do(step, self.total, self.came)
        self.came = self.links.swap(away, self.axis)

    def second(self):
        column = self.links.column

        def step(total, came):
            total = add(total, came)
            if self.axis == ROW:
                return at(total, 1 - column, 2).astype(BF), at(total, column, 2)
            return total[1].astype(BF), total[0]
        away, self.total = self.order.do(step, self.total, self.came)
        self.came = self.links.swap(away, (ROW | COLUMN) ^ self.axis)

    def halve(self, index, axis, bits):
        def step(total, came):
            total = add(total, came)
            return at(total, 1 - index, axis).astype(BF), at(total, index, axis)
        away, self.total = self.order.do(step, self.total, self.came)
        self.came = self.links.swap(away, bits)

    def near_deep(self):
        self.halve(self.links.near_deep, 1, NEAR_DEPTH)

    def far_deep(self):
        self.halve(self.links.far_deep, 0, FAR_DEPTH)

    def spread_far(self):
        self.total = self.order.do(lambda a, b: add(a, b).astype(BF), self.total, self.came)
        self.came = self.links.swap(self.total, FAR_DEPTH)

    def spread(self, index, axis, bits):
        self.total = self.order.do(lambda a, b: in_order(index, a, b, axis), self.total, self.came)
        self.came = self.links.swap(self.total, bits)

    def spread_near(self):
        self.spread(self.links.far_deep, 0, NEAR_DEPTH)

    def spread_column(self):
        self.spread(self.links.near_deep, 1, COLUMN)

    def whole(self):
        self.result = self.order.do(lambda a, b: in_order(self.links.column, a, b, 2).astype(F32).reshape(self.shape), self.total, self.came)


class Slots:
    def __init__(self, links, order, axes, masks):
        self.links, self.order, self.axes, self.masks = links, order, axes, masks
        self.slots, self.came = [], []

    def far(self, slots):
        self.slots.append(slots)
        self.came.append(self.links.swap(slots[0], self.axes[0]))

    def near(self):
        def step(mids, came):
            return jnp.concatenate([add(m, c[4:]).astype(BF) for m, c in zip(mids, came)], axis=1)
        self.beside = self.links.swap(self.order.do(step, [s[1] for s in self.slots], self.came), self.axes[1])

    def deep(self, which, first, last):
        slots, came, beside = which
        return jnp.concatenate([add(s, c[first:last]) for s, c in zip(slots, came)], axis=1) + beside[first:last].astype(F32)

    def near_deep(self):
        step = lambda *which: self.deep(which, 2, 4).astype(BF)
        sent = self.order.do(step, [s[2] for s in self.slots], self.came, self.beside)
        self.behind = self.links.swap(sent, NEAR_DEPTH)

    def far_deep(self):
        def step(which, behind):
            total = self.deep(which, 0, 2) + behind.astype(F32)
            return total[1].astype(BF), total[0]
        sent, self.total = self.order.do(step, ([s[3] for s in self.slots], self.came, self.beside), self.behind)
        self.came = self.links.swap(sent, FAR_DEPTH)

    def spread_far(self):
        def step(total, came):
            total = total + came.astype(F32)
            row, masks, rest = 0, [], []
            for slots, count in zip(self.slots, self.masks):
                rows = slots[0].shape[1]
                masks.append(total[row:row + count])
                rest.append(total[row + count:row + rows])
                row += rows
            return jnp.concatenate(rest)[None].astype(BF), masks
        self.whole, self.mask_rows = self.order.do(step, self.total, self.came)
        self.came = self.links.swap(self.whole, FAR_DEPTH)

    def spread_near(self):
        self.spread(NEAR_DEPTH)

    def gather_column(self):
        self.spread(COLUMN)

    def gather_row(self):
        self.spread(ROW)

    def gather_core(self):
        self.spread(CORE)

    def spread(self, bits):
        self.whole = self.order.do(lambda a, b: jnp.concatenate([a, b]), self.whole, self.came)
        self.came = self.links.swap(self.whole, bits)


def body(dp, mp, tokens, w_qkv, bias_q, bias_v, w_out, bias_out, norm1_gain, norm1_bias, w_in, bias_in, w_down, bias_down,
         norm2_gain, norm2_bias, mask_logits, mask_noise, grad_out):
    width = w_out.shape[0]
    heads, rows_own, length = mask_logits.shape
    half = heads // 2
    links, order = Links(dp, mp), Order()
    core, info, swap, do = links.core, links.info, links.swap, order.do

    def chances(logits, noise):
        fraction = noise.astype(F32) / 65536.0
        return logits + jnp.log(fraction) - jnp.log(1.0 - fraction)

    def codes(logits, noise):
        logit = chances(logits, noise)
        tail = jax.nn.sigmoid(-jnp.abs(logit)) * MASK_SCALE
        return jnp.where(logit < 0.0, tail, -tail).astype(BF)

    shift = jnp.concatenate([wide(bias_q), jnp.zeros((width,), F32), wide(bias_v)])[None]
    norms = (bias_out, norm1_gain, norm1_bias, bias_down, norm2_gain, norm2_bias)
    pack = lambda *v: jnp.concatenate([wide(x) for x in v] + [jnp.zeros(((8 - len(v)) * width,), F32)]).reshape(8, width)
    mixed, totals, came = [], [], []

    def attention(part, pieces):
        own, other, total = do(lambda q, m: attend(*PARTS[part], info, q, m), qkv, pieces)
        mixed.append((own, other))
        came.append(swap(other, CORE))
        totals.append(total)

    if links.direct:
        plane = (1, rows_own, length)

        def two_sides(logits, noise, bias):
            code = codes(logits, noise)
            row = jnp.pad(bias, (0, rows_own * length - bias.shape[0])).reshape(plane)
            return jnp.concatenate([pick(core, code[half:], code[:half]), row]), pick(core, code[:half], code[half:])
        away, keep = do(two_sides, mask_logits, mask_noise, bias_in)
        beside = swap(away, CORE)
        other_tokens = swap(tokens, CORE)

        parts = half // 2

        def chip_codes(keep, beside):
            chip = in_order(core, keep, beside[:half], 1).reshape(parts, 2, 1, 2 * rows_own, length)
            return [[chip[p:p + n, h] for h in range(2)] for p, n in PARTS], beside[half].reshape(-1)[:bias_in.shape[0]]
        chip, near_bias = do(chip_codes, keep, beside)
        flat = lambda tree: jnp.concatenate([v for part in tree for v in part])
        behind = swap(flat(chip), FAR_DEPTH)
        eighth = w_in.shape[0] // 8
        split = lambda w: w.reshape(4, 2, eighth, width)
        z_at, x_at = links.at_dp // 2, links.column

        def to_row(w_in, w_down, *biases):
            parts = [at(at(split(w), z_at, 0), x_at, 0) for w in (w_in, w_down)]
            return jnp.concatenate([*parts, jnp.pad(jnp.stack(biases), ((0, 14), (0, 0)))])
        piece = swap(do(to_row, w_in, w_down, bias_in, near_bias), ROW)
        qkv = do(lambda *v: project(info, *v), tokens, other_tokens, w_qkv, shift)
        piece = order.hold(piece)
        axes = ((COLUMN, ROW), (ROW, COLUMN))
        groups, seconds, fars = [None] * 2, [None] * 2, [None] * 2

        def deep_parts(chip, behind):
            result, row = [], 0
            for part, (p, n) in zip(chip, PARTS):
                heads = []
                for own in part:
                    heads.append(jnp.concatenate([own, behind[row:row + n]], axis=1))
                    row += n
                result.append(jnp.concatenate(heads))
            return result
        deep = do(deep_parts, chip, behind)
        deep = [(v, swap(v, NEAR_DEPTH)) for v in deep]

        def gather_near(part):
            n = PARTS[part][1]
            groups[part] = do(lambda a, b: [jnp.concatenate([a[h * n:h * n + n], b[h * n:h * n + n]], axis=1) for h in range(2)], *deep[part])
            seconds[part] = [swap(groups[part][h], axes[h][0]) for h in range(2)]

        def gather_far(part):
            both = do(lambda g, s: [jnp.concatenate(v, axis=1) for v in zip(g, s)], groups[part], seconds[part])
            fars[part] = [swap(both[h], axes[h][1]) for h in range(2)]

        behind = swap(piece[:2 * eighth], FAR_DEPTH)
        gather_near(0)
        gather_far(0)
        gather_near(1)
        vecs = do(pack, *norms)
        biases = do(lambda *v: wide(jnp.concatenate(v)).reshape(4, width), bias_in, near_bias, piece[2 * eighth], piece[2 * eighth + 1])
        pair = do(lambda a, b: in_order(links.far_deep, a[:2 * eighth], b), piece, behind)
        behind = swap(pair, NEAR_DEPTH)
        gather_far(1)
        pieces = [[v for h in range(2) for v in (groups[p][h], seconds[p][h], fars[p][h])] for p in range(2)]
        beside = swap(do(lambda *v: jnp.stack(v), w_in, w_down), CORE)
        attention(0, pieces[0])
        beside = order.hold(beside)

        def group_step(own, came, w):
            group = in_order(links.near_deep, own, came, 1)
            return [v.reshape(4, eighth, width) for v in jnp.split(group, 2, axis=2)], at(split(w), 1 - x_at, 1)
        group, straight = do(group_step, pair, behind, w_down)
        around, straight = swap(group[0], COLUMN), swap(straight, ROW)
        near_in, near_down = do(lambda v: [v[0], v[1]], beside)
        attention(1, pieces[1])
        came[0] = order.hold(came[0])
        blocks_in, blocks_down = [w_in, near_in], [w_down, near_down]
    else:
        other_tokens = swap(tokens, CORE)
        qkv = project(info, tokens, other_tokens, w_qkv, shift)
        whole = lax.all_gather(codes(mask_logits, mask_noise), AXES, axis=1, tiled=True)
        own = lax.dynamic_slice_in_dim(whole, core * half, half, 0).reshape(half // 2, 2, 16, length // 16, length)
        own = own.transpose(1, 0, 2, 3, 4)
        pieces = [[own[h, p:p + n, a:b] for h in range(2) for a, b in ((0, 4), (4, 8), (8, 16))] for p, n in PARTS]
        attention(0, pieces[0])
        attention(1, pieces[1])
        vecs = pack(*norms)
        blocks_in, blocks_down, blocks_bias = ([v[links.at_mp ^ k] for k in range(4)]
                                               for v in (lax.all_gather(w, "mp") for w in (w_in, w_down, bias_in)))
        biases = wide(jnp.stack(blocks_bias))
    first_low, active, slope, normal, inverse, branch = do(
        lambda *v: ffn_first(info, *v), tokens, [own for own, _ in mixed] + came, w_out, vecs, biases, blocks_in[:2], blocks_down[:2])
    if links.direct:
        across = do(lambda *v: [in_order(links.column, a, b, 1).reshape(w_in.shape) for a, b in (v[:2], v[2:])],
                    group[0], around, group[1], straight)
        blocks_in += [across[0], swap(across[0], CORE)]
        blocks_down += [across[1], swap(across[1], CORE)]
    out, active_two, slope_two, grad_second, grad_branch, sums = do(
        ffn_second, first_low, branch, grad_out, vecs, biases, blocks_in[2:], blocks_down[2:])
    d_own, d_other, slots = [None] * 3, [None] * 3, [None] * 3
    hidden = [Hidden(links, order, COLUMN), Hidden(links, order, COLUMN)]
    keep, grads, settled = [None] * 2, {}, []

    def send_down():
        grads["sent_down"] = swap(do(functools.partial(outer, (1, 1), bf), active, active_two, grad_branch), CORE)

    def own_down():
        keep[0] = do(functools.partial(outer, (0, 0), f32), active, active_two, grad_branch)
        hidden[0].begin(keep[0], grads["sent_down"])

    def ffn_gradient():
        grads["pre"], grads["one"], grads["attn"], grads["small"] = do(
            lambda *v: ffn_back(info, *v), grad_branch, [slope, slope_two], grad_second, normal, inverse, vecs, sums, blocks_in, blocks_down)
        grads["pair"] = grads["attn"], swap(grads["attn"], CORE)

    def settle():
        for pair in range(3):
            if d_other[pair] is not None and pair not in settled:
                settled.append(pair)
                d_other[pair] = order.hold(d_other[pair])

    def send_in():
        sent = do(functools.partial(outer, (1, 3), bf), grads["pre"], grads["pre"], first_low)
        settle()
        grads["sent_in"] = swap(sent, CORE)

    def own_in():
        keep[1] = do(functools.partial(outer, (0, 2), f32), grads["pre"], grads["pre"], first_low)
        hidden[1].begin(keep[1], grads["sent_in"])

    def back(step):
        pair, place, segments = STEPS[step]
        part = min(pair, 1)
        local = pair - PARTS[part][0]
        own, other, *outs = do(
            lambda *v: attend_back(pair, local, [(place, segments)], info, *v), qkv, mixed[part], grads["pair"], w_out,
            totals[part], (tokens, other_tokens), pieces[part], () if step else mixed, grads["small"])
        settle()
        slots[step] = outs
        if links.direct:
            chains[step].far(outs)
        d_own[pair] = own
        d_other[pair] = swap(other, CORE)

    def grad_input():
        grads["tokens"] = do(lambda *v: grad_tokens(info, *v), [*d_own, *d_other], grads["one"], w_qkv)

    def place(step):
        pair, _, segments = STEPS[step]
        found, row = {}, 0
        for kind, k in segments:
            if kind != "mask":
                found[kind, k] = row
                row += segment_rows(kind, length, width)
        whole = [] if result[0] is None else [result[0]]
        result[0], *extras = do(lambda a, b, *w: place_pair(pair, [found["weight", k] for k in range(3)], found["extra", 0],
                                                            found.get(("out", 0)), info, width, a, b, *w), *placed[step], *whole)
        if step == 0:
            result[1] = extras.pop()
            result[2] = (extras[0][:60] + extras[1][:60]).reshape(10, width)
        bias[pair] = jnp.stack([e[64:67] for e in extras])

    result, bias, placed = [None] * 3, [None] * 3, [None] * 3
    masks = [sum(kind == "mask" for kind, _ in segments) * length // 4 for _, _, segments in STEPS]
    chains = [Slots(links, order, axes_of(place), [count]) for (_, place, _), count in zip(STEPS, masks)]
    kernels = {"send_down": send_down, "own_down": own_down, "ffn": ffn_gradient, "send_in": send_in, "own_in": own_in, "tokens": grad_input}
    for step in range(3):
        kernels[step] = functools.partial(back, step)
    mask_rows = [None] * 3
    for name in SCHEDULE:
        if name in kernels:
            kernels[name]()
        elif links.direct:
            who, what = name
            chain = hidden[who - 3] if who >= 3 else chains[who]
            if what == "place":
                placed[who] = (chain.whole, chain.came)
                place(who)
            else:
                getattr(chain, what)()
    if links.direct:
        grad_w_down, grad_w_in = (chain.result for chain in hidden)
        mask_rows = [chain.mask_rows[0].reshape(2, 4, length // 16, 128) for chain in chains]
    else:
        grad_w_down, grad_w_in = (any_hidden(links, k + wide(grads[s])) for k, s in zip(keep, ("sent_down", "sent_in")))
        for step, (s, count) in enumerate(zip(slots, masks)):
            own = wide(jnp.concatenate(s[::-1]))
            both = lax.psum(in_order(core, own, jnp.zeros_like(own)), AXES)
            sides = [both[core], both[1 - core]]
            placed[step] = [v[:, count:].astype(BF) for v in sides]
            mask_rows[step] = jnp.stack([v[:, :count].reshape(16, 2, 4, length // 16, 128).transpose(1, 2, 0, 3, 4) for v in sides])
    if not links.direct:
        for step in range(3):
            place(step)
    grad_w_qkv, grad_w_out, small = result
    by_pair = [None] * 3
    for (pair, _, _), rows in zip(STEPS, mask_rows):
        by_pair[pair] = rows
    bias = jnp.stack(bias, axis=2)
    bias = pick(core, bias, bias[::-1]).transpose(1, 0, 2, 3).reshape(3, width)
    if links.direct:
        mask_sum = jnp.stack(by_pair).transpose(0, 1, 3, 2, 4).reshape(half, 2 * rows_own, length)
        mine = pick(core, mask_sum[:, :rows_own], mask_sum[:, rows_own:])
        theirs = swap(pick(core, mask_sum[:, rows_own:], mask_sum[:, :rows_own]), CORE)
    else:
        mine, theirs = jnp.stack(by_pair, axis=1).transpose(0, 1, 2, 4, 5, 3, 6).reshape(2, half, length, length)
        place = (links.at_dp * mp + links.at_mp) * rows_own
        mine, theirs = (lax.dynamic_slice_in_dim(m, place, rows_own, 1) for m in (mine, theirs))
    mask_sum = pick(core, jnp.concatenate([mine, theirs]), jnp.concatenate([theirs, mine]))
    mask_own = jax.nn.sigmoid(chances(mask_logits, mask_noise))
    grad_mask_logits = mask_sum * (MASK_SCALE * mask_own * (1.0 - mask_own))
    return (out, grads["tokens"], grad_w_qkv, bias[0], bias[2], grad_w_out, small[5], small[3], small[4], grad_w_in, small[6 + links.at_mp],
            grad_w_down, small[2], small[0], small[1], grad_mask_logits)


def solution(mesh):
    both, none = ("dp", "mp"), P()
    rows, mask, split = P(both, None), P(None, both, None), P("mp", None)
    ins = (rows, none, none, none, none, none, none, none, split, P("mp"), split, none, none, none, mask, mask, rows)
    outs = (rows, rows, none, none, none, none, none, none, none, split, P("mp"), split, none, none, none, mask)
    step = functools.partial(body, mesh.shape["dp"], mesh.shape["mp"])
    return jax.shard_map(step, mesh=mesh, in_specs=ins, out_specs=outs, check_vma=False)
```

```python
import functools

import jax
import jax.numpy as jnp
from jax import lax
from jax.experimental import pallas as pl
from jax.experimental.pallas import tpu as pltpu
from jax.sharding import PartitionSpec as P

MASK_SCALE = 4.0

BF = jnp.bfloat16
F32 = jnp.float32
NT = (((1,), (1,)), ((), ()))
NN = (((1,), (0,)), ((), ()))
TN = (((0,), (0,)), ((), ()))
VMEM_LIMIT = 56 * 1024 * 1024
SIZES = (8, 4, 2, 2)

ORDER_A, ORDER_B, OWN_CORE, OTHER_CORE, PLACE, COLUMN_AT, NEAR_AT, FAR_AT = 0, 16, 32, 33, 34, 38, 39, 40

COST = 0.001

def cost(us):
    return pl.CostEstimate(flops=int(us * 1.0e9 * COST), transcendentals=0, bytes_accessed=int(us * 2.0e6 * COST))

def dot(a, b, dims=NN):
    return lax.dot_general(a, b, dims, preferred_element_type=F32)

def bf(*shape):
    return jax.ShapeDtypeStruct(shape, BF)

def f32(*shape):
    return jax.ShapeDtypeStruct(shape, F32)

def identity(n):
    return (lax.broadcasted_iota(jnp.int32, (n, n), 0) == lax.broadcasted_iota(jnp.int32, (n, n), 1)).astype(F32).astype(BF)

def params(*sem):
    return pltpu.CompilerParams(dimension_semantics=sem or None, vmem_limit_bytes=VMEM_LIMIT)

def place_mask(order_ref, pieces, codes, bias, eye):
    rows = codes.shape[0] // 16
    for head in range(2):
        slot = 0
        for group in pieces[head * 3:head * 3 + 3]:
            for j in range(group.shape[1]):
                start = pl.multiple_of(order_ref[head * 16 + slot] * rows, rows)
                codes[pl.ds(start, rows), :] = group[0, j]
                slot += 1
        turned = dot(eye, codes[...], NT)
        bias[head] = jnp.where(turned > 0.0, turned - 4.0, turned)

def halves(seqs, length, lane):
    half = seqs // 2
    return [pl.BlockSpec((length, lane), lambda i, s, *_: (jnp.minimum(s, half - 1), i)),
            pl.BlockSpec((length, lane), lambda i, s, *_: (jnp.maximum(s - half, 0), i))]

def mask_specs(pieces):
    return [pl.BlockSpec((1, *p.shape[1:]), lambda i, s, *_: (i, 0, 0, 0)) for p in pieces]

def qkv_specs(first, length):
    def part(which):
        return pl.BlockSpec((1, length, 128), lambda i, s, *_: (which, s, first + i))
    return [part(0), part(1), part(2)]

def split_heads(value, first):
    zero = jnp.zeros_like(value)
    return jnp.concatenate([jnp.where(first, value, zero), jnp.where(first, zero, value)])

def attend_body(order_ref, q_ref, k_ref, v_ref, *refs):
    pieces, (own_ref, other_ref, total_ref), (codes, bias) = refs[:6], refs[6:9], refs[9:]
    length = codes.shape[0]
    step, count = pl.program_id(1), pl.num_programs(1)
    @pl.when(step == 0)
    def _():
        place_mask(order_ref, pieces, codes, bias, identity(length))
    half = q_ref.shape[2] // 2
    lanes = lax.broadcasted_iota(jnp.int32, (1, 2 * half), 1)
    query, keys = q_ref[0], k_ref[0]
    values_t = v_ref[0].T
    outs = []
    both = dot(split_heads(keys, lanes < half), query, NT)
    for head in range(2):
        scores = both[head * length:(head + 1) * length] + bias[head]
        highest = jnp.max(scores, axis=0, keepdims=True)
        powers = jnp.exp(scores - highest)
        summed = jnp.sum(powers, axis=0, keepdims=True)
        probs = (powers * (1.0 / summed)).astype(BF)
        outs.append(dot(values_t[head * half:(head + 1) * half], probs))
        total_ref[0, 0, head:head + 1, :] = highest + jnp.log(summed)
    mixed = jnp.concatenate(outs, axis=0).T.astype(BF)
    @pl.when(step < count // 2)
    def _():
        own_ref[...] = mixed
    @pl.when(step >= count // 2)
    def _():
        other_ref[...] = mixed

def attend(first, count, order, qkv, pieces):
    _, tokens, width = qkv.shape
    length = pieces[0].shape[3]
    seqs = tokens // length
    sds = jax.ShapeDtypeStruct
    return pl.pallas_call(
        attend_body,
        grid_spec=pltpu.PrefetchScalarGridSpec(
            num_scalar_prefetch=1, grid=(count, seqs),
            in_specs=qkv_specs(first, length) + mask_specs(pieces),
            out_specs=[*halves(seqs, length, 128), pl.BlockSpec((1, 1, 8, length), lambda i, s, *_: (i, s, 0, 0))],
            scratch_shapes=[pltpu.VMEM((length, length), BF), pltpu.VMEM((2, length, length), F32)],
        ),
        out_shape=[sds((tokens // 2, count * 128), BF)] * 2 + [sds((count, seqs, 8, length), F32)],
        compiler_params=params("arbitrary", "arbitrary"),
        cost_estimate=cost(9 * count),
        name="attend",
    )(order, qkv, qkv, qkv, *pieces)

def attend_back_body(groups, has_out, info_ref, *refs):
    (q_ref, k_ref, v_ref, mixed_own, mixed_other, ga_own, ga_other, wout_ref, total_ref, tok_own, tok_other), refs = refs[:11], refs[11:]
    pieces, refs = refs[:6], refs[6:]
    all_own, all_other, small_ref = (), (), None
    if has_out:
        all_own, all_other, small_ref, refs = refs[:has_out], refs[has_out:2 * has_out], refs[2 * has_out], refs[2 * has_out + 1:]
    own_ref, other_ref, refs = refs[0], refs[1], refs[2:]
    outs, refs = refs[:4 * len(groups)], refs[4 * len(groups):]
    codes, bias, acc, weight, extra = refs[:5]
    weight_out = refs[5] if has_out else None
    length = codes.shape[0]
    step, steps = pl.program_id(0), pl.num_programs(0)
    @pl.when(step == 0)
    def _():
        place_mask(info_ref, pieces, codes, bias, identity(length))
        acc[...] = jnp.zeros_like(acc)
        weight[...] = jnp.zeros_like(weight)
        extra[...] = jnp.zeros_like(extra)
        if has_out:
            extra[0:small_ref.shape[0], :] = small_ref[...]
            weight_out[...] = jnp.zeros_like(weight_out)
    half = q_ref.shape[2] // 2
    lanes = lax.broadcasted_iota(jnp.int32, (1, 2 * half), 1)
    query, keys, values = q_ref[0], k_ref[0], v_ref[0]
    keys_t = keys.T
    is_own = step < steps // 2
    grad_attn = jnp.where(is_own, ga_own[...], ga_other[...])
    grad = dot(grad_attn, wout_ref[...], NT).astype(BF)
    mixed = jnp.where(is_own, mixed_own[...], mixed_other[...])
    inner = (grad.astype(F32) * mixed.astype(F32)).T
    first = lanes < half
    scores_both = dot(split_heads(keys, first), query, NT)
    grads_both = dot(split_heads(values, first), grad, NT)
    dq, lows, rounded = [], [], []
    for head in range(2):
        at = slice(head * length, (head + 1) * length)
        probs = jnp.exp(scores_both[at] + bias[head] - total_ref[0, 0, head:head + 1, :])
        delta = jnp.sum(inner[head * half:(head + 1) * half], axis=0, keepdims=True)
        grad_scores = probs * (grads_both[at] - delta)
        acc[head] += grad_scores
        lows.append(grad_scores.astype(BF))
        rounded.append(probs.astype(BF))
        dq.append(dot(keys_t[head * half:(head + 1) * half], lows[head]))
    dv = dot(jnp.concatenate(rounded), grad)
    dk = dot(jnp.concatenate(lows), query)
    dv, dk = (jnp.split(v, 2) for v in (dv, dk))
    result = jnp.concatenate([(jnp.concatenate(dq, axis=0).T * 0.125).astype(BF),
                              jnp.where(first, dk[0], dk[1]).astype(BF),
                              jnp.where(first, dv[0], dv[1]).astype(BF)], axis=1)
    @pl.when(is_own)
    def _():
        own_ref[...] = result
    @pl.when(jnp.logical_not(is_own))
    def _():
        other_ref[...] = result
    weight[...] += dot(jnp.where(is_own, tok_own[...], tok_other[...]), result, TN)
    sums = jnp.sum(result.astype(F32), axis=0, keepdims=True)
    for third in range(3):
        extra[64 + third:65 + third, :] += sums[:, third * 128:(third + 1) * 128]
    if has_out:
        whole = jnp.where(is_own, jnp.concatenate([m[...] for m in all_own], axis=1),
                          jnp.concatenate([m[...] for m in all_other], axis=1))
        weight_out[...] += dot(grad_attn, whole, TN)
    rows, wrows = length // 16, weight.shape[0] // 16
    @pl.when(step == steps - 1)
    def _():
        eye = identity(length)
        for head in range(2):
            acc[head] = dot(eye, acc[head].astype(BF), NT)
        for g, (order, segments) in enumerate(groups):
            at = 16
            for out in outs[4 * g:4 * g + 4]:
                at -= out.shape[0]
                for j in range(out.shape[0]):
                    place = info_ref[order + at + j]
                    row = 0
                    for kind, k in segments:
                        if kind == "mask":
                            value = acc[k, pl.ds(pl.multiple_of(place * rows, rows), rows), :].astype(BF)
                            for t in range(length // 128):
                                out[j, row:row + rows, :] = value[:, t * 128:(t + 1) * 128]
                                row += rows
                        elif kind == "extra":
                            out[j, row:row + 16, :] = extra[pl.ds(pl.multiple_of(place * 16, 16), 16), :].astype(BF)
                            row += 16
                        else:
                            source = weight if kind == "weight" else weight_out
                            value = source[pl.ds(pl.multiple_of(place * wrows, wrows), wrows), k * 128:(k + 1) * 128]
                            out[j, row:row + wrows, :] = value.astype(BF)
                            row += wrows

def segment_rows(kind, length, width):
    return {"mask": length // 4, "extra": 16}.get(kind, width // 16)

def attend_back(pair, local, groups, info, qkv, mixed, grad_attn, w_out, total, tokens, pieces, all_mixed=(), small=None):
    _, seqs, _, length = total.shape
    rows_all, width = 2 * tokens[0].shape[0], tokens[0].shape[1]
    half = seqs // 2
    def split(wide, at=0):
        return [pl.BlockSpec((length, wide), lambda s, *_: (jnp.minimum(s, half - 1), at)),
                pl.BlockSpec((length, wide), lambda s, *_: (jnp.maximum(s - half, 0), at))]
    def part(which):
        return pl.BlockSpec((1, length, 128), lambda s, *_: (which, s, pair))
    masks = [pl.BlockSpec((1, *p.shape[1:]), lambda s, *_: (local, 0, 0, 0)) for p in pieces]
    extras, extra_specs = [], []
    scratch = [pltpu.VMEM((length, length), BF), pltpu.VMEM((2, length, length), F32), pltpu.VMEM((2, length, length), F32),
               pltpu.VMEM((width, 384), F32), pltpu.VMEM((256, 128), F32)]
    if all_mixed:
        extras = [m[0] for m in all_mixed] + [m[1] for m in all_mixed] + [small]
        extra_specs = [split(m.shape[1])[k // len(all_mixed)] for k, m in enumerate(extras[:-1])] + [full(small.shape)]
        scratch.append(pltpu.VMEM((width, width // 2), F32))
    sds = jax.ShapeDtypeStruct
    shapes = [(n, sum(segment_rows(kind, length, width) for kind, _ in segments), 128) for _, segments in groups for n in SIZES]
    return pl.pallas_call(
        functools.partial(attend_back_body, groups, len(all_mixed)),
        grid_spec=pltpu.PrefetchScalarGridSpec(
            num_scalar_prefetch=1, grid=(seqs,),
            in_specs=[part(0), part(1), part(2), *split(128, local), *split(width),
                      pl.BlockSpec((128, width), lambda s, info: (info[OWN_CORE] * 3 + pair, 0)),
                      pl.BlockSpec((1, 1, 8, length), lambda s, *_: (local, s, 0, 0)), *split(width), *masks, *extra_specs],
            out_specs=split(384) + [full(x) for x in shapes],
            scratch_shapes=scratch,
        ),
        out_shape=[sds((rows_all // 2, 384), BF)] * 2 + [sds(x, BF) for x in shapes],
        compiler_params=params("arbitrary"),
        cost_estimate=cost(18 + 3 * bool(all_mixed)),
        name="attend_back",
    )(info, qkv, qkv, qkv, *mixed, *grad_attn, w_out, total, *tokens, *pieces, *extras)

def full(shape):
    return pl.BlockSpec(shape, lambda *_: (0,) * len(shape))

def project_body(info_ref, own_ref, other_ref, w_ref, shift_ref, out_ref):
    third = pl.program_id(0)
    scale = jnp.where(third == 0, 0.125, 1.0)
    rows = own_ref.shape[0]
    for i, ref in enumerate((own_ref, other_ref)):
        value = (dot(ref[...], w_ref[...]) + shift_ref[...]).astype(BF)
        out_ref[0, i * rows:(i + 1) * rows] = (value.astype(F32) * scale).astype(BF)

def project(info, own_tokens, other_tokens, w_qkv, shift):
    rows, width = own_tokens.shape
    own = width // 2
    return pl.pallas_call(
        project_body,
        grid_spec=pltpu.PrefetchScalarGridSpec(
            num_scalar_prefetch=1, grid=(3,),
            in_specs=[full((rows, width)), full((rows, width)),
                      pl.BlockSpec((width, own), lambda t, info: (0, 2 * t + info[OWN_CORE])),
                      pl.BlockSpec((1, own), lambda t, info: (0, 2 * t + info[OWN_CORE]))],
            out_specs=pl.BlockSpec((1, 2 * rows, own), lambda t, c: (t, 0, 0)),
        ),
        out_shape=jax.ShapeDtypeStruct((3, 2 * rows, own), BF),
        compiler_params=params("arbitrary"),
        cost_estimate=cost(8),
        name="project",
    )(info, own_tokens, other_tokens, w_qkv, shift)

def erf_parts(u):
    d = 1.0 + 0.23164189 * jnp.abs(u)
    t = pl.reciprocal(d, approx=True)
    t = t * (2.0 - d * t)
    e = jnp.exp2((-0.7213475204444817 * u) * u)
    poly = t * (0.127414796 + t * (-0.142248368 + t * (0.7107068705 + t * (-0.7265760135 + t * 0.5307027145))))
    tail = poly * e
    return jnp.where(u < 0.0, tail, 1.0 - tail), e * 0.3989422804014327

def row_mean(v):
    return jnp.mean(v, axis=-1, keepdims=True)

def column_sum(v):
    return jnp.sum(v, axis=0, keepdims=True)

def norm_parts(value):
    centered = value - row_mean(value)
    inverse = lax.rsqrt(row_mean(centered * centered) + 1e-12)
    return centered * inverse, inverse

def norm_back(inner, normal, inverse):
    return inverse * (inner - row_mean(inner) - normal * row_mean(inner * normal))

ANYWHERE = pl.BlockSpec(memory_space=pl.ANY)

def hidden_blocks(first, low, branch, bin_ref, w_in, w_down, active_ref, slope_ref):
    width = low.shape[1]
    pre = dot(low, w_in[0][...], NT)
    for b in range(len(w_in)):
        ahead = dot(low, w_in[b + 1][...], NT) if b + 1 < len(w_in) else None
        strips = []
        for r in range(0, pre.shape[0], 64):
            parts = []
            for c in range(0, width, 256):
                u = pre[r:r + 64, c:c + 256] + bin_ref[first + b:first + b + 1, c:c + 256]
                cum, dens = erf_parts(u)
                parts.append((u * cum).astype(BF))
                slope_ref[r:r + 64, b * width + c:b * width + c + 256] = (cum + u * dens).astype(slope_ref.dtype)
            strips.append(jnp.concatenate(parts, axis=1))
        act = jnp.concatenate(strips, axis=0)
        active_ref[b * width:(b + 1) * width, :] = act.T
        branch += dot(act, w_down[b][...])
        pre = ahead
    return branch

def ffn_first_body(info_ref, tok_ref, *refs):
    count = len(refs) - 13
    mixed, (wout_ref, vec_ref, bin_ref), refs = refs[:count], refs[count:3 + count], refs[3 + count:]
    w_in, w_down, (low_ref, active_ref, slope_ref, norm_ref, inv_ref, branch_ref) = refs[:2], refs[2:4], refs[4:]
    bias_out, gain1, shift1, bias_down = (vec_ref[i:i + 1] for i in range(4))
    value = tok_ref[...].astype(F32) + bias_out
    half = wout_ref.shape[0] // 2
    for side in range(2):
        part = jnp.concatenate([m[...] for m in mixed[side * count // 2:(side + 1) * count // 2]], axis=1)
        start = pl.multiple_of(info_ref[OWN_CORE + side] * half, half)
        value += dot(part, wout_ref[pl.ds(start, half), :])
    normal, inverse = norm_parts(value)
    norm_ref[...] = normal
    inv_ref[...] = jnp.broadcast_to(inverse, inv_ref.shape)
    first = normal * gain1 + shift1
    low = first.astype(BF)
    low_ref[...] = low
    branch_ref[...] = hidden_blocks(0, low, first + bias_down, bin_ref, w_in, w_down, active_ref, slope_ref)

def ffn_second_body(low_ref, branch_ref, gout_ref, vec_ref, bin_ref, *refs):
    w_in, w_down, (out_ref, active_ref, slope_ref, gsec_ref, gbr_ref, sums_ref) = refs[:2], refs[2:4], refs[4:]
    gain2, shift2 = vec_ref[4:5], vec_ref[5:6]
    branch = hidden_blocks(2, low_ref[...], branch_ref[...], bin_ref, w_in, w_down, active_ref, slope_ref)
    normal, inverse = norm_parts(branch)
    out_ref[...] = (normal * gain2 + shift2).astype(BF)
    grad = gout_ref[...].astype(F32)
    back = norm_back(grad * gain2, normal, inverse)
    gsec_ref[...] = back
    gbr_ref[...] = back.astype(BF)
    @pl.when(pl.program_id(0) == 0)
    def _():
        sums_ref[...] = jnp.zeros_like(sums_ref)
    sums_ref[0:1] += column_sum(grad * normal)
    sums_ref[1:2] += column_sum(grad)
    sums_ref[2:3] += column_sum(back)

def ffn_first(info, tokens, mixed, w_out, vecs, b_in, w_in, w_down, tile=256):
    rows, width = tokens.shape
    hidden = 2 * width
    row = lambda n: pl.BlockSpec((tile, n), lambda i, *_: (i, 0))
    return pl.pallas_call(
        ffn_first_body,
        grid_spec=pltpu.PrefetchScalarGridSpec(
            num_scalar_prefetch=1, grid=(rows // tile,),
            in_specs=[row(width)] + [row(m.shape[1]) for m in mixed] + [full(a.shape) for a in (w_out, vecs, b_in, *w_in, *w_down)],
            out_specs=[row(width), pl.BlockSpec((hidden, tile), lambda i, *_: (0, i)), row(hidden), row(width), row(128), row(width)]),
        out_shape=[bf(rows, width), bf(hidden, rows), bf(rows, hidden), f32(rows, width), f32(rows, 128), f32(rows, width)],
        compiler_params=params("arbitrary"),
        cost_estimate=cost(17),
        name="ffn_first",
    )(info, tokens, *mixed, w_out, vecs, b_in, *w_in, *w_down)

def ffn_second(low, branch, grad_out, vecs, b_in, w_in, w_down, tile=256):
    rows, width = low.shape
    hidden = 2 * width
    row = lambda n: pl.BlockSpec((tile, n), lambda i: (i, 0))
    return pl.pallas_call(
        ffn_second_body,
        grid=(rows // tile,),
        in_specs=[row(width)] * 3 + [full(a.shape) for a in (vecs, b_in, *w_in, *w_down)],
        out_specs=[row(width), pl.BlockSpec((hidden, tile), lambda i: (0, i)), row(hidden), row(width), row(width), full((8, width))],
        out_shape=[bf(rows, width), bf(hidden, rows), bf(rows, hidden), f32(rows, width), bf(rows, width), f32(8, width)],
        compiler_params=params("arbitrary"),
        cost_estimate=cost(17),
        name="ffn_second",
    )(low, branch, grad_out, vecs, b_in, *w_in, *w_down)

def ffn_back_body(info_ref, *refs):
    gbr_ref, *slopes, gsec_ref, norm_ref, inv_ref, vec_ref, before_ref = refs[:8]
    w_in, w_down = refs[8:12], refs[12:16]
    gpre_ref, gone_ref, gattn_ref, small_ref, sums_ref = refs[16:]
    gain1 = vec_ref[1:2]
    @pl.when(pl.program_id(0) == 0)
    def _():
        sums_ref[...] = jnp.zeros_like(sums_ref)
    total = lambda v: jnp.sum(v, axis=0, keepdims=True)
    width = gbr_ref.shape[1]
    grad = gsec_ref[...]
    low = gbr_ref[...]
    for b in range(4):
        at = slice(b * width, (b + 1) * width)
        slope = slopes[b // 2][:, b % 2 * width:(b % 2 + 1) * width]
        gpre = (dot(low, w_down[b][...], NT) * slope.astype(F32)).astype(BF)
        gpre_ref[at, :] = gpre.T
        sums_ref[4 + b:5 + b] += total(gpre.astype(F32))
        grad += dot(gpre, w_in[b][...])
    normal, inverse = norm_ref[...], inv_ref[:, 0:1]
    inner = grad * gain1
    back = inverse * (inner - row_mean(inner) - normal * row_mean(inner * normal))
    gone_ref[...] = back
    gattn_ref[...] = back.astype(BF)
    sums_ref[0:1] += total(grad * normal)
    sums_ref[1:2] += total(grad)
    sums_ref[2:3] += total(back)
    @pl.when(pl.program_id(0) == pl.num_programs(0) - 1)
    def _():
        small_ref[...] = jnp.zeros_like(small_ref)
        tiles = width // 128
        for t in range(tiles):
            at = slice(t * 128, (t + 1) * 128)
            for k in range(3):
                small_ref[k * tiles + t:k * tiles + t + 1] = before_ref[k:k + 1, at]
                small_ref[(3 + k) * tiles + t:(3 + k) * tiles + t + 1] = sums_ref[k:k + 1, at]
            for k in range(4):
                small_ref[pl.ds((6 + info_ref[PLACE + k]) * tiles + t, 1), :] = sums_ref[4 + k:5 + k, at]

def ffn_back(info, grad_branch, slopes, grad_second, normal, inverse, vecs, before, w_in, w_down, tile=256):
    rows, width = grad_branch.shape
    hidden = 4 * width
    row = lambda n: pl.BlockSpec((tile, n), lambda i, *_: (i, 0))
    sds = jax.ShapeDtypeStruct
    return pl.pallas_call(
        ffn_back_body,
        grid_spec=pltpu.PrefetchScalarGridSpec(num_scalar_prefetch=1, grid=(rows // tile,), in_specs=[row(width), row(hidden // 2), row(hidden // 2), row(width), row(width), row(128)]
            + [full(a.shape) for a in (vecs, before, *w_in, *w_down)],
        out_specs=[pl.BlockSpec((hidden, tile), lambda i, *_: (0, i)), row(width), row(width), full((64, 128))],
            scratch_shapes=[pltpu.VMEM((8, width), F32)]),
        out_shape=[sds((hidden, rows), BF), sds((rows, width), F32), sds((rows, width), BF), sds((64, 128), F32)],
        compiler_params=params("arbitrary"),
        cost_estimate=cost(18),
        name="ffn_back",
    )(info, grad_branch, *slopes, grad_second, normal, inverse, vecs, before, *w_in, *w_down)

def outer_body(a_ref, other_ref, b_ref, out_ref):
    for k, ref in enumerate((a_ref, other_ref)):
        @pl.when(pl.program_id(0) == k)
        def _(ref=ref):
            out_ref[0] = dot(ref[...], b_ref[...]).astype(out_ref.dtype)

def outer(firsts, kind, a, other, b):
    rows, width = b.shape
    return pl.pallas_call(
        outer_body,
        grid=(2,),
        in_specs=[pl.BlockSpec((width, rows), lambda i: (firsts[0], 0)), pl.BlockSpec((width, rows), lambda i: (firsts[1], 0)), full((rows, width))],
        out_specs=pl.BlockSpec((1, width, width), lambda i: (i, 0, 0)),
        out_shape=kind(2, width, width),
        compiler_params=params("arbitrary"),
        cost_estimate=cost(6),
        name="outer",
    )(a, other, b)

def grad_tokens_body(info_ref, *refs):
    pieces, (one_ref, w_ref, out_ref, sides) = refs[:-4], refs[-4:]
    width = one_ref.shape[1]
    @pl.when(pl.program_id(0) == 0)
    def _():
        for side in range(2):
            for pair in range(3):
                for third in range(3):
                    start = pl.multiple_of(third * width + (info_ref[OWN_CORE + side] * 3 + pair) * 128, 128)
                    at = ((side * 3 + pair) * 3 + third) * 128
                    sides[:, at:at + 128] = w_ref[:, pl.ds(start, 128)]
    wide = jnp.concatenate([r[...] for r in pieces], axis=1)
    out_ref[...] = (one_ref[...] + dot(wide, sides[...], NT)).astype(BF)

def grad_tokens(info, pieces, grad_one, w, tile=256):
    rows, width = grad_one.shape
    row = lambda n: pl.BlockSpec((tile, n), lambda i, *_: (i, 0))
    return pl.pallas_call(
        grad_tokens_body,
        grid_spec=pltpu.PrefetchScalarGridSpec(
            num_scalar_prefetch=1, grid=(rows // tile,),
            in_specs=[row(p.shape[1]) for p in pieces] + [row(width), full(w.shape)],
            out_specs=row(width),
            scratch_shapes=[pltpu.VMEM(w.shape, BF)]),
        out_shape=jax.ShapeDtypeStruct((rows, width), BF),
        compiler_params=params("arbitrary"),
        cost_estimate=cost(9),
        name="grad_tokens",
    )(info, *pieces, grad_one, w)

def wide(ref_value):
    return ref_value.astype(F32)

def place_pairs_body(pairs, out_at, aliased, info_ref, *refs):
    refs = refs[aliased:]
    sides, (out_ref, vector_ref), refs = refs[:2], refs[2:4], refs[4:]
    turned = out_at is not None
    (turned_ref, small_ref), refs = (refs[:2], refs[2:]) if turned else ((None, None), refs)
    columns, extras, sems = refs[:3]
    width = columns.shape[1]
    rows = width // 16
    copies = []
    vector_ref[...] = jnp.zeros_like(vector_ref)
    for p, (pair, firsts, extra_at) in enumerate(pairs):
        for side in range(2):
            for slot in range(16):
                start = pl.multiple_of(info_ref[ORDER_A + slot] * 16, 16)
                extras[side, pl.ds(start, 16), :] = sides[side][slot, extra_at:extra_at + 16, :].astype(F32)
            for third, first in enumerate(firsts):
                which = (p * 2 + side) * 3 + third
                for slot in range(16):
                    start = pl.multiple_of(info_ref[ORDER_A + slot] * rows, rows)
                    columns[which, pl.ds(start, rows), :] = sides[side][slot, first:first + rows, :].astype(F32)
                head = pl.multiple_of((info_ref[OWN_CORE + side] * 3 + pair) * 128, 128)
                copy = pltpu.make_async_copy(columns.at[which], out_ref.at[:, pl.ds(pl.multiple_of(third * width + head, 128), 128)],
                                             sems.at[which])
                copy.start()
                copies.append(copy)
                vector_ref[third:third + 1, pl.ds(head, 128)] = extras[side, 64 + third:65 + third, :]
    if turned:
        acc = refs[3]
        wide = acc.shape[1]
        for side in range(2):
            for slot in range(16):
                start = pl.multiple_of(info_ref[ORDER_A + slot] * rows, rows)
                for t in range(3):
                    at = out_at + t * rows
                    acc[pl.ds(start, rows), t * 128:(t + 1) * 128] = sides[side][slot, at:at + rows, :].astype(F32)
            start = pl.multiple_of(info_ref[OWN_CORE + side] * wide, wide)
            turned_ref[pl.ds(start, wide), :] = acc[...].T
        small_ref[...] = jnp.zeros_like(small_ref)
        for r in range(10):
            for t in range(width // 128):
                at = r * (width // 128) + t
                small_ref[r:r + 1, t * 128:(t + 1) * 128] = extras[0, at:at + 1, :] + extras[1, at:at + 1, :]
    for copy in copies:
        copy.wait()

def place_pairs(pairs, out_at, info, width, own, other, whole=None):
    aliased = int(whole is not None)
    turned = out_at is not None
    count = 6 * len(pairs)
    return pl.pallas_call(
        functools.partial(place_pairs_body, pairs, out_at, aliased),
        grid_spec=pltpu.PrefetchScalarGridSpec(
            num_scalar_prefetch=1, grid=(1,),
            in_specs=[ANYWHERE] * aliased + [full(own.shape), full(other.shape)],
            out_specs=[ANYWHERE, full((8, width))] + [full((width, width)), full((16, width))] * turned,
            scratch_shapes=[pltpu.VMEM((count, width, 128), F32), pltpu.VMEM((2, 256, 128), F32), pltpu.SemaphoreType.DMA((count,))]
            + [pltpu.VMEM((width, width // 2), F32)] * turned),
        out_shape=[f32(width, 3 * width), f32(8, width)] + [f32(width, width), f32(16, width)] * turned,
        input_output_aliases={1: 0} if aliased else {},
        compiler_params=params("arbitrary"),
        cost_estimate=cost(3),
        name="place_pairs",
    )(info, *([whole] if aliased else []), own, other)


AXES = ("dp", "mp")
CORE, ROW, COLUMN, NEAR_DEPTH, FAR_DEPTH = 1, 2, 4, 8, 16
PARTS = ((0, 1), (1, 2))
WEIGHT = [("weight", k) for k in range(3)]
MASKS = [("mask", 0), ("mask", 1)]
OUT = [("out", k) for k in range(3)]
STEPS = ((1, ORDER_B, [*MASKS, *WEIGHT, *OUT, ("extra", 0)]), (2, ORDER_B, [*MASKS, *WEIGHT, ("extra", 0)]),
         (0, ORDER_B, [*MASKS, *WEIGHT, ("extra", 0)]))
SCHEDULE = (
    "send_down", "own_down", (3, "first"), "ffn", 0, (3, "second"), 1, (3, "near_deep"), 2, (0, "near"), (3, "far_deep"),
    (1, "near"), "send_in", (3, "spread_far"), "own_in", (4, "first"), (0, "near_deep"), (2, "near"), (1, "near_deep"),
    (3, "spread_near"), "tokens", (0, "far_deep"), (2, "near_deep"), (1, "far_deep"), (3, "spread_column"), (4, "second"),
    (0, "spread_far"), (2, "far_deep"), (1, "spread_far"), (0, "spread_near"), (3, "whole"), (4, "near_deep"),
    (2, "spread_far"), (0, "gather_column"), (1, "spread_near"), (4, "far_deep"), (2, "spread_near"), (0, "gather_row"),
    (1, "gather_column"), (4, "spread_far"), (2, "gather_column"), (1, "gather_row"), (2, "gather_row"), (4, "spread_near"),
    (0, "gather_core"), (1, "gather_core"), (0, "place"), (4, "spread_column"), (2, "gather_core"), (1, "place"),
    (2, "place"), (4, "whole"),
)


class Order:
    def __init__(self):
        self.last = None

    def hold(self, value):
        return value if self.last is None else lax.optimization_barrier((value, self.last))[0]

    def do(self, step, *operands):
        result = step(*self.hold(operands))
        self.last = jax.tree.leaves(result)[0]
        return result


class Links:
    def __init__(self, dp, mp):
        self.dp, self.mp = dp, mp
        self.direct = dp == 8 and mp == 4
        self.at_dp, self.at_mp = lax.axis_index("dp"), lax.axis_index("mp")
        self.core, self.row, self.column = self.at_mp % 2, self.at_mp // 2, self.at_dp % 2
        self.near_deep, self.far_deep = self.at_dp // 2 % 2, self.at_dp // 4
        slot = jnp.arange(16)
        z, low, high = (((slot >> 1) & 1) << 1) | ((slot & 1) << 2), (slot >> 2) & 1, slot >> 3
        if self.direct:
            def chip(x, y):
                return (self.at_dp ^ (x | z)) * 2 + (self.row ^ y)
            orders = [chip(low, high), chip(high, low)]
        else:
            orders = [slot, slot]
        rest = jnp.stack([self.core, 1 - self.core, *(self.at_mp ^ k for k in range(4)),
                          self.column, self.near_deep, self.far_deep])
        self.info = jnp.concatenate([*orders, rest]).astype(jnp.int32)

    def swap(self, value, bits):
        count = self.dp * self.mp
        return lax.ppermute(value, AXES, [(i, i ^ bits) for i in range(count)])

    def grow(self, value, *axes):
        for bits in axes:
            value = jnp.concatenate([value, self.swap(value, bits)])
        return value


def pick(index, first, second):
    return jnp.where(index == 0, first, second)


def in_order(index, own, other, axis=0):
    return pick(index, jnp.stack([own, other], axis), jnp.stack([other, own], axis))


def at(value, index, axis):
    return lax.dynamic_index_in_dim(value, index, axis, False)


def axes_of(order):
    return (ROW, COLUMN) if order == ORDER_A else (COLUMN, ROW)


def add(*values):
    return sum(v.astype(F32) for v in values)


def any_hidden(links, keep):
    zero = jnp.zeros_like(keep[0])
    blocks = jnp.stack([keep[0], zero, keep[1], zero])
    blocks = jnp.stack([blocks[links.at_mp ^ k] for k in range(4)])
    return lax.psum(lax.psum_scatter(blocks, "mp", scatter_dimension=0, tiled=False), "dp")


class Hidden:
    def __init__(self, links, order, axis):
        self.links, self.order, self.axis = links, order, axis

    def begin(self, keep, came):
        self.shape = keep.shape[1:]
        self.parts = (2, 2, 2, 2, self.shape[0] // 8, self.shape[1])
        self.total, self.came = keep, came

    def first(self):
        column = self.links.column

        def step(keep, came):
            total = add(keep, came).reshape(self.parts)
            if self.axis == ROW:
                return total[1].astype(BF), total[0]
            return at(total, 1 - column, 3).astype(BF), at(total, column, 3)
        away, self.total = self.order.do(step, self.total, self.came)
        self.came = self.links.swap(away, self.axis)

    def second(self):
        column = self.links.column

        def step(total, came):
            total = add(total, came)
            if self.axis == ROW:
                return at(total, 1 - column, 2).astype(BF), at(total, column, 2)
            return total[1].astype(BF), total[0]
        away, self.total = self.order.do(step, self.total, self.came)
        self.came = self.links.swap(away, (ROW | COLUMN) ^ self.axis)

    def halve(self, index, axis, bits):
        def step(total, came):
            total = add(total, came)
            return at(total, 1 - index, axis).astype(BF), at(total, index, axis)
        away, self.total = self.order.do(step, self.total, self.came)
        self.came = self.links.swap(away, bits)

    def near_deep(self):
        self.halve(self.links.near_deep, 1, NEAR_DEPTH)

    def far_deep(self):
        self.halve(self.links.far_deep, 0, FAR_DEPTH)

    def spread_far(self):
        self.total = self.order.do(lambda a, b: add(a, b).astype(BF), self.total, self.came)
        self.came = self.links.swap(self.total, FAR_DEPTH)

    def spread(self, index, axis, bits):
        self.total = self.order.do(lambda a, b: in_order(index, a, b, axis), self.total, self.came)
        self.came = self.links.swap(self.total, bits)

    def spread_near(self):
        self.spread(self.links.far_deep, 0, NEAR_DEPTH)

    def spread_column(self):
        self.spread(self.links.near_deep, 1, COLUMN)

    def whole(self):
        self.result = self.order.do(lambda a, b: in_order(self.links.column, a, b, 2).astype(F32).reshape(self.shape), self.total, self.came)


class Slots:
    def __init__(self, links, order, axes, masks):
        self.links, self.order, self.axes, self.masks = links, order, axes, masks
        self.slots, self.came = [], []

    def far(self, slots):
        self.slots.append(slots)
        self.came.append(self.links.swap(slots[0], self.axes[0]))

    def near(self):
        def step(mids, came):
            return jnp.concatenate([add(m, c[4:]).astype(BF) for m, c in zip(mids, came)], axis=1)
        self.beside = self.links.swap(self.order.do(step, [s[1] for s in self.slots], self.came), self.axes[1])

    def deep(self, which, first, last):
        slots, came, beside = which
        return jnp.concatenate([add(s, c[first:last]) for s, c in zip(slots, came)], axis=1) + beside[first:last].astype(F32)

    def near_deep(self):
        step = lambda *which: self.deep(which, 2, 4).astype(BF)
        sent = self.order.do(step, [s[2] for s in self.slots], self.came, self.beside)
        self.behind = self.links.swap(sent, NEAR_DEPTH)

    def far_deep(self):
        def step(which, behind):
            total = self.deep(which, 0, 2) + behind.astype(F32)
            return total[1].astype(BF), total[0]
        sent, self.total = self.order.do(step, ([s[3] for s in self.slots], self.came, self.beside), self.behind)
        self.came = self.links.swap(sent, FAR_DEPTH)

    def spread_far(self):
        def step(total, came):
            total = total + came.astype(F32)
            row, masks, rest = 0, [], []
            for slots, count in zip(self.slots, self.masks):
                rows = slots[0].shape[1]
                masks.append(total[row:row + count])
                rest.append(total[row + count:row + rows])
                row += rows
            return jnp.concatenate(rest)[None].astype(BF), masks
        self.whole, self.mask_rows = self.order.do(step, self.total, self.came)
        self.came = self.links.swap(self.whole, FAR_DEPTH)

    def spread_near(self):
        self.spread(NEAR_DEPTH)

    def gather_column(self):
        self.spread(COLUMN)

    def gather_row(self):
        self.spread(ROW)

    def gather_core(self):
        self.spread(CORE)

    def spread(self, bits):
        self.whole = self.order.do(lambda a, b: jnp.concatenate([a, b]), self.whole, self.came)
        self.came = self.links.swap(self.whole, bits)


def body(dp, mp, tokens, w_qkv, bias_q, bias_v, w_out, bias_out, norm1_gain, norm1_bias, w_in, bias_in, w_down, bias_down,
         norm2_gain, norm2_bias, mask_logits, mask_noise, grad_out):
    width = w_out.shape[0]
    heads, rows_own, length = mask_logits.shape
    half = heads // 2
    links, order = Links(dp, mp), Order()
    core, info, swap, do = links.core, links.info, links.swap, order.do

    def chances(logits, noise):
        fraction = noise.astype(F32) / 65536.0
        return logits + jnp.log(fraction) - jnp.log(1.0 - fraction)

    def codes(logits, noise):
        logit = chances(logits, noise)
        tail = jax.nn.sigmoid(-jnp.abs(logit)) * MASK_SCALE
        return jnp.where(logit < 0.0, tail, -tail).astype(BF)

    shift = jnp.concatenate([wide(bias_q), jnp.zeros((width,), F32), wide(bias_v)])[None]
    norms = (bias_out, norm1_gain, norm1_bias, bias_down, norm2_gain, norm2_bias)
    pack = lambda *v: jnp.concatenate([wide(x) for x in v] + [jnp.zeros(((8 - len(v)) * width,), F32)]).reshape(8, width)
    mixed, totals, came = [], [], []

    def attention(part, pieces):
        own, other, total = do(lambda q, m: attend(*PARTS[part], info, q, m), qkv, pieces)
        mixed.append((own, other))
        came.append(swap(other, CORE))
        totals.append(total)

    if links.direct:
        plane = (1, rows_own, length)

        def two_sides(logits, noise, bias):
            code = codes(logits, noise)
            row = jnp.pad(bias, (0, rows_own * length - bias.shape[0])).reshape(plane)
            return jnp.concatenate([pick(core, code[half:], code[:half]), row]), pick(core, code[:half], code[half:])
        away, keep = do(two_sides, mask_logits, mask_noise, bias_in)
        beside = swap(away, CORE)
        other_tokens = swap(tokens, CORE)

        parts = half // 2

        def chip_codes(keep, beside):
            chip = in_order(core, keep, beside[:half], 1).reshape(parts, 2, 1, 2 * rows_own, length)
            return [[chip[p:p + n, h] for h in range(2)] for p, n in PARTS], beside[half].reshape(-1)[:bias_in.shape[0]]
        chip, near_bias = do(chip_codes, keep, beside)
        flat = lambda tree: jnp.concatenate([v for part in tree for v in part])
        behind = swap(flat(chip), FAR_DEPTH)
        eighth = w_in.shape[0] // 8
        split = lambda w: w.reshape(4, 2, eighth, width)
        z_at, x_at = links.at_dp // 2, links.column

        def to_row(w_in, w_down, *biases):
            parts = [at(at(split(w), z_at, 0), x_at, 0) for w in (w_in, w_down)]
            return jnp.concatenate([*parts, jnp.pad(jnp.stack(biases), ((0, 14), (0, 0)))])
        piece = swap(do(to_row, w_in, w_down, bias_in, near_bias), ROW)
        qkv = do(lambda *v: project(info, *v), tokens, other_tokens, w_qkv, shift)
        piece = order.hold(piece)
        axes = ((COLUMN, ROW), (ROW, COLUMN))
        groups, seconds, fars = [None] * 2, [None] * 2, [None] * 2

        def deep_parts(chip, behind):
            result, row = [], 0
            for part, (p, n) in zip(chip, PARTS):
                heads = []
                for own in part:
                    heads.append(jnp.concatenate([own, behind[row:row + n]], axis=1))
                    row += n
                result.append(jnp.concatenate(heads))
            return result
        deep = do(deep_parts, chip, behind)
        deep = [(v, swap(v, NEAR_DEPTH)) for v in deep]

        def gather_near(part):
            n = PARTS[part][1]
            groups[part] = do(lambda a, b: [jnp.concatenate([a[h * n:h * n + n], b[h * n:h * n + n]], axis=1) for h in range(2)], *deep[part])
            seconds[part] = [swap(groups[part][h], axes[h][0]) for h in range(2)]

        def gather_far(part):
            both = do(lambda g, s: [jnp.concatenate(v, axis=1) for v in zip(g, s)], groups[part], seconds[part])
            fars[part] = [swap(both[h], axes[h][1]) for h in range(2)]

        behind = swap(piece[:2 * eighth], FAR_DEPTH)
        gather_near(0)
        gather_far(0)
        gather_near(1)
        vecs = do(pack, *norms)
        biases = do(lambda *v: wide(jnp.concatenate(v)).reshape(4, width), bias_in, near_bias, piece[2 * eighth], piece[2 * eighth + 1])
        pair = do(lambda a, b: in_order(links.far_deep, a[:2 * eighth], b), piece, behind)
        behind = swap(pair, NEAR_DEPTH)
        gather_far(1)
        pieces = [[v for h in range(2) for v in (groups[p][h], seconds[p][h], fars[p][h])] for p in range(2)]
        beside = swap(do(lambda *v: jnp.stack(v), w_in, w_down), CORE)
        attention(0, pieces[0])
        beside = order.hold(beside)

        def group_step(own, came, w):
            group = in_order(links.near_deep, own, came, 1)
            return [v.reshape(4, eighth, width) for v in jnp.split(group, 2, axis=2)], at(split(w), 1 - x_at, 1)
        group, straight = do(group_step, pair, behind, w_down)
        around, straight = swap(group[0], COLUMN), swap(straight, ROW)
        near_in, near_down = do(lambda v: [v[0], v[1]], beside)
        attention(1, pieces[1])
        came[0] = order.hold(came[0])
        blocks_in, blocks_down = [w_in, near_in], [w_down, near_down]
    else:
        other_tokens = swap(tokens, CORE)
        qkv = project(info, tokens, other_tokens, w_qkv, shift)
        whole = lax.all_gather(codes(mask_logits, mask_noise), AXES, axis=1, tiled=True)
        own = lax.dynamic_slice_in_dim(whole, core * half, half, 0).reshape(half // 2, 2, 16, length // 16, length)
        own = own.transpose(1, 0, 2, 3, 4)
        pieces = [[own[h, p:p + n, a:b] for h in range(2) for a, b in ((0, 4), (4, 8), (8, 16))] for p, n in PARTS]
        attention(0, pieces[0])
        attention(1, pieces[1])
        vecs = pack(*norms)
        blocks_in, blocks_down, blocks_bias = ([v[links.at_mp ^ k] for k in range(4)]
                                               for v in (lax.all_gather(w, "mp") for w in (w_in, w_down, bias_in)))
        biases = wide(jnp.stack(blocks_bias))
    first_low, active, slope, normal, inverse, branch = do(
        lambda *v: ffn_first(info, *v), tokens, [own for own, _ in mixed] + came, w_out, vecs, biases, blocks_in[:2], blocks_down[:2])
    if links.direct:
        across = do(lambda *v: [in_order(links.column, a, b, 1).reshape(w_in.shape) for a, b in (v[:2], v[2:])],
                    group[0], around, group[1], straight)
        blocks_in += [across[0], swap(across[0], CORE)]
        blocks_down += [across[1], swap(across[1], CORE)]
    out, active_two, slope_two, grad_second, grad_branch, sums = do(
        ffn_second, first_low, branch, grad_out, vecs, biases, blocks_in[2:], blocks_down[2:])
    d_own, d_other, slots = [None] * 3, [None] * 3, [None] * 3
    hidden = [Hidden(links, order, COLUMN), Hidden(links, order, COLUMN)]
    keep, grads, settled = [None] * 2, {}, []

    def send_down():
        grads["sent_down"] = swap(do(functools.partial(outer, (1, 1), bf), active, active_two, grad_branch), CORE)

    def own_down():
        keep[0] = do(functools.partial(outer, (0, 0), f32), active, active_two, grad_branch)
        hidden[0].begin(keep[0], grads["sent_down"])

    def ffn_gradient():
        grads["pre"], grads["one"], grads["attn"], grads["small"] = do(
            lambda *v: ffn_back(info, *v), grad_branch, [slope, slope_two], grad_second, normal, inverse, vecs, sums, blocks_in, blocks_down)
        grads["pair"] = grads["attn"], swap(grads["attn"], CORE)

    def settle():
        for pair in range(3):
            if d_other[pair] is not None and pair not in settled:
                settled.append(pair)
                d_other[pair] = order.hold(d_other[pair])

    def send_in():
        sent = do(functools.partial(outer, (1, 3), bf), grads["pre"], grads["pre"], first_low)
        settle()
        grads["sent_in"] = swap(sent, CORE)

    def own_in():
        keep[1] = do(functools.partial(outer, (0, 2), f32), grads["pre"], grads["pre"], first_low)
        hidden[1].begin(keep[1], grads["sent_in"])

    def back(step):
        pair, place, segments = STEPS[step]
        part = min(pair, 1)
        local = pair - PARTS[part][0]
        own, other, *outs = do(
            lambda *v: attend_back(pair, local, [(place, segments)], info, *v), qkv, mixed[part], grads["pair"], w_out,
            totals[part], (tokens, other_tokens), pieces[part], () if step else mixed, grads["small"])
        settle()
        slots[step] = outs
        if links.direct:
            chains[step].far(outs)
        d_own[pair] = own
        d_other[pair] = swap(other, CORE)

    def grad_input():
        grads["tokens"] = do(lambda *v: grad_tokens(info, *v), [*d_own, *d_other], grads["one"], w_qkv)

    def place(steps, own, other):
        pairs, row = [], 0
        for step in steps:
            pair, _, segments = STEPS[step]
            found = {}
            for kind, k in segments:
                if kind != "mask":
                    found[kind, k] = row
                    row += segment_rows(kind, length, width)
            pairs.append((pair, [found["weight", k] for k in range(3)], found["extra", 0]))
        out_at = found.get(("out", 0))
        whole = [] if result[0] is None else [result[0]]
        result[0], vector, *extras = do(lambda a, b, *w: place_pairs(pairs, out_at, info, width, a, b, *w), own, other, *whole)
        vectors.append(vector)
        if extras:
            result[1:] = extras

    result, vectors = [None] * 3, []
    masks = [sum(kind == "mask" for kind, _ in segments) * length // 4 for _, _, segments in STEPS]
    chains = [Slots(links, order, axes_of(place), [count]) for (_, place, _), count in zip(STEPS, masks)]
    kernels = {"send_down": send_down, "own_down": own_down, "ffn": ffn_gradient, "send_in": send_in, "own_in": own_in, "tokens": grad_input}
    for step in range(3):
        kernels[step] = functools.partial(back, step)
    mask_rows = [None] * 3
    for name in SCHEDULE:
        if name in kernels:
            kernels[name]()
        elif links.direct:
            who, what = name
            chain = (*chains, *hidden)[who]
            if what == "place":
                place((who,), chain.whole, chain.came)
            else:
                getattr(chain, what)()
    if links.direct:
        grad_w_down, grad_w_in = (chain.result for chain in hidden)
        mask_rows = [chain.mask_rows[0].reshape(2, 4, length // 16, 128) for chain in chains]
    else:
        grad_w_down, grad_w_in = (any_hidden(links, k + wide(grads[s])) for k, s in zip(keep, ("sent_down", "sent_in")))
        for step, (s, count) in enumerate(zip(slots, masks)):
            own = wide(jnp.concatenate(s[::-1]))
            both = lax.psum(in_order(core, own, jnp.zeros_like(own)), AXES)
            sides = [both[core], both[1 - core]]
            place((step,), *(v[:, count:].astype(BF) for v in sides))
            mask_rows[step] = jnp.stack([v[:, :count].reshape(16, 2, 4, length // 16, 128).transpose(1, 2, 0, 3, 4) for v in sides])
    grad_w_qkv, grad_w_out, small = result
    bias = sum(vectors)
    by_pair = [None] * 3
    for (pair, _, _), rows in zip(STEPS, mask_rows):
        by_pair[pair] = rows
    if links.direct:
        mask_sum = jnp.stack(by_pair).transpose(0, 1, 3, 2, 4).reshape(half, 2 * rows_own, length)
        mine = pick(core, mask_sum[:, :rows_own], mask_sum[:, rows_own:])
        theirs = swap(pick(core, mask_sum[:, rows_own:], mask_sum[:, :rows_own]), CORE)
    else:
        mine, theirs = jnp.stack(by_pair, axis=1).transpose(0, 1, 2, 4, 5, 3, 6).reshape(2, half, length, length)
        place = (links.at_dp * mp + links.at_mp) * rows_own
        mine, theirs = (lax.dynamic_slice_in_dim(m, place, rows_own, 1) for m in (mine, theirs))
    mask_sum = pick(core, jnp.concatenate([mine, theirs]), jnp.concatenate([theirs, mine]))
    mask_own = jax.nn.sigmoid(chances(mask_logits, mask_noise))
    grad_mask_logits = mask_sum * (MASK_SCALE * mask_own * (1.0 - mask_own))
    return (out, grads["tokens"], grad_w_qkv, bias[0], bias[2], grad_w_out, small[5], small[3], small[4], grad_w_in, small[6 + links.at_mp],
            grad_w_down, small[2], small[0], small[1], grad_mask_logits)


def solution(mesh):
    both, none = ("dp", "mp"), P()
    rows, mask, split = P(both, None), P(None, both, None), P("mp", None)
    ins = (rows, none, none, none, none, none, none, none, split, P("mp"), split, none, none, none, mask, mask, rows)
    outs = (rows, rows, none, none, none, none, none, none, none, split, P("mp"), split, none, none, none, mask)
    step = functools.partial(body, mesh.shape["dp"], mesh.shape["mp"])
    return jax.shard_map(step, mesh=mesh, in_specs=ins, out_specs=outs, check_vma=False)
```

```python
import functools

import jax
import jax.numpy as jnp
from jax import lax
from jax.experimental import pallas as pl
from jax.experimental.pallas import tpu as pltpu
from jax.sharding import PartitionSpec as P

MASK_SCALE = 4.0

BF = jnp.bfloat16
F32 = jnp.float32
NT = (((1,), (1,)), ((), ()))
NN = (((1,), (0,)), ((), ()))
TN = (((0,), (0,)), ((), ()))
VMEM_LIMIT = 56 * 1024 * 1024
SIZES = (8, 4, 2, 2)

ORDER_A, ORDER_B, OWN_CORE, OTHER_CORE, PLACE, COLUMN_AT, NEAR_AT, FAR_AT = 0, 16, 32, 33, 34, 38, 39, 40

COST = 0.001

def cost(us):
    return pl.CostEstimate(flops=int(us * 1.0e9 * COST), transcendentals=0, bytes_accessed=int(us * 2.0e6 * COST))

def dot(a, b, dims=NN):
    return lax.dot_general(a, b, dims, preferred_element_type=F32)

def bf(*shape):
    return jax.ShapeDtypeStruct(shape, BF)

def f32(*shape):
    return jax.ShapeDtypeStruct(shape, F32)

def identity(n):
    return (lax.broadcasted_iota(jnp.int32, (n, n), 0) == lax.broadcasted_iota(jnp.int32, (n, n), 1)).astype(F32).astype(BF)

def params(*sem):
    return pltpu.CompilerParams(dimension_semantics=sem or None, vmem_limit_bytes=VMEM_LIMIT)

def place_mask(order_ref, pieces, codes, bias, eye):
    rows = codes.shape[0] // 16
    for head in range(2):
        slot = 0
        for group in pieces[head * 3:head * 3 + 3]:
            for j in range(group.shape[1]):
                start = pl.multiple_of(order_ref[head * 16 + slot] * rows, rows)
                codes[pl.ds(start, rows), :] = group[0, j]
                slot += 1
        turned = dot(eye, codes[...], NT)
        bias[head] = jnp.where(turned > 0.0, turned - 4.0, turned)

def halves(seqs, length, lane):
    half = seqs // 2
    return [pl.BlockSpec((length, lane), lambda i, s, *_: (jnp.minimum(s, half - 1), i)),
            pl.BlockSpec((length, lane), lambda i, s, *_: (jnp.maximum(s - half, 0), i))]

def mask_specs(pieces):
    return [pl.BlockSpec((1, *p.shape[1:]), lambda i, s, *_: (i, 0, 0, 0)) for p in pieces]

def qkv_specs(first, length):
    def part(which):
        return pl.BlockSpec((1, length, 128), lambda i, s, *_: (which, s, first + i))
    return [part(0), part(1), part(2)]

def split_heads(value, first):
    zero = jnp.zeros_like(value)
    return jnp.concatenate([jnp.where(first, value, zero), jnp.where(first, zero, value)])

def attend_body(order_ref, q_ref, k_ref, v_ref, *refs):
    pieces, (own_ref, other_ref, total_ref), (codes, bias) = refs[:6], refs[6:9], refs[9:]
    length = codes.shape[0]
    step, count = pl.program_id(1), pl.num_programs(1)
    @pl.when(step == 0)
    def _():
        place_mask(order_ref, pieces, codes, bias, identity(length))
    half = q_ref.shape[2] // 2
    lanes = lax.broadcasted_iota(jnp.int32, (1, 2 * half), 1)
    query, keys = q_ref[0], k_ref[0]
    values_t = v_ref[0].T
    outs = []
    both = dot(split_heads(keys, lanes < half), query, NT)
    for head in range(2):
        scores = both[head * length:(head + 1) * length] + bias[head]
        highest = jnp.max(scores, axis=0, keepdims=True)
        powers = jnp.exp(scores - highest)
        summed = jnp.sum(powers, axis=0, keepdims=True)
        probs = (powers * (1.0 / summed)).astype(BF)
        outs.append(dot(values_t[head * half:(head + 1) * half], probs))
        total_ref[0, 0, head:head + 1, :] = highest + jnp.log(summed)
    mixed = jnp.concatenate(outs, axis=0).T.astype(BF)
    @pl.when(step < count // 2)
    def _():
        own_ref[...] = mixed
    @pl.when(step >= count // 2)
    def _():
        other_ref[...] = mixed

def attend(first, count, order, qkv, pieces):
    _, tokens, width = qkv.shape
    length = pieces[0].shape[3]
    seqs = tokens // length
    sds = jax.ShapeDtypeStruct
    return pl.pallas_call(
        attend_body,
        grid_spec=pltpu.PrefetchScalarGridSpec(
            num_scalar_prefetch=1, grid=(count, seqs),
            in_specs=qkv_specs(first, length) + mask_specs(pieces),
            out_specs=[*halves(seqs, length, 128), pl.BlockSpec((1, 1, 8, length), lambda i, s, *_: (i, s, 0, 0))],
            scratch_shapes=[pltpu.VMEM((length, length), BF), pltpu.VMEM((2, length, length), F32)],
        ),
        out_shape=[sds((tokens // 2, count * 128), BF)] * 2 + [sds((count, seqs, 8, length), F32)],
        compiler_params=params("arbitrary", "arbitrary"),
        cost_estimate=cost(9 * count),
        name="attend",
    )(order, qkv, qkv, qkv, *pieces)

def attend_back_body(groups, has_out, info_ref, *refs):
    (q_ref, k_ref, v_ref, mixed_own, mixed_other, ga_own, ga_other, wout_ref, total_ref, tok_own, tok_other), refs = refs[:11], refs[11:]
    pieces, refs = refs[:6], refs[6:]
    all_own, all_other, small_ref = (), (), None
    if has_out:
        all_own, all_other, small_ref, refs = refs[:has_out], refs[has_out:2 * has_out], refs[2 * has_out], refs[2 * has_out + 1:]
    own_ref, other_ref, refs = refs[0], refs[1], refs[2:]
    outs, refs = refs[:4 * len(groups)], refs[4 * len(groups):]
    codes, bias, acc, weight, extra = refs[:5]
    weight_out = refs[5] if has_out else None
    length = codes.shape[0]
    step, steps = pl.program_id(0), pl.num_programs(0)
    @pl.when(step == 0)
    def _():
        place_mask(info_ref, pieces, codes, bias, identity(length))
        acc[...] = jnp.zeros_like(acc)
        weight[...] = jnp.zeros_like(weight)
        extra[...] = jnp.zeros_like(extra)
        if has_out:
            extra[0:small_ref.shape[0], :] = small_ref[...]
            weight_out[...] = jnp.zeros_like(weight_out)
    half = q_ref.shape[2] // 2
    lanes = lax.broadcasted_iota(jnp.int32, (1, 2 * half), 1)
    query, keys, values = q_ref[0], k_ref[0], v_ref[0]
    keys_t = keys.T
    is_own = step < steps // 2
    grad_attn = jnp.where(is_own, ga_own[...], ga_other[...])
    grad = dot(grad_attn, wout_ref[...], NT).astype(BF)
    mixed = jnp.where(is_own, mixed_own[...], mixed_other[...])
    inner = (grad.astype(F32) * mixed.astype(F32)).T
    first = lanes < half
    scores_both = dot(split_heads(keys, first), query, NT)
    grads_both = dot(split_heads(values, first), grad, NT)
    dq, lows, rounded = [], [], []
    for head in range(2):
        at = slice(head * length, (head + 1) * length)
        probs = jnp.exp(scores_both[at] + bias[head] - total_ref[0, 0, head:head + 1, :])
        delta = jnp.sum(inner[head * half:(head + 1) * half], axis=0, keepdims=True)
        grad_scores = probs * (grads_both[at] - delta)
        acc[head] += grad_scores
        lows.append(grad_scores.astype(BF))
        rounded.append(probs.astype(BF))
        dq.append(dot(keys_t[head * half:(head + 1) * half], lows[head]))
    dv = dot(jnp.concatenate(rounded), grad)
    dk = dot(jnp.concatenate(lows), query)
    dv, dk = (jnp.split(v, 2) for v in (dv, dk))
    result = jnp.concatenate([(jnp.concatenate(dq, axis=0).T * 0.125).astype(BF),
                              jnp.where(first, dk[0], dk[1]).astype(BF),
                              jnp.where(first, dv[0], dv[1]).astype(BF)], axis=1)
    @pl.when(is_own)
    def _():
        own_ref[...] = result
    @pl.when(jnp.logical_not(is_own))
    def _():
        other_ref[...] = result
    weight[...] += dot(jnp.where(is_own, tok_own[...], tok_other[...]), result, TN)
    sums = jnp.sum(result.astype(F32), axis=0, keepdims=True)
    for third in range(3):
        extra[64 + third:65 + third, :] += sums[:, third * 128:(third + 1) * 128]
    if has_out:
        whole = jnp.where(is_own, jnp.concatenate([m[...] for m in all_own], axis=1),
                          jnp.concatenate([m[...] for m in all_other], axis=1))
        weight_out[...] += dot(grad_attn, whole, TN)
    rows, wrows = length // 16, weight.shape[0] // 16
    @pl.when(step == steps - 1)
    def _():
        eye = identity(length)
        for head in range(2):
            acc[head] = dot(eye, acc[head].astype(BF), NT)
        for g, (order, segments) in enumerate(groups):
            at = 16
            for out in outs[4 * g:4 * g + 4]:
                at -= out.shape[0]
                for j in range(out.shape[0]):
                    place = info_ref[order + at + j]
                    row = 0
                    for kind, k in segments:
                        if kind == "mask":
                            value = acc[k, pl.ds(pl.multiple_of(place * rows, rows), rows), :].astype(BF)
                            for t in range(length // 128):
                                out[j, row:row + rows, :] = value[:, t * 128:(t + 1) * 128]
                                row += rows
                        elif kind == "extra":
                            out[j, row:row + 16, :] = extra[pl.ds(pl.multiple_of(place * 16, 16), 16), :].astype(BF)
                            row += 16
                        else:
                            source = weight if kind == "weight" else weight_out
                            value = source[pl.ds(pl.multiple_of(place * wrows, wrows), wrows), k * 128:(k + 1) * 128]
                            out[j, row:row + wrows, :] = value.astype(BF)
                            row += wrows

def segment_rows(kind, length, width):
    return {"mask": length // 4, "extra": 16}.get(kind, width // 16)

def attend_back(pair, local, groups, info, qkv, mixed, grad_attn, w_out, total, tokens, pieces, all_mixed=(), small=None):
    _, seqs, _, length = total.shape
    rows_all, width = 2 * tokens[0].shape[0], tokens[0].shape[1]
    half = seqs // 2
    def split(wide, at=0):
        return [pl.BlockSpec((length, wide), lambda s, *_: (jnp.minimum(s, half - 1), at)),
                pl.BlockSpec((length, wide), lambda s, *_: (jnp.maximum(s - half, 0), at))]
    def part(which):
        return pl.BlockSpec((1, length, 128), lambda s, *_: (which, s, pair))
    masks = [pl.BlockSpec((1, *p.shape[1:]), lambda s, *_: (local, 0, 0, 0)) for p in pieces]
    extras, extra_specs = [], []
    scratch = [pltpu.VMEM((length, length), BF), pltpu.VMEM((2, length, length), F32), pltpu.VMEM((2, length, length), F32),
               pltpu.VMEM((width, 384), F32), pltpu.VMEM((256, 128), F32)]
    if all_mixed:
        extras = [m[0] for m in all_mixed] + [m[1] for m in all_mixed] + [small]
        extra_specs = [split(m.shape[1])[k // len(all_mixed)] for k, m in enumerate(extras[:-1])] + [full(small.shape)]
        scratch.append(pltpu.VMEM((width, width // 2), F32))
    sds = jax.ShapeDtypeStruct
    shapes = [(n, sum(segment_rows(kind, length, width) for kind, _ in segments), 128) for _, segments in groups for n in SIZES]
    return pl.pallas_call(
        functools.partial(attend_back_body, groups, len(all_mixed)),
        grid_spec=pltpu.PrefetchScalarGridSpec(
            num_scalar_prefetch=1, grid=(seqs,),
            in_specs=[part(0), part(1), part(2), *split(128, local), *split(width),
                      pl.BlockSpec((128, width), lambda s, info: (info[OWN_CORE] * 3 + pair, 0)),
                      pl.BlockSpec((1, 1, 8, length), lambda s, *_: (local, s, 0, 0)), *split(width), *masks, *extra_specs],
            out_specs=split(384) + [full(x) for x in shapes],
            scratch_shapes=scratch,
        ),
        out_shape=[sds((rows_all // 2, 384), BF)] * 2 + [sds(x, BF) for x in shapes],
        compiler_params=params("arbitrary"),
        cost_estimate=cost(18 + 3 * bool(all_mixed)),
        name="attend_back",
    )(info, qkv, qkv, qkv, *mixed, *grad_attn, w_out, total, *tokens, *pieces, *extras)

def full(shape):
    return pl.BlockSpec(shape, lambda *_: (0,) * len(shape))

def project_body(info_ref, own_ref, other_ref, w_ref, shift_ref, out_ref):
    third = pl.program_id(0)
    scale = jnp.where(third == 0, 0.125, 1.0)
    rows = own_ref.shape[0]
    for i, ref in enumerate((own_ref, other_ref)):
        value = (dot(ref[...], w_ref[...]) + shift_ref[...]).astype(BF)
        out_ref[0, i * rows:(i + 1) * rows] = (value.astype(F32) * scale).astype(BF)

def project(info, own_tokens, other_tokens, w_qkv, shift):
    rows, width = own_tokens.shape
    own = width // 2
    return pl.pallas_call(
        project_body,
        grid_spec=pltpu.PrefetchScalarGridSpec(
            num_scalar_prefetch=1, grid=(3,),
            in_specs=[full((rows, width)), full((rows, width)),
                      pl.BlockSpec((width, own), lambda t, info: (0, 2 * t + info[OWN_CORE])),
                      pl.BlockSpec((1, own), lambda t, info: (0, 2 * t + info[OWN_CORE]))],
            out_specs=pl.BlockSpec((1, 2 * rows, own), lambda t, c: (t, 0, 0)),
        ),
        out_shape=jax.ShapeDtypeStruct((3, 2 * rows, own), BF),
        compiler_params=params("arbitrary"),
        cost_estimate=cost(8),
        name="project",
    )(info, own_tokens, other_tokens, w_qkv, shift)

def erf_parts(u):
    d = 1.0 + 0.23164189 * jnp.abs(u)
    t = pl.reciprocal(d, approx=True)
    t = t * (2.0 - d * t)
    e = jnp.exp2((-0.7213475204444817 * u) * u)
    poly = t * (0.127414796 + t * (-0.142248368 + t * (0.7107068705 + t * (-0.7265760135 + t * 0.5307027145))))
    tail = poly * e
    return jnp.where(u < 0.0, tail, 1.0 - tail), e * 0.3989422804014327

def row_mean(v):
    return jnp.mean(v, axis=-1, keepdims=True)

def column_sum(v):
    return jnp.sum(v, axis=0, keepdims=True)

def norm_parts(value):
    centered = value - row_mean(value)
    inverse = lax.rsqrt(row_mean(centered * centered) + 1e-12)
    return centered * inverse, inverse

def norm_back(inner, normal, inverse):
    return inverse * (inner - row_mean(inner) - normal * row_mean(inner * normal))

ANYWHERE = pl.BlockSpec(memory_space=pl.ANY)

def hidden_blocks(first, low, branch, bin_ref, w_in, w_down, active_ref, slope_ref):
    width = low.shape[1]
    pre = dot(low, w_in[0][...], NT)
    for b in range(len(w_in)):
        ahead = dot(low, w_in[b + 1][...], NT) if b + 1 < len(w_in) else None
        strips = []
        for r in range(0, pre.shape[0], 64):
            parts = []
            for c in range(0, width, 256):
                u = pre[r:r + 64, c:c + 256] + bin_ref[first + b:first + b + 1, c:c + 256]
                cum, dens = erf_parts(u)
                parts.append((u * cum).astype(BF))
                slope_ref[r:r + 64, b * width + c:b * width + c + 256] = (cum + u * dens).astype(slope_ref.dtype)
            strips.append(jnp.concatenate(parts, axis=1))
        act = jnp.concatenate(strips, axis=0)
        active_ref[b * width:(b + 1) * width, :] = act.T
        branch += dot(act, w_down[b][...])
        pre = ahead
    return branch

def ffn_first_body(info_ref, tok_ref, *refs):
    count = len(refs) - 13
    mixed, (wout_ref, vec_ref, bin_ref), refs = refs[:count], refs[count:3 + count], refs[3 + count:]
    w_in, w_down, (low_ref, active_ref, slope_ref, norm_ref, inv_ref, branch_ref) = refs[:2], refs[2:4], refs[4:]
    bias_out, gain1, shift1, bias_down = (vec_ref[i:i + 1] for i in range(4))
    value = tok_ref[...].astype(F32) + bias_out
    half = wout_ref.shape[0] // 2
    for side in range(2):
        part = jnp.concatenate([m[...] for m in mixed[side * count // 2:(side + 1) * count // 2]], axis=1)
        start = pl.multiple_of(info_ref[OWN_CORE + side] * half, half)
        value += dot(part, wout_ref[pl.ds(start, half), :])
    normal, inverse = norm_parts(value)
    norm_ref[...] = normal
    inv_ref[...] = jnp.broadcast_to(inverse, inv_ref.shape)
    first = normal * gain1 + shift1
    low = first.astype(BF)
    low_ref[...] = low
    branch_ref[...] = hidden_blocks(0, low, first + bias_down, bin_ref, w_in, w_down, active_ref, slope_ref)

def ffn_second_body(low_ref, branch_ref, gout_ref, vec_ref, bin_ref, *refs):
    w_in, w_down, (out_ref, active_ref, slope_ref, gsec_ref, gbr_ref, sums_ref) = refs[:2], refs[2:4], refs[4:]
    gain2, shift2 = vec_ref[4:5], vec_ref[5:6]
    branch = hidden_blocks(2, low_ref[...], branch_ref[...], bin_ref, w_in, w_down, active_ref, slope_ref)
    normal, inverse = norm_parts(branch)
    out_ref[...] = (normal * gain2 + shift2).astype(BF)
    grad = gout_ref[...].astype(F32)
    back = norm_back(grad * gain2, normal, inverse)
    gsec_ref[...] = back
    gbr_ref[...] = back.astype(BF)
    @pl.when(pl.program_id(0) == 0)
    def _():
        sums_ref[...] = jnp.zeros_like(sums_ref)
    sums_ref[0:1] += column_sum(grad * normal)
    sums_ref[1:2] += column_sum(grad)
    sums_ref[2:3] += column_sum(back)

def ffn_first(info, tokens, mixed, w_out, vecs, b_in, w_in, w_down, tile=256):
    rows, width = tokens.shape
    hidden = 2 * width
    row = lambda n: pl.BlockSpec((tile, n), lambda i, *_: (i, 0))
    return pl.pallas_call(
        ffn_first_body,
        grid_spec=pltpu.PrefetchScalarGridSpec(
            num_scalar_prefetch=1, grid=(rows // tile,),
            in_specs=[row(width)] + [row(m.shape[1]) for m in mixed] + [full(a.shape) for a in (w_out, vecs, b_in, *w_in, *w_down)],
            out_specs=[row(width), pl.BlockSpec((hidden, tile), lambda i, *_: (0, i)), row(hidden), row(width), row(128), row(width)]),
        out_shape=[bf(rows, width), bf(hidden, rows), bf(rows, hidden), f32(rows, width), f32(rows, 128), f32(rows, width)],
        compiler_params=params("arbitrary"),
        cost_estimate=cost(17),
        name="ffn_first",
    )(info, tokens, *mixed, w_out, vecs, b_in, *w_in, *w_down)

def ffn_second(low, branch, grad_out, vecs, b_in, w_in, w_down, tile=256):
    rows, width = low.shape
    hidden = 2 * width
    row = lambda n: pl.BlockSpec((tile, n), lambda i: (i, 0))
    return pl.pallas_call(
        ffn_second_body,
        grid=(rows // tile,),
        in_specs=[row(width)] * 3 + [full(a.shape) for a in (vecs, b_in, *w_in, *w_down)],
        out_specs=[row(width), pl.BlockSpec((hidden, tile), lambda i: (0, i)), row(hidden), row(width), row(width), full((8, width))],
        out_shape=[bf(rows, width), bf(hidden, rows), bf(rows, hidden), f32(rows, width), bf(rows, width), f32(8, width)],
        compiler_params=params("arbitrary"),
        cost_estimate=cost(17),
        name="ffn_second",
    )(low, branch, grad_out, vecs, b_in, *w_in, *w_down)

def ffn_back_body(info_ref, *refs):
    gbr_ref, *slopes, gsec_ref, norm_ref, inv_ref, vec_ref, before_ref = refs[:8]
    w_in, w_down = refs[8:12], refs[12:16]
    gpre_ref, gone_ref, gattn_ref, small_ref, sums_ref = refs[16:]
    gain1 = vec_ref[1:2]
    @pl.when(pl.program_id(0) == 0)
    def _():
        sums_ref[...] = jnp.zeros_like(sums_ref)
    total = lambda v: jnp.sum(v, axis=0, keepdims=True)
    width = gbr_ref.shape[1]
    grad = gsec_ref[...]
    low = gbr_ref[...]
    for b in range(4):
        at = slice(b * width, (b + 1) * width)
        slope = slopes[b // 2][:, b % 2 * width:(b % 2 + 1) * width]
        gpre = (dot(low, w_down[b][...], NT) * slope.astype(F32)).astype(BF)
        gpre_ref[at, :] = gpre.T
        sums_ref[4 + b:5 + b] += total(gpre.astype(F32))
        grad += dot(gpre, w_in[b][...])
    normal, inverse = norm_ref[...], inv_ref[:, 0:1]
    inner = grad * gain1
    back = inverse * (inner - row_mean(inner) - normal * row_mean(inner * normal))
    gone_ref[...] = back
    gattn_ref[...] = back.astype(BF)
    sums_ref[0:1] += total(grad * normal)
    sums_ref[1:2] += total(grad)
    sums_ref[2:3] += total(back)
    @pl.when(pl.program_id(0) == pl.num_programs(0) - 1)
    def _():
        small_ref[...] = jnp.zeros_like(small_ref)
        tiles = width // 128
        for t in range(tiles):
            at = slice(t * 128, (t + 1) * 128)
            for k in range(3):
                small_ref[k * tiles + t:k * tiles + t + 1] = before_ref[k:k + 1, at]
                small_ref[(3 + k) * tiles + t:(3 + k) * tiles + t + 1] = sums_ref[k:k + 1, at]
            for k in range(4):
                small_ref[pl.ds((6 + info_ref[PLACE + k]) * tiles + t, 1), :] = sums_ref[4 + k:5 + k, at]

def ffn_back(info, grad_branch, slopes, grad_second, normal, inverse, vecs, before, w_in, w_down, tile=256):
    rows, width = grad_branch.shape
    hidden = 4 * width
    row = lambda n: pl.BlockSpec((tile, n), lambda i, *_: (i, 0))
    sds = jax.ShapeDtypeStruct
    return pl.pallas_call(
        ffn_back_body,
        grid_spec=pltpu.PrefetchScalarGridSpec(num_scalar_prefetch=1, grid=(rows // tile,), in_specs=[row(width), row(hidden // 2), row(hidden // 2), row(width), row(width), row(128)]
            + [full(a.shape) for a in (vecs, before, *w_in, *w_down)],
        out_specs=[pl.BlockSpec((hidden, tile), lambda i, *_: (0, i)), row(width), row(width), full((64, 128))],
            scratch_shapes=[pltpu.VMEM((8, width), F32)]),
        out_shape=[sds((hidden, rows), BF), sds((rows, width), F32), sds((rows, width), BF), sds((64, 128), F32)],
        compiler_params=params("arbitrary"),
        cost_estimate=cost(18),
        name="ffn_back",
    )(info, grad_branch, *slopes, grad_second, normal, inverse, vecs, before, *w_in, *w_down)

def outer_body(a_ref, other_ref, b_ref, out_ref):
    for k, ref in enumerate((a_ref, other_ref)):
        @pl.when(pl.program_id(0) == k)
        def _(ref=ref):
            out_ref[0] = dot(ref[...], b_ref[...]).astype(out_ref.dtype)

def outer(firsts, kind, a, other, b):
    rows, width = b.shape
    return pl.pallas_call(
        outer_body,
        grid=(2,),
        in_specs=[pl.BlockSpec((width, rows), lambda i: (firsts[0], 0)), pl.BlockSpec((width, rows), lambda i: (firsts[1], 0)), full((rows, width))],
        out_specs=pl.BlockSpec((1, width, width), lambda i: (i, 0, 0)),
        out_shape=kind(2, width, width),
        compiler_params=params("arbitrary"),
        cost_estimate=cost(6),
        name="outer",
    )(a, other, b)

def grad_tokens_body(info_ref, *refs):
    pieces, (one_ref, w_ref, out_ref, sides) = refs[:-4], refs[-4:]
    width = one_ref.shape[1]
    @pl.when(pl.program_id(0) == 0)
    def _():
        for side in range(2):
            for pair in range(3):
                for third in range(3):
                    start = pl.multiple_of(third * width + (info_ref[OWN_CORE + side] * 3 + pair) * 128, 128)
                    at = ((side * 3 + pair) * 3 + third) * 128
                    sides[:, at:at + 128] = w_ref[:, pl.ds(start, 128)]
    wide = jnp.concatenate([r[...] for r in pieces], axis=1)
    out_ref[...] = (one_ref[...] + dot(wide, sides[...], NT)).astype(BF)

def grad_tokens(info, pieces, grad_one, w, tile=256):
    rows, width = grad_one.shape
    row = lambda n: pl.BlockSpec((tile, n), lambda i, *_: (i, 0))
    return pl.pallas_call(
        grad_tokens_body,
        grid_spec=pltpu.PrefetchScalarGridSpec(
            num_scalar_prefetch=1, grid=(rows // tile,),
            in_specs=[row(p.shape[1]) for p in pieces] + [row(width), full(w.shape)],
            out_specs=row(width),
            scratch_shapes=[pltpu.VMEM(w.shape, BF)]),
        out_shape=jax.ShapeDtypeStruct((rows, width), BF),
        compiler_params=params("arbitrary"),
        cost_estimate=cost(9),
        name="grad_tokens",
    )(info, *pieces, grad_one, w)

def wide(ref_value):
    return ref_value.astype(F32)

def place_pairs_body(pairs, out_at, aliased, info_ref, *refs):
    refs = refs[aliased:]
    sides, (out_ref, vector_ref), refs = refs[:2], refs[2:4], refs[4:]
    turned = out_at is not None
    (turned_ref, small_ref), refs = (refs[:2], refs[2:]) if turned else ((None, None), refs)
    columns, extras, sems = refs[:3]
    width = columns.shape[1]
    rows = width // 16
    copies = []
    vector_ref[...] = jnp.zeros_like(vector_ref)
    for p, (pair, firsts, extra_at) in enumerate(pairs):
        for side in range(2):
            for slot in range(16):
                start = pl.multiple_of(info_ref[ORDER_A + slot] * 16, 16)
                extras[side, pl.ds(start, 16), :] = sides[side][slot, extra_at:extra_at + 16, :].astype(F32)
            for third, first in enumerate(firsts):
                which = (p * 2 + side) * 3 + third
                for slot in range(16):
                    start = pl.multiple_of(info_ref[ORDER_A + slot] * rows, rows)
                    columns[which, pl.ds(start, rows), :] = sides[side][slot, first:first + rows, :].astype(F32)
                head = pl.multiple_of((info_ref[OWN_CORE + side] * 3 + pair) * 128, 128)
                copy = pltpu.make_async_copy(columns.at[which], out_ref.at[:, pl.ds(pl.multiple_of(third * width + head, 128), 128)],
                                             sems.at[which])
                copy.start()
                copies.append(copy)
                vector_ref[third:third + 1, pl.ds(head, 128)] = extras[side, 64 + third:65 + third, :]
    if turned:
        acc = refs[3]
        wide = acc.shape[1]
        for side in range(2):
            for slot in range(16):
                start = pl.multiple_of(info_ref[ORDER_A + slot] * rows, rows)
                for t in range(3):
                    at = out_at + t * rows
                    acc[pl.ds(start, rows), t * 128:(t + 1) * 128] = sides[side][slot, at:at + rows, :].astype(F32)
            start = pl.multiple_of(info_ref[OWN_CORE + side] * wide, wide)
            turned_ref[pl.ds(start, wide), :] = acc[...].T
        small_ref[...] = jnp.zeros_like(small_ref)
        for r in range(10):
            for t in range(width // 128):
                at = r * (width // 128) + t
                small_ref[r:r + 1, t * 128:(t + 1) * 128] = extras[0, at:at + 1, :] + extras[1, at:at + 1, :]
    for copy in copies:
        copy.wait()

def place_pairs(pairs, out_at, info, width, own, other, whole=None):
    aliased = int(whole is not None)
    turned = out_at is not None
    count = 6 * len(pairs)
    return pl.pallas_call(
        functools.partial(place_pairs_body, pairs, out_at, aliased),
        grid_spec=pltpu.PrefetchScalarGridSpec(
            num_scalar_prefetch=1, grid=(1,),
            in_specs=[ANYWHERE] * aliased + [full(own.shape), full(other.shape)],
            out_specs=[ANYWHERE, full((8, width))] + [full((width, width)), full((16, width))] * turned,
            scratch_shapes=[pltpu.VMEM((count, width, 128), F32), pltpu.VMEM((2, 256, 128), F32), pltpu.SemaphoreType.DMA((count,))]
            + [pltpu.VMEM((width, width // 2), F32)] * turned),
        out_shape=[f32(width, 3 * width), f32(8, width)] + [f32(width, width), f32(16, width)] * turned,
        input_output_aliases={1: 0} if aliased else {},
        compiler_params=params("arbitrary"),
        cost_estimate=cost(3),
        name="place_pairs",
    )(info, *([whole] if aliased else []), own, other)


AXES = ("dp", "mp")
CORE, ROW, COLUMN, NEAR_DEPTH, FAR_DEPTH = 1, 2, 4, 8, 16
PARTS = ((0, 1), (1, 2))
WEIGHT = [("weight", k) for k in range(3)]
MASKS = [("mask", 0), ("mask", 1)]
OUT = [("out", k) for k in range(3)]
STEPS = ((1, ORDER_B, [*MASKS, *WEIGHT, *OUT, ("extra", 0)]), (2, ORDER_B, [*MASKS, *WEIGHT, ("extra", 0)]),
         (0, ORDER_B, [*MASKS, *WEIGHT, ("extra", 0)]))
SCHEDULE = (
    "send_down", "own_down", (3, "first"), "ffn", 0, (3, "second"), 1, (3, "near_deep"), 2, (0, "near"), (3, "far_deep"),
    (1, "near"), "send_in", "own_in", (3, "spread_far"), (4, "first"), (0, "near_deep"), (2, "near"), (1, "near_deep"),
    (3, "spread_near"), "tokens", (0, "far_deep"), (2, "near_deep"), (1, "far_deep"), (3, "spread_column"), (4, "second"),
    (0, "spread_far"), (2, "far_deep"), (1, "spread_far"), (0, "spread_near"), (3, "whole"), (4, "near_deep"),
    (2, "spread_far"), (0, "gather_column"), (1, "spread_near"), (4, "far_deep"), (2, "spread_near"), (0, "gather_row"),
    (1, "gather_column"), (4, "spread_far"), (2, "gather_column"), (1, "gather_row"), (2, "gather_row"), (4, "spread_near"),
    (0, "gather_core"), (1, "gather_core"), (4, "spread_column"), (0, "place"), (2, "gather_core"), (1, "place"),
    (2, "place"), (4, "whole"),
)


class Order:
    def __init__(self):
        self.last = None

    def hold(self, value):
        return value if self.last is None else lax.optimization_barrier((value, self.last))[0]

    def do(self, step, *operands):
        result = step(*self.hold(operands))
        self.last = jax.tree.leaves(result)[0]
        return result


class Links:
    def __init__(self, dp, mp):
        self.dp, self.mp = dp, mp
        self.direct = dp == 8 and mp == 4
        self.at_dp, self.at_mp = lax.axis_index("dp"), lax.axis_index("mp")
        self.core, self.row, self.column = self.at_mp % 2, self.at_mp // 2, self.at_dp % 2
        self.near_deep, self.far_deep = self.at_dp // 2 % 2, self.at_dp // 4
        slot = jnp.arange(16)
        z, low, high = (((slot >> 1) & 1) << 1) | ((slot & 1) << 2), (slot >> 2) & 1, slot >> 3
        if self.direct:
            def chip(x, y):
                return (self.at_dp ^ (x | z)) * 2 + (self.row ^ y)
            orders = [chip(low, high), chip(high, low)]
        else:
            orders = [slot, slot]
        rest = jnp.stack([self.core, 1 - self.core, *(self.at_mp ^ k for k in range(4)),
                          self.column, self.near_deep, self.far_deep])
        self.info = jnp.concatenate([*orders, rest]).astype(jnp.int32)

    def swap(self, value, bits):
        count = self.dp * self.mp
        return lax.ppermute(value, AXES, [(i, i ^ bits) for i in range(count)])

    def grow(self, value, *axes):
        for bits in axes:
            value = jnp.concatenate([value, self.swap(value, bits)])
        return value


def pick(index, first, second):
    return jnp.where(index == 0, first, second)


def in_order(index, own, other, axis=0):
    return pick(index, jnp.stack([own, other], axis), jnp.stack([other, own], axis))


def at(value, index, axis):
    return lax.dynamic_index_in_dim(value, index, axis, False)


def axes_of(order):
    return (ROW, COLUMN) if order == ORDER_A else (COLUMN, ROW)


def add(*values):
    return sum(v.astype(F32) for v in values)


def any_hidden(links, keep):
    zero = jnp.zeros_like(keep[0])
    blocks = jnp.stack([keep[0], zero, keep[1], zero])
    blocks = jnp.stack([blocks[links.at_mp ^ k] for k in range(4)])
    return lax.psum(lax.psum_scatter(blocks, "mp", scatter_dimension=0, tiled=False), "dp")


class Hidden:
    def __init__(self, links, order, axis):
        self.links, self.order, self.axis = links, order, axis

    def begin(self, keep, came):
        self.shape = keep.shape[1:]
        self.parts = (2, 2, 2, 2, self.shape[0] // 8, self.shape[1])
        self.total, self.came = keep, came

    def first(self):
        column = self.links.column

        def step(keep, came):
            total = add(keep, came).reshape(self.parts)
            if self.axis == ROW:
                return total[1].astype(BF), total[0]
            return at(total, 1 - column, 3).astype(BF), at(total, column, 3)
        away, self.total = self.order.do(step, self.total, self.came)
        self.came = self.links.swap(away, self.axis)

    def second(self):
        column = self.links.column

        def step(total, came):
            total = add(total, came)
            if self.axis == ROW:
                return at(total, 1 - column, 2).astype(BF), at(total, column, 2)
            return total[1].astype(BF), total[0]
        away, self.total = self.order.do(step, self.total, self.came)
        self.came = self.links.swap(away, (ROW | COLUMN) ^ self.axis)

    def halve(self, index, axis, bits):
        def step(total, came):
            total = add(total, came)
            return at(total, 1 - index, axis).astype(BF), at(total, index, axis)
        away, self.total = self.order.do(step, self.total, self.came)
        self.came = self.links.swap(away, bits)

    def near_deep(self):
        self.halve(self.links.near_deep, 1, NEAR_DEPTH)

    def far_deep(self):
        self.halve(self.links.far_deep, 0, FAR_DEPTH)

    def spread_far(self):
        self.total = self.order.do(lambda a, b: add(a, b).astype(BF), self.total, self.came)
        self.came = self.links.swap(self.total, FAR_DEPTH)

    def spread(self, index, axis, bits):
        self.total = self.order.do(lambda a, b: in_order(index, a, b, axis), self.total, self.came)
        self.came = self.links.swap(self.total, bits)

    def spread_near(self):
        self.spread(self.links.far_deep, 0, NEAR_DEPTH)

    def spread_column(self):
        self.spread(self.links.near_deep, 1, COLUMN)

    def whole(self):
        self.result = self.order.do(lambda a, b: in_order(self.links.column, a, b, 2).astype(F32).reshape(self.shape), self.total, self.came)


class Slots:
    def __init__(self, links, order, axes, masks):
        self.links, self.order, self.axes, self.masks = links, order, axes, masks
        self.slots, self.came = [], []

    def far(self, slots):
        self.slots.append(slots)
        self.came.append(self.links.swap(slots[0], self.axes[0]))

    def near(self):
        def step(mids, came):
            return jnp.concatenate([add(m, c[4:]).astype(BF) for m, c in zip(mids, came)], axis=1)
        self.beside = self.links.swap(self.order.do(step, [s[1] for s in self.slots], self.came), self.axes[1])

    def deep(self, which, first, last):
        slots, came, beside = which
        return jnp.concatenate([add(s, c[first:last]) for s, c in zip(slots, came)], axis=1) + beside[first:last].astype(F32)

    def near_deep(self):
        step = lambda *which: self.deep(which, 2, 4).astype(BF)
        sent = self.order.do(step, [s[2] for s in self.slots], self.came, self.beside)
        self.behind = self.links.swap(sent, NEAR_DEPTH)

    def far_deep(self):
        def step(which, behind):
            total = self.deep(which, 0, 2) + behind.astype(F32)
            return total[1].astype(BF), total[0]
        sent, self.total = self.order.do(step, ([s[3] for s in self.slots], self.came, self.beside), self.behind)
        self.came = self.links.swap(sent, FAR_DEPTH)

    def spread_far(self):
        def step(total, came):
            total = total + came.astype(F32)
            row, masks, rest = 0, [], []
            for slots, count in zip(self.slots, self.masks):
                rows = slots[0].shape[1]
                masks.append(total[row:row + count])
                rest.append(total[row + count:row + rows])
                row += rows
            return jnp.concatenate(rest)[None].astype(BF), masks
        self.whole, self.mask_rows = self.order.do(step, self.total, self.came)
        self.came = self.links.swap(self.whole, FAR_DEPTH)

    def spread_near(self):
        self.spread(NEAR_DEPTH)

    def gather_column(self):
        self.spread(COLUMN)

    def gather_row(self):
        self.spread(ROW)

    def gather_core(self):
        self.spread(CORE)

    def spread(self, bits):
        self.whole = self.order.do(lambda a, b: jnp.concatenate([a, b]), self.whole, self.came)
        self.came = self.links.swap(self.whole, bits)


def body(dp, mp, tokens, w_qkv, bias_q, bias_v, w_out, bias_out, norm1_gain, norm1_bias, w_in, bias_in, w_down, bias_down,
         norm2_gain, norm2_bias, mask_logits, mask_noise, grad_out):
    width = w_out.shape[0]
    heads, rows_own, length = mask_logits.shape
    half = heads // 2
    links, order = Links(dp, mp), Order()
    core, info, swap, do = links.core, links.info, links.swap, order.do

    def chances(logits, noise):
        fraction = noise.astype(F32) / 65536.0
        return logits + jnp.log(fraction) - jnp.log(1.0 - fraction)

    def codes(logits, noise):
        logit = chances(logits, noise)
        tail = jax.nn.sigmoid(-jnp.abs(logit)) * MASK_SCALE
        return jnp.where(logit < 0.0, tail, -tail).astype(BF)

    shift = jnp.concatenate([wide(bias_q), jnp.zeros((width,), F32), wide(bias_v)])[None]
    norms = (bias_out, norm1_gain, norm1_bias, bias_down, norm2_gain, norm2_bias)
    pack = lambda *v: jnp.concatenate([wide(x) for x in v] + [jnp.zeros(((8 - len(v)) * width,), F32)]).reshape(8, width)
    mixed, totals, came = [], [], []

    def attention(part, pieces):
        own, other, total = do(lambda q, m: attend(*PARTS[part], info, q, m), qkv, pieces)
        mixed.append((own, other))
        came.append(swap(other, CORE))
        totals.append(total)

    if links.direct:
        plane = (1, rows_own, length)

        def two_sides(logits, noise, bias):
            code = codes(logits, noise)
            row = jnp.pad(bias, (0, rows_own * length - bias.shape[0])).reshape(plane)
            return jnp.concatenate([pick(core, code[half:], code[:half]), row]), pick(core, code[:half], code[half:])
        away, keep = do(two_sides, mask_logits, mask_noise, bias_in)
        beside = swap(away, CORE)
        other_tokens = swap(tokens, CORE)

        parts = half // 2

        def chip_codes(keep, beside):
            chip = in_order(core, keep, beside[:half], 1).reshape(parts, 2, 1, 2 * rows_own, length)
            return [[chip[p:p + n, h] for h in range(2)] for p, n in PARTS], beside[half].reshape(-1)[:bias_in.shape[0]]
        chip, near_bias = do(chip_codes, keep, beside)
        flat = lambda tree: jnp.concatenate([v for part in tree for v in part])
        behind = swap(flat(chip), FAR_DEPTH)
        eighth = w_in.shape[0] // 8
        split = lambda w: w.reshape(4, 2, eighth, width)
        z_at, x_at = links.at_dp // 2, links.column

        def to_row(w_in, w_down, *biases):
            parts = [at(at(split(w), z_at, 0), x_at, 0) for w in (w_in, w_down)]
            return jnp.concatenate([*parts, jnp.pad(jnp.stack(biases), ((0, 14), (0, 0)))])
        piece = swap(do(to_row, w_in, w_down, bias_in, near_bias), ROW)
        qkv = do(lambda *v: project(info, *v), tokens, other_tokens, w_qkv, shift)
        piece = order.hold(piece)
        axes = ((COLUMN, ROW), (ROW, COLUMN))
        groups, seconds, fars = [None] * 2, [None] * 2, [None] * 2

        def deep_parts(chip, behind):
            result, row = [], 0
            for part, (p, n) in zip(chip, PARTS):
                heads = []
                for own in part:
                    heads.append(jnp.concatenate([own, behind[row:row + n]], axis=1))
                    row += n
                result.append(jnp.concatenate(heads))
            return result
        deep = do(deep_parts, chip, behind)
        deep = [(v, swap(v, NEAR_DEPTH)) for v in deep]

        def gather_near(part):
            n = PARTS[part][1]
            groups[part] = do(lambda a, b: [jnp.concatenate([a[h * n:h * n + n], b[h * n:h * n + n]], axis=1) for h in range(2)], *deep[part])
            seconds[part] = [swap(groups[part][h], axes[h][0]) for h in range(2)]

        def gather_far(part):
            both = do(lambda g, s: [jnp.concatenate(v, axis=1) for v in zip(g, s)], groups[part], seconds[part])
            fars[part] = [swap(both[h], axes[h][1]) for h in range(2)]

        behind = swap(piece[:2 * eighth], FAR_DEPTH)
        gather_near(0)
        gather_far(0)
        gather_near(1)
        vecs = do(pack, *norms)
        biases = do(lambda *v: wide(jnp.concatenate(v)).reshape(4, width), bias_in, near_bias, piece[2 * eighth], piece[2 * eighth + 1])
        pair = do(lambda a, b: in_order(links.far_deep, a[:2 * eighth], b), piece, behind)
        behind = swap(pair, NEAR_DEPTH)
        gather_far(1)
        pieces = [[v for h in range(2) for v in (groups[p][h], seconds[p][h], fars[p][h])] for p in range(2)]
        beside = swap(do(lambda *v: jnp.stack(v), w_in, w_down), CORE)
        attention(0, pieces[0])
        beside = order.hold(beside)

        def group_step(own, came, w):
            group = in_order(links.near_deep, own, came, 1)
            return [v.reshape(4, eighth, width) for v in jnp.split(group, 2, axis=2)], at(split(w), 1 - x_at, 1)
        group, straight = do(group_step, pair, behind, w_down)
        around, straight = swap(group[0], COLUMN), swap(straight, ROW)
        near_in, near_down = do(lambda v: [v[0], v[1]], beside)
        attention(1, pieces[1])
        came[0] = order.hold(came[0])
        blocks_in, blocks_down = [w_in, near_in], [w_down, near_down]
    else:
        other_tokens = swap(tokens, CORE)
        qkv = project(info, tokens, other_tokens, w_qkv, shift)
        whole = lax.all_gather(codes(mask_logits, mask_noise), AXES, axis=1, tiled=True)
        own = lax.dynamic_slice_in_dim(whole, core * half, half, 0).reshape(half // 2, 2, 16, length // 16, length)
        own = own.transpose(1, 0, 2, 3, 4)
        pieces = [[own[h, p:p + n, a:b] for h in range(2) for a, b in ((0, 4), (4, 8), (8, 16))] for p, n in PARTS]
        attention(0, pieces[0])
        attention(1, pieces[1])
        vecs = pack(*norms)
        blocks_in, blocks_down, blocks_bias = ([v[links.at_mp ^ k] for k in range(4)]
                                               for v in (lax.all_gather(w, "mp") for w in (w_in, w_down, bias_in)))
        biases = wide(jnp.stack(blocks_bias))
    first_low, active, slope, normal, inverse, branch = do(
        lambda *v: ffn_first(info, *v), tokens, [own for own, _ in mixed] + came, w_out, vecs, biases, blocks_in[:2], blocks_down[:2])
    if links.direct:
        across = do(lambda *v: [in_order(links.column, a, b, 1).reshape(w_in.shape) for a, b in (v[:2], v[2:])],
                    group[0], around, group[1], straight)
        blocks_in += [across[0], swap(across[0], CORE)]
        blocks_down += [across[1], swap(across[1], CORE)]
    out, active_two, slope_two, grad_second, grad_branch, sums = do(
        ffn_second, first_low, branch, grad_out, vecs, biases, blocks_in[2:], blocks_down[2:])
    d_own, d_other, slots = [None] * 3, [None] * 3, [None] * 3
    hidden = [Hidden(links, order, COLUMN), Hidden(links, order, COLUMN)]
    keep, grads, settled = [None] * 2, {}, []

    def send_down():
        grads["sent_down"] = swap(do(functools.partial(outer, (1, 1), bf), active, active_two, grad_branch), CORE)

    def own_down():
        keep[0] = do(functools.partial(outer, (0, 0), f32), active, active_two, grad_branch)
        hidden[0].begin(keep[0], grads["sent_down"])

    def ffn_gradient():
        grads["pre"], grads["one"], grads["attn"], grads["small"] = do(
            lambda *v: ffn_back(info, *v), grad_branch, [slope, slope_two], grad_second, normal, inverse, vecs, sums, blocks_in, blocks_down)
        grads["pair"] = grads["attn"], swap(grads["attn"], CORE)

    def settle():
        for pair in range(3):
            if d_other[pair] is not None and pair not in settled:
                settled.append(pair)
                d_other[pair] = order.hold(d_other[pair])

    def send_in():
        sent = do(functools.partial(outer, (1, 3), bf), grads["pre"], grads["pre"], first_low)
        settle()
        grads["sent_in"] = swap(sent, CORE)

    def own_in():
        keep[1] = do(functools.partial(outer, (0, 2), f32), grads["pre"], grads["pre"], first_low)
        hidden[1].begin(keep[1], grads["sent_in"])

    def back(step):
        pair, place, segments = STEPS[step]
        part = min(pair, 1)
        local = pair - PARTS[part][0]
        own, other, *outs = do(
            lambda *v: attend_back(pair, local, [(place, segments)], info, *v), qkv, mixed[part], grads["pair"], w_out,
            totals[part], (tokens, other_tokens), pieces[part], () if step else mixed, grads["small"])
        settle()
        slots[step] = outs
        if links.direct:
            chains[step].far(outs)
        d_own[pair] = own
        d_other[pair] = swap(other, CORE)

    def grad_input():
        grads["tokens"] = do(lambda *v: grad_tokens(info, *v), [*d_own, *d_other], grads["one"], w_qkv)

    def place(steps, own, other):
        pairs, row = [], 0
        for step in steps:
            pair, _, segments = STEPS[step]
            found = {}
            for kind, k in segments:
                if kind != "mask":
                    found[kind, k] = row
                    row += segment_rows(kind, length, width)
            pairs.append((pair, [found["weight", k] for k in range(3)], found["extra", 0]))
        out_at = found.get(("out", 0))
        whole = [] if result[0] is None else [result[0]]
        result[0], vector, *extras = do(lambda a, b, *w: place_pairs(pairs, out_at, info, width, a, b, *w), own, other, *whole)
        vectors.append(vector)
        if extras:
            result[1:] = extras

    result, vectors = [None] * 3, []
    masks = [sum(kind == "mask" for kind, _ in segments) * length // 4 for _, _, segments in STEPS]
    chains = [Slots(links, order, axes_of(place), [count]) for (_, place, _), count in zip(STEPS, masks)]
    kernels = {"send_down": send_down, "own_down": own_down, "ffn": ffn_gradient, "send_in": send_in, "own_in": own_in, "tokens": grad_input}
    for step in range(3):
        kernels[step] = functools.partial(back, step)
    mask_rows = [None] * 3
    for name in SCHEDULE:
        if name in kernels:
            kernels[name]()
        elif links.direct:
            who, what = name
            chain = (*chains, *hidden)[who]
            if what == "place":
                place((who,), chain.whole, chain.came)
            else:
                getattr(chain, what)()
    if links.direct:
        grad_w_down, grad_w_in = (chain.result for chain in hidden)
        mask_rows = [chain.mask_rows[0].reshape(2, 4, length // 16, 128) for chain in chains]
    else:
        grad_w_down, grad_w_in = (any_hidden(links, k + wide(grads[s])) for k, s in zip(keep, ("sent_down", "sent_in")))
        for step, (s, count) in enumerate(zip(slots, masks)):
            own = wide(jnp.concatenate(s[::-1]))
            both = lax.psum(in_order(core, own, jnp.zeros_like(own)), AXES)
            sides = [both[core], both[1 - core]]
            place((step,), *(v[:, count:].astype(BF) for v in sides))
            mask_rows[step] = jnp.stack([v[:, :count].reshape(16, 2, 4, length // 16, 128).transpose(1, 2, 0, 3, 4) for v in sides])
    grad_w_qkv, grad_w_out, small = result
    bias = sum(vectors)
    by_pair = [None] * 3
    for (pair, _, _), rows in zip(STEPS, mask_rows):
        by_pair[pair] = rows
    if links.direct:
        mask_sum = jnp.stack(by_pair).transpose(0, 1, 3, 2, 4).reshape(half, 2 * rows_own, length)
        mine = pick(core, mask_sum[:, :rows_own], mask_sum[:, rows_own:])
        theirs = swap(pick(core, mask_sum[:, rows_own:], mask_sum[:, :rows_own]), CORE)
    else:
        mine, theirs = jnp.stack(by_pair, axis=1).transpose(0, 1, 2, 4, 5, 3, 6).reshape(2, half, length, length)
        place = (links.at_dp * mp + links.at_mp) * rows_own
        mine, theirs = (lax.dynamic_slice_in_dim(m, place, rows_own, 1) for m in (mine, theirs))
    mask_sum = pick(core, jnp.concatenate([mine, theirs]), jnp.concatenate([theirs, mine]))
    mask_own = jax.nn.sigmoid(chances(mask_logits, mask_noise))
    grad_mask_logits = mask_sum * (MASK_SCALE * mask_own * (1.0 - mask_own))
    return (out, grads["tokens"], grad_w_qkv, bias[0], bias[2], grad_w_out, small[5], small[3], small[4], grad_w_in, small[6 + links.at_mp],
            grad_w_down, small[2], small[0], small[1], grad_mask_logits)


def solution(mesh):
    both, none = ("dp", "mp"), P()
    rows, mask, split = P(both, None), P(None, both, None), P("mp", None)
    ins = (rows, none, none, none, none, none, none, none, split, P("mp"), split, none, none, none, mask, mask, rows)
    outs = (rows, rows, none, none, none, none, none, none, none, split, P("mp"), split, none, none, none, mask)
    step = functools.partial(body, mesh.shape["dp"], mesh.shape["mp"])
    return jax.shard_map(step, mesh=mesh, in_specs=ins, out_specs=outs, check_vma=False)
```
